128 devices in a mesh: dp: 16 (over x, y_hi, core), fsdp: 8 (over y_lo, z).
Axes of the slice: x: 4, y: 4 (y_hi: 2, y_lo: 2; y = y_hi * 2 + y_lo), z: 4, core: 2. Of those that a mesh axis runs over, the one named last changes fastest.
Arguments:
- tokens: bfloat16 [32768, 768], P(('dp', 'fsdp')), may hold values from -6 to 6
- lengths: int32 [128], P(('dp', 'fsdp')), may hold values from 128 to 256, as said below
- cotangent: bfloat16 [32768, 768], P(('dp', 'fsdp')), may hold values from -24 to 24
- joint_weight: float32 [2, 768, 2304], P(None, None, ('dp', 'fsdp')), may hold values from -0.21875 to 0.21875
- output_weight: float32 [2, 768, 768], P(None, None, ('dp', 'fsdp')), may hold values from -0.4375 to 0.4375
- expand_weight: float32 [2, 768, 3072], P(None, None, ('dp', 'fsdp')), may hold values from -0.21875 to 0.21875
- shrink_weight: float32 [2, 3072, 768], P(None, ('dp', 'fsdp')), may hold values from -0.109375 to 0.109375
- layer_gains: float32 [2, 4, 768], P(None, None, ('dp', 'fsdp')), may hold values from -0.3 to 1.4
- joint_moment: float32 [2, 768, 2304], P(None, None, ('dp', 'fsdp')), may hold values from -0.00021922641 to 0.00021922641
- output_moment: float32 [2, 768, 768], P(None, None, ('dp', 'fsdp')), may hold values from -7.0152453e-05 to 7.0152453e-05
- expand_moment: float32 [2, 768, 3072], P(None, None, ('dp', 'fsdp')), may hold values from -6.13834e-05 to 6.13834e-05
- shrink_moment: float32 [2, 3072, 768], P(None, ('dp', 'fsdp')), may hold values from -8.769057e-05 to 8.769057e-05
- gains_moment: float32 [2, 4, 768], P(None, None, ('dp', 'fsdp')), may hold values from -0.0002630717 to 0.0002630717
- joint_square: float32 [2, 768, 2304], P(None, None, ('dp', 'fsdp')), may hold values from 1.76529736e-11 to 1.7652974e-09
- output_square: float32 [2, 768, 768], P(None, None, ('dp', 'fsdp')), may hold values from 4.519161e-11 to 1.8076645e-10
- expand_square: float32 [2, 768, 3072], P(None, None, ('dp', 'fsdp')), may hold values from 3.459983e-11 to 1.38399313e-10
- shrink_square: float32 [2, 3072, 768], P(None, ('dp', 'fsdp')), may hold values from 7.061189e-11 to 2.82447578e-10
- gains_square: float32 [2, 4, 768], P(None, None, ('dp', 'fsdp')), may hold values from 6.3550705e-10 to 2.5420282e-09
Outputs:
- layer_output: bfloat16 [32768, 768], P(('dp', 'fsdp'))
- input_gradient: float32 [32768, 768], P(('dp', 'fsdp'))
- gradient_norm: float32 [], replicated
- joint_master: float32 [2, 768, 2304], P(None, None, ('dp', 'fsdp'))
- output_master: float32 [2, 768, 768], P(None, None, ('dp', 'fsdp'))
- expand_master: float32 [2, 768, 3072], P(None, None, ('dp', 'fsdp'))
- shrink_master: float32 [2, 3072, 768], P(None, ('dp', 'fsdp'))
- gains_master: float32 [2, 4, 768], P(None, None, ('dp', 'fsdp'))
- joint_momentum: float32 [2, 768, 2304], P(None, None, ('dp', 'fsdp'))
- output_momentum: float32 [2, 768, 768], P(None, None, ('dp', 'fsdp'))
- expand_momentum: float32 [2, 768, 3072], P(None, None, ('dp', 'fsdp'))
- shrink_momentum: float32 [2, 3072, 768], P(None, ('dp', 'fsdp'))
- gains_momentum: float32 [2, 4, 768], P(None, None, ('dp', 'fsdp'))
- joint_variance: float32 [2, 768, 2304], P(None, None, ('dp', 'fsdp'))
- output_variance: float32 [2, 768, 768], P(None, None, ('dp', 'fsdp'))
- expand_variance: float32 [2, 768, 3072], P(None, None, ('dp', 'fsdp'))
- shrink_variance: float32 [2, 3072, 768], P(None, ('dp', 'fsdp'))
- gains_variance: float32 [2, 4, 768], P(None, None, ('dp', 'fsdp'))
The draws below stay inside these ranges and needn't reach their ends.
Inputs may be any that keep to these rules, and one draw needn't show every extreme that they name: The sequence of device d fills its first lengths[d] slots; the later slots are padding.
All inputs are finite; a program needn't handle non-finite values.
Results may differ from the reference program's by a relative error of at most 0.017.
Values may be sent and summed in bfloat16 or wider, within the bound.
A program may use at most 256 MiB of HBM per device.

```python
import math
import jax
import jax.numpy as jnp
from jax import lax

D = 768
HEADS = 12
FF = 3072
HEAD_DIM = 64
LAYERS = 2
STEP = 5
TOK_DEV = 256
SEQS = 128
TOKENS = 32768
PARAMS = 14161920


def draw_lengths(key, part):
    base = jax.random.randint(jax.random.fold_in(key, 1), (SEQS,), TOK_DEV // 2, TOK_DEV + 1, dtype=jnp.int32)
    order = jax.random.permutation(jax.random.fold_in(key, 2), SEQS)
    base = base.at[order[0]].set(TOK_DEV)
    base = base.at[order[1]].set(TOK_DEV // 2)
    return base.astype(jnp.int32)


def draw_layer_gains(key, part):
    shape = (LAYERS, 4, D)
    gain_part = jax.random.uniform(jax.random.fold_in(key, 3), shape, jnp.float32, 0.6, 1.4)
    shift_part = jax.random.uniform(jax.random.fold_in(key, 4), shape, jnp.float32, -0.3, 0.3)
    is_gain = (jnp.arange(4) % 2 == 0)[None, :, None]
    return jnp.where(is_gain, gain_part, shift_part).astype(jnp.float32)


def first_moment(key, shape, salt, factor):
    typical = 0.11 * factor / math.sqrt(PARAMS)
    noise = jax.random.truncated_normal(jax.random.fold_in(key, salt), -3.0, 3.0, shape, jnp.float32)
    return (typical * noise).astype(jnp.float32)


def second_moment(key, shape, salt, factor):
    lowest = 0.001 * factor * factor / PARAMS
    spread = jax.random.uniform(jax.random.fold_in(key, salt), shape, jnp.float32, 0.0, math.log(4.0))
    return (lowest * jnp.exp(spread)).astype(jnp.float32)


def joint_factor():
    columns = jnp.arange(3 * D, dtype=jnp.int32)
    return jnp.where(columns < 2 * D, 0.5, 2.5).astype(jnp.float32)[None, None, :]


def draw_joint_moment(key, part):
    return first_moment(key, (LAYERS, D, 3 * D), 11, joint_factor())


def draw_output_moment(key, part):
    return first_moment(key, (LAYERS, D, D), 12, 0.8)


def draw_expand_moment(key, part):
    return first_moment(key, (LAYERS, D, FF), 13, 0.7)


def draw_shrink_moment(key, part):
    return first_moment(key, (LAYERS, FF, D), 14, 1.0)


def draw_gains_moment(key, part):
    return first_moment(key, (LAYERS, 4, D), 15, 3.0)


def draw_joint_square(key, part):
    return second_moment(key, (LAYERS, D, 3 * D), 21, joint_factor())


def draw_output_square(key, part):
    return second_moment(key, (LAYERS, D, D), 22, 0.8)


def draw_expand_square(key, part):
    return second_moment(key, (LAYERS, D, FF), 23, 0.7)


def draw_shrink_square(key, part):
    return second_moment(key, (LAYERS, FF, D), 24, 1.0)


def draw_gains_square(key, part):
    return second_moment(key, (LAYERS, 4, D), 25, 3.0)


def spiked(values, key, source, target, shards_of, factor):
    def block_of(dim):
        return (jnp.arange(values.shape[dim]) // (values.shape[dim] // shards_of)).reshape((-1,) + (1,) * (values.ndim - 1 - dim))

    one_side = jax.random.permutation(key, shards_of)[block_of(target)]
    second = (block_of(target) + shards_of // 2) % shards_of
    return jnp.where((block_of(source) == one_side) | (block_of(source) == second), factor * values, values)


def block_levels(own_key, dims, cuts, smallest, largest):
    loudness = 1.0
    for axis_at, blocks in cuts:
        steps = jax.random.uniform(jax.random.fold_in(jax.random.fold_in(own_key, 6), axis_at), (blocks,), jnp.float32, smallest / len(cuts), largest / len(cuts))
        loudness = loudness * jnp.repeat(jnp.exp(steps), dims[axis_at] // blocks).reshape((-1,) + (1,) * (len(dims) - 1 - axis_at))
    return loudness


def bell_draw(rng, shape, scale, bound, cuts=(), kind=jnp.bfloat16):
    values = scale * jax.random.normal(rng, shape, jnp.float32)
    if cuts:
        values = values * block_levels(rng, shape, cuts, -0.22, 0.18)
    return jnp.clip(values, -bound, bound).astype(kind)


def gaussian_with(key, shape, scale, limit, pieces, heavy, kind=jnp.bfloat16):
    values = scale * jax.random.normal(key, shape, jnp.float32)
    if pieces:
        values = values * block_levels(key, shape, pieces, -0.22, 0.18)
    return jnp.clip(spiked(values, jax.random.fold_in(key, 3), *heavy), -limit, limit).astype(kind)


def setup_inputs(seed: int = 0) -> dict:
    streams_of = jax.random.split(jax.random.key(seed), 19)
    tokens = bell_draw(streams_of[0], (TOKENS, D), 1.0, 6.0, ((0, 128),))
    lengths = draw_lengths(jax.random.fold_in(streams_of[18], 71), 0)
    cotangent = gaussian_with(streams_of[2], (TOKENS, D), 1.0, 24.0, ((0, 128),), (0, 1, 128, 5.5))
    joint_weight = bell_draw(streams_of[3], (LAYERS, D, 3 * D), D ** -0.5, 0.21875, ((2, 128),), jnp.float32)
    output_weight = bell_draw(streams_of[4], (LAYERS, D, D), (D // 4) ** -0.5, 0.4375, ((2, 128),), jnp.float32)
    expand_weight = bell_draw(streams_of[5], (LAYERS, D, FF), D ** -0.5, 0.21875, ((2, 128),), jnp.float32)
    shrink_weight = bell_draw(streams_of[6], (LAYERS, FF, D), FF ** -0.5, 0.109375, ((1, 128),), jnp.float32)
    layer_gains = draw_layer_gains(jax.random.fold_in(streams_of[18], 71), 0)
    joint_moment = draw_joint_moment(jax.random.fold_in(streams_of[18], 71), 0)
    output_moment = draw_output_moment(jax.random.fold_in(streams_of[18], 71), 0)
    expand_moment = draw_expand_moment(jax.random.fold_in(streams_of[18], 71), 0)
    shrink_moment = draw_shrink_moment(jax.random.fold_in(streams_of[18], 71), 0)
    gains_moment = draw_gains_moment(jax.random.fold_in(streams_of[18], 71), 0)
    joint_square = draw_joint_square(jax.random.fold_in(streams_of[18], 71), 0)
    output_square = draw_output_square(jax.random.fold_in(streams_of[18], 71), 0)
    expand_square = draw_expand_square(jax.random.fold_in(streams_of[18], 71), 0)
    shrink_square = draw_shrink_square(jax.random.fold_in(streams_of[18], 71), 0)
    gains_square = draw_gains_square(jax.random.fold_in(streams_of[18], 71), 0)
    return dict(tokens=tokens, lengths=lengths, cotangent=cotangent, joint_weight=joint_weight, output_weight=output_weight, expand_weight=expand_weight, shrink_weight=shrink_weight, layer_gains=layer_gains, joint_moment=joint_moment, output_moment=output_moment, expand_moment=expand_moment, shrink_moment=shrink_moment, gains_moment=gains_moment, joint_square=joint_square, output_square=output_square, expand_square=expand_square, shrink_square=shrink_square, gains_square=gains_square)


highest = lax.Precision.HIGHEST
beta_first = 0.9
beta_second = 0.999
adam_epsilon = 1e-08
decay_matrix = 0.1
rate_matrix = 0.05
rate_gains = 0.25
clip_limit = 1.0
norm_epsilon = 1e-05
masked_value = -1e+30

@jax.custom_vjp
def low(v):
    return lax.optimization_barrier(v.astype(jnp.bfloat16)).astype(jnp.float32)

@jax.custom_vjp
def low_back(v):
    return v

def low_keep(v):
    return (low(v), None)

def low_pass(kept, grad):
    return (grad,)

def back_keep(v):
    return (v, None)

def back_low(kept, grad):
    return (low(grad),)
low.defvjp(low_keep, low_pass)
low_back.defvjp(back_keep, back_low)

def layer_norm(features, gain_row, shift_row):
    mean_value = lax.optimization_barrier(jnp.mean(features, axis=-1, keepdims=True))
    centred = features - mean_value
    variance = lax.optimization_barrier(jnp.mean(centred * centred, axis=-1, keepdims=True))
    return centred * lax.rsqrt(variance + norm_epsilon) * gain_row + shift_row

def adam_update(master, gradient, moment, square, rate, decay, clip_factor):
    clipped = gradient * clip_factor
    momentum = beta_first * moment + (1.0 - beta_first) * clipped
    variance = beta_second * square + (1.0 - beta_second) * clipped * clipped
    corrected_first = momentum / (1.0 - beta_first ** STEP)
    corrected_second = variance / (1.0 - beta_second ** STEP)
    updated = master - rate * (corrected_first / (jnp.sqrt(corrected_second) + adam_epsilon) + decay * master)
    return (updated, momentum, variance)

def forward(group_tokens, group_lengths, joint_all, output_all, expand_all, shrink_all, gains_all):
    batch = group_tokens.shape[0]
    slots = group_tokens.shape[1]
    positions = jnp.arange(slots, dtype=jnp.int32)
    live_rows = positions[None, :] < group_lengths[:, None]
    causal = positions[None, :] <= positions[:, None]
    allowed = causal[None] & live_rows[:, None, :]
    select_base = (positions[None, :] > 0) & (positions[None, :] < positions[:, None])
    selectable = select_base[None] & live_rows[:, :, None]
    score_scale = HEAD_DIM ** (-0.5)
    stream = group_tokens
    for which_layer in range(LAYERS):
        gains = low(gains_all[which_layer])
        normed = low(layer_norm(stream, gains[0], gains[1]))
        projected = jnp.einsum('btd,de->bte', normed, low(joint_all[which_layer]), precision=highest)
        projected = low_back(low(projected))
        query_rows = projected[..., :D].reshape(batch, slots, HEADS, HEAD_DIM)
        key_rows = projected[..., D:2 * D].reshape(batch, slots, HEADS, HEAD_DIM)
        value_rows = projected[..., 2 * D:].reshape(batch, slots, HEADS, HEAD_DIM)
        scores = low_back(jnp.einsum('bihd,bjhd->bhij', query_rows, key_rows, precision=highest) * score_scale)
        chosen = jnp.where(selectable, jax.nn.softplus(scores[:, 0]), 0.0)
        summed = jnp.cumsum(chosen, axis=1)
        forget = jnp.pad(summed[:, :-1], ((0, 0), (1, 0), (0, 0)))
        logits = jnp.where(allowed[:, None], scores - forget[:, None], masked_value)
        softmax_low = low(jax.nn.softmax(logits, axis=-1))
        attended = jnp.einsum('bhij,bjhd->bihd', softmax_low, value_rows, precision=highest)
        attended = low_back(low(attended.reshape(batch, slots, D)))
        branch = low_back(jnp.einsum('bte,ed->btd', attended, low(output_all[which_layer]), precision=highest))
        stream = stream + branch
        normed_second = low(layer_norm(stream, gains[2], gains[3]))
        raised = low_back(jnp.einsum('btd,df->btf', normed_second, low(expand_all[which_layer]), precision=highest))
        hidden = low(jax.nn.gelu(raised, approximate=True))
        branch = low_back(jnp.einsum('btf,fd->btd', hidden, low(shrink_all[which_layer]), precision=highest))
        stream = stream + branch
    return stream

def reference(tokens, lengths, cotangent, joint_weight, output_weight, expand_weight, shrink_weight, layer_gains, joint_moment, output_moment, expand_moment, shrink_moment, gains_moment, joint_square, output_square, expand_square, shrink_square, gains_square):
    masters = (joint_weight, output_weight, expand_weight, shrink_weight, layer_gains)
    group_size = math.gcd(SEQS, max(1, 4096 // TOK_DEV))
    group_count = SEQS // group_size
    token_groups = tokens.astype(jnp.float32).reshape(group_count, group_size, TOK_DEV, D)
    back_groups = cotangent.astype(jnp.float32).reshape(group_count, group_size, TOK_DEV, D)
    length_groups = lengths.reshape(group_count, group_size)

    def accumulate(totals, items):
        group_tokens, group_back, group_lengths = items

        def run(features, joint_all, output_all, expand_all, shrink_all, gains_all):
            return forward(features, group_lengths, joint_all, output_all, expand_all, shrink_all, gains_all)
        result, pullback = jax.vjp(run, group_tokens, joint_weight, output_weight, expand_weight, shrink_weight, layer_gains)
        live = (jnp.arange(TOK_DEV, dtype=jnp.int32)[None, :] < group_lengths[:, None]).astype(group_back.dtype)
        pulled = pullback(group_back * live[:, :, None])
        totals = tuple((total + piece for total, piece in zip(totals, pulled[1:])))
        return (totals, (result, pulled[0]))
    starts = tuple((jnp.zeros_like(master) for master in masters))
    totals, outputs = lax.scan(accumulate, starts, (token_groups, back_groups, length_groups))
    results, input_grads = outputs
    squares = [jnp.sum(piece * piece) for piece in totals]
    gradient_norm = jnp.sqrt(squares[0] + squares[1] + squares[2] + squares[3] + squares[4])
    clip_factor = jnp.minimum(1.0, clip_limit / (gradient_norm + 1e-06))
    joint_new = adam_update(joint_weight, totals[0], joint_moment, joint_square, rate_matrix, decay_matrix, clip_factor)
    output_new = adam_update(output_weight, totals[1], output_moment, output_square, rate_matrix, decay_matrix, clip_factor)
    expand_new = adam_update(expand_weight, totals[2], expand_moment, expand_square, rate_matrix, decay_matrix, clip_factor)
    shrink_new = adam_update(shrink_weight, totals[3], shrink_moment, shrink_square, rate_matrix, decay_matrix, clip_factor)
    gains_new = adam_update(layer_gains, totals[4], gains_moment, gains_square, rate_gains, 0.0, clip_factor)
    layer_output = results.reshape(TOKENS, D).astype(jnp.bfloat16)
    input_gradient = input_grads.reshape(TOKENS, D)
    return (layer_output, input_gradient, gradient_norm, joint_new[0], output_new[0], expand_new[0], shrink_new[0], gains_new[0], joint_new[1], output_new[1], expand_new[1], shrink_new[1], gains_new[1], joint_new[2], output_new[2], expand_new[2], shrink_new[2], gains_new[2])
```

```python
import functools
import itertools

import jax
import jax.numpy as jnp
from jax import lax
from jax.experimental import pallas as pl
from jax.experimental.pallas import tpu as pltpu
from jax.sharding import PartitionSpec as P

MESH = pl.DeviceIdType.MESH
BF = jnp.bfloat16
F32 = jnp.float32

def place():
    dp = lax.axis_index("dp"); fs = lax.axis_index("fsdp")
    return (dp // 4, lax.rem(dp // 2, 2) * 2 + fs // 4, lax.rem(fs, 4), lax.rem(dp, 2))

def device_at(x, y, z, c):
    return ((x * 2 + y // 2) * 2 + c, lax.rem(y, 2) * 4 + z)

def moved(co, axis, k):
    n = 2 if axis == 3 else 4
    co = list(co)
    co[axis] = lax.rem(co[axis] + (k % n), n)
    return tuple(co)

def greet(co):
    bar = pltpu.get_barrier_semaphore()
    peers = [(a, k) for a in range(3) for k in (1, 2, 3)] + [(3, 1)]
    for a, k in peers:
        pl.semaphore_signal(bar, inc=1, device_id=device_at(*moved(co, a, k)), device_id_type=MESH)
    pl.semaphore_wait(bar, len(peers))

class Link:
    def __init__(self, co, ss, rs):
        self.co, self.ss, self.rs = co, ss, rs
        self.n = 0
        self.out = []
    def send(self, src, dst, axis, k):
        i = self.n
        self.n += 1
        cp = pltpu.make_async_remote_copy(src_ref=src, dst_ref=dst, send_sem=self.ss.at[i], recv_sem=self.rs.at[i],
            device_id=device_at(*moved(self.co, axis, k)), device_id_type=MESH)
        cp.start()
        self.out.append(cp)
        return cp
    def drain(self):
        for cp in self.out:
            cp.wait_send()

class Local:
    def __init__(self, sems):
        self.sems, self.n = sems, 0
    def copy(self, src, dst):
        cp = pltpu.make_async_copy(src, dst, self.sems.at[self.n])
        self.n += 1
        cp.start()
        return cp

class RowSum:
    def __init__(self, link, slots):
        self.link, self.slots, self.n = link, slots, 0

    def send(self, value):
        axis = (2, 1, 0, 3)[self.n]
        mine = self.slots.at[self.n, self.link.co[axis]]
        mine[...] = value
        self.going = [self.link.send(mine, mine, axis, k) for k in ((1, 3, 2) if axis < 3 else (1,))]

    def total(self):
        for cp in self.going:
            cp.wait_recv()
        count = 4 if self.n < 3 else 2
        value = self.slots[self.n, 0]
        for k in range(1, count):
            value = value + self.slots[self.n, k]
        self.n += 1
        return value


def gather_kernel(L, pa, pb, pc, gains, JT, OT, E, S, gains_all, abuf, jf, of, jst, ost, gbuf, ss, rs, ls):
    co = place()
    x, y, z, c = co
    lo, hi = pl.ds(0, 2), pl.ds(2, 2)
    greet(co)
    link, loc = Link(co, ss, rs), Local(ls)
    gain_sum = RowSum(link, gbuf)
    gain_sum.send(gains[...])
    own = []
    ph1 = {}
    for l in range(L):
        o = [loc.copy(pa.at[l], abuf.at[l, y, z]), loc.copy(pb.at[l], E.at[l, c, x, y, z]), loc.copy(pc.at[l], S.at[l, c, x, y, z])]
        own.append(o)
        for k in (1, 3, 2):
            ph1[l, k] = [link.send(pa.at[l], abuf.at[l, y, z], 2, k), link.send(pb.at[l], E.at[l, c, x, y, z], 0, k),
                         link.send(pc.at[l], S.at[l, c, x, y, z], 1, k)]
    ph2 = {}
    for l in range(L):
        for part in range(3):
            own[l][part].wait()
            for k in (1, 3, 2):
                ph1[l, k][part].wait_recv()
            ref, axis = ((abuf.at[l, y], 1), (E.at[l, c, :, y, z], 2), (S.at[l, c, x, :, z], 0))[part]
            ph2[l, part] = [link.send(ref, ref, axis, 1), link.send(ref, ref, axis, 3)]
    gain_sum.send(gain_sum.total())
    ph2f = {}
    for l in range(L):
        for part in range(3):
            axis = (1, 2, 0)[part]
            f = []
            for side, (back, half) in enumerate(((3, lo), (1, hi))):
                ph2[l, part][side].wait_recv()
                q = moved(co, axis, back)
                ref = (lambda: abuf.at[l, q[1], half], lambda: E.at[l, c, half, y, q[2]], lambda: S.at[l, c, q[0], half, z])[part]()
                f.append(link.send(ref, ref, axis, (1, 3)[side]))
            ph2f[l, part] = f
    gain_sum.send(gain_sum.total())
    ph3 = {}
    sib = []
    def to_sibling(ref):
        sib.append(link.send(ref, ref, 3, 1))
    loc_out = []
    for l in range(L):
        for part in (1, 2, 0):
            for cp in ph2f[l, part]:
                cp.wait_recv()
            if part == 0:
                for yy in range(4):
                    for zz in range(4):
                        v = abuf[l, yy, zz].astype(F32)
                        at = (yy // 2) * 144 + ((yy % 2) * 4 + zz) * 18
                        jf[at:at + 18] = v[:18]
                        at = (yy // 2) * 48 + ((yy % 2) * 4 + zz) * 6
                        of[at:at + 6] = v[18:24]
                for h in range(2):
                    jst[l, h] = jf[h * 144:h * 144 + 144].astype(BF)
                    ost[l, h] = of[h * 48:h * 48 + 48].astype(BF)
                loc_out += [loc.copy(jst.at[l], JT.at[l, x, :, c]), loc.copy(ost.at[l], OT.at[l, x, :, c])]
                pairs = [(jst.at[l], JT.at[l, x, :, c]), (ost.at[l], OT.at[l, x, :, c])]
                axis = 0
            else:
                ref, axis = ((E.at[l, c, :, y, :], 1), (S.at[l, c, :, :, z], 2))[part - 1]
                pairs = [(ref, ref)]
            ph3[l, part] = [[link.send(s, d, axis, k) for s, d in pairs] for k in (1, 3)]
            for s, d in pairs:
                sib.append(link.send(s, d, 3, 1))
    gain_sum.send(gain_sum.total())
    ph3f = {}
    for l in range(L):
        for part in (1, 2, 0):
            axis = (0, 1, 2)[part]
            f = []
            for side, (back, h) in enumerate(((3, 0), (1, 1))):
                for cp in ph3[l, part][side]:
                    cp.wait_recv()
                q = moved(co, axis, back)
                half = (lo, hi)[h]
                if part == 0:
                    whole = [JT.at[l, q[0], :, c], OT.at[l, q[0], :, c]]
                    halves = [JT.at[l, q[0], h, c], OT.at[l, q[0], h, c]]
                elif part == 1:
                    whole, halves = [E.at[l, c, :, q[1], :]], [E.at[l, c, half, q[1], :]]
                else:
                    whole, halves = [S.at[l, c, :, :, q[2]]], [S.at[l, c, half, :, q[2]]]
                for ref in halves:
                    f.append((link.send(ref, ref, axis, (1, 3)[side]), h))
                for ref in whole:
                    to_sibling(ref)
            ph3f[l, part] = f
    for l in range(L):
        for part in (1, 2, 0):
            axis = (0, 1, 2)[part]
            q = moved(co, axis, 2)
            for n, (cp, h) in enumerate(ph3f[l, part]):
                cp.wait_recv()
                half = (lo, hi)[h]
                if part == 0:
                    ref = (JT, OT)[n % 2].at[l, q[0], h, c]
                elif part == 1:
                    ref = E.at[l, c, half, q[1], :]
                else:
                    ref = S.at[l, c, half, :, q[2]]
                to_sibling(ref)
    gains_all[...] = gain_sum.total()
    for cp in sib:
        cp.wait_recv()
    for cp in loc_out:
        cp.wait()
    link.drain()

def gather(pa, pb, pc, gains):
    L = pa.shape[0]
    sd = jax.ShapeDtypeStruct
    return pl.pallas_call(functools.partial(gather_kernel, L),
        out_shape=(sd((L, 4, 2, 2, 144, 768), BF), sd((L, 4, 2, 2, 48, 768), BF), sd((L, 2, 4, 4, 4, 24, 768), BF), sd((L, 2, 4, 4, 4, 24, 768), BF), sd(gains.shape, F32)),
        in_specs=[pl.BlockSpec(memory_space=pl.ANY)] * 3 + [pl.BlockSpec(memory_space=pltpu.VMEM)],
        out_specs=(pl.BlockSpec(memory_space=pl.ANY),) * 4 + (pl.BlockSpec(memory_space=pltpu.VMEM),),
        scratch_shapes=[pltpu.VMEM((L, 4, 4, 24, 768), BF), pltpu.VMEM((288, 768), F32), pltpu.VMEM((96, 768), F32),
            pltpu.VMEM((L, 2, 144, 768), BF), pltpu.VMEM((L, 2, 48, 768), BF),
            pltpu.VMEM((4, 4, *gains.shape), F32),
            pltpu.SemaphoreType.DMA((L * 64 + 16,)), pltpu.SemaphoreType.DMA((L * 64 + 16,)), pltpu.SemaphoreType.DMA((L * 8,))],
        compiler_params=pltpu.CompilerParams(collective_id=0, has_side_effects=True, vmem_limit_bytes=32 << 20))(pa, pb, pc, gains)


def acc(dst, srcs, lead):
    total = 1
    for d in lead:
        total *= d
    def body(t, carry):
        idx = []
        for d in reversed(lead):
            idx.append(lax.rem(t, d))
            t = t // d
        idx = tuple(reversed(idx))
        v = srcs[0][idx].astype(F32)
        for s in srcs[1:]:
            v = v + s[idx].astype(F32)
        dst[idx] = v.astype(dst.dtype)
        return carry
    lax.fori_loop(0, total, body, 0)

def reduce_kernel(L, *refs):
    n_in = 4 * L
    grads = refs[:n_in]
    gain_in = refs[n_in]
    outA, outB, outC, gain_out, norm_out = refs[n_in + 1:n_in + 6]
    (oJ, oO, oE, oS, sJ, sO, sE, sS, r1J, r1O, r1E, r1S, r2J, r2O, r2E, r2S, fJ, fO, r3, t1, t2, r4, u1,
     gbuf, nbuf, ss, rs, ls) = refs[n_in + 6:]
    co = place()
    x, y, z, c = co
    greet(co)
    link, loc = Link(co, ss, rs), Local(ls)
    other = 1 - c
    order = [(l, p) for l in reversed(range(L)) for p in range(3)]
    first = (0, 1, 2)
    second = (1, 2, 0)
    third = (2, 0, 1)

    def src_block(l, part, q, cc):
        J, O, E, S = grads[4 * l:4 * l + 4]
        if part == 0:
            return [J.at[q, :, cc], O.at[q, :, cc]]
        if part == 1:
            return [E.at[cc, :, q]]
        return [S.at[cc, :, :, q]]
    def own_block(l, part, k):
        if part == 0:
            return [oJ.at[l, k], oO.at[l, k]]
        return [(oE, oS)[part - 1].at[l, k]]
    def sib_block(l, part, k):
        if part == 0:
            return [sJ.at[l, k], sO.at[l, k]]
        return [(sE, sS)[part - 1].at[l, k]]
    def buf(r, l, part, *k):
        if part == 0:
            return [r[0].at[(l, *k)], r[1].at[(l, *k)]]
        return [r[part + 1].at[(l, *k)]]
    r1 = (r1J, r1O, r1E, r1S)
    r2 = (r2J, r2O, r2E, r2S)
    def half(rs_, part, h):
        return [r.at[pl.ds(h * (1 if part == 0 else 2), 1 if part == 0 else 2)] for r in rs_]
    def lead(part, halved):
        return (1 if halved else 2,) if part == 0 else ((2 if halved else 4), 4)
    def add(dsts, srcs, part, halved):
        for n, d in enumerate(dsts):
            acc(d, [s[n] for s in srcs], lead(part, halved))
    def send(srcs, dsts, axis, k):
        return [link.send(s, d, axis, k) for s, d in zip(srcs, dsts)]

    arrive = {}
    dist = (2, 1, 3, 0)
    for l, p in order:
        for k in dist:
            q = moved(co, first[p], k)[first[p]]
            mine = [loc.copy(s, d) for s, d in zip(src_block(l, p, q, c), own_block(l, p, k))]
            sibs = send(src_block(l, p, q, other), sib_block(l, p, k), 3, 1)
            arrive[l, p, k] = (mine, sibs)
    def join(l, p, k):
        mine, sibs = arrive[l, p, k]
        for cp in mine:
            cp.wait()
        for cp in sibs:
            cp.wait_recv()
        add(own_block(l, p, k), [own_block(l, p, k), sib_block(l, p, k)], p, False)

    gain_sum = RowSum(link, gbuf)
    gain_sum.send(gain_in[...])

    step1 = {}
    for l, p in order:
        join(l, p, 2)
        a = first[p]
        o = own_block(l, p, 2)
        step1[l, p] = (send(half(o, p, 0), buf(r1, l, p, 0), a, 1), send(half(o, p, 1), buf(r1, l, p, 1), a, 3))
    gain_sum.send(gain_sum.total())
    step2 = {}
    for l, p in order:
        a = first[p]
        join(l, p, 1)
        join(l, p, 3)
        step2[l, p] = send(half(own_block(l, p, 1), p, 1), half(buf(r2, l, p, 0), p, 1), a, 1) + \
            send(half(own_block(l, p, 3), p, 0), half(buf(r2, l, p, 1), p, 0), a, 3)
    gain_sum.send(gain_sum.total())
    for l, p in order:
        a = first[p]
        for side, k in ((0, 1), (1, 3)):
            for cp in step1[l, p][side]:
                cp.wait_recv()
            o = half(own_block(l, p, k), p, side)
            add(o, [o, buf(r1, l, p, side)], p, True)
            step2[l, p] += send(o, half(buf(r2, l, p, side), p, side), a, k)
    gain_sum.send(gain_sum.total())
    for l, p in order:
        join(l, p, 0)
    gain_out[...] = gain_sum.total()
    def small(l, p, q):
        return r3.at[l, p, q] if p != 1 else r3.at[l, p, :, q]
    step3 = {}
    for l, p in order:
        for cp in step2[l, p]:
            cp.wait_recv()
        o, a, b = own_block(l, p, 0), buf(r2, l, p, 0), buf(r2, l, p, 1)
        if p == 0:
            for h in range(2):
                for n, (f, rows) in enumerate(((fJ, 144), (fO, 48))):
                    f[h * rows:(h + 1) * rows] = o[n][h].astype(F32) + a[n][h].astype(F32) + b[n][h].astype(F32)
            for yy in range(4):
                for zz in range(4):
                    at = (yy // 2) * 144 + ((yy % 2) * 4 + zz) * 18
                    stage_j = fJ[at:at + 18]
                    at = (yy // 2) * 48 + ((yy % 2) * 4 + zz) * 6
                    r3[l, 0, yy, zz] = jnp.concatenate([stage_j, fO[at:at + 6]], axis=0).astype(BF)
        else:
            acc(r3.at[l, p], [o[0], a[0], b[0]], (4, 4))
        ax = second[p]
        me = co[ax]
        def blk(k, h=None, l=l, p=p, me=me):
            q = lax.rem(me + k, 4)
            s = slice(None) if h is None else pl.ds(2 * h, 2)
            return r3.at[l, p, q, s] if p != 1 else r3.at[l, p, s, q]
        step3[l, p] = ([link.send(blk(2, 0), t1.at[l, p, 0], ax, 1), link.send(blk(2, 1), t1.at[l, p, 1], ax, 3)],
                       [link.send(blk(1, 1), t2.at[l, p, 0, pl.ds(2, 2)], ax, 1), link.send(blk(3, 0), t2.at[l, p, 1, pl.ds(0, 2)], ax, 3)], blk)
    for l, p in order:
        hop1, hop2, blk = step3[l, p]
        ax = second[p]
        for side, k in ((0, 1), (1, 3)):
            hop1[side].wait_recv()
            o = blk(k, side)
            acc(o, [o, t1.at[l, p, side]], (2,))
            hop2.append(link.send(o, t2.at[l, p, side, pl.ds(2 * side, 2)], ax, k))
    step4 = {}
    for l, p in order:
        hop1, hop2, blk = step3[l, p]
        for cp in hop2:
            cp.wait_recv()
        acc(r4.at[l, p], [blk(0), t2.at[l, p, 0], t2.at[l, p, 1]], (4,))
        ax = third[p]
        me = co[ax]
        step4[l, p] = [link.send(r4.at[l, p, lax.rem(me + k, 4)], u1.at[l, p, k - 1], ax, k) for k in (1, 3, 2)]
    square = jnp.zeros((24, 768), F32)
    for l, p in order:
        for cp in step4[l, p]:
            cp.wait_recv()
        v = r4[l, p, co[third[p]]].astype(F32) + u1[l, p, 0].astype(F32) + u1[l, p, 1].astype(F32) + u1[l, p, 2].astype(F32)
        (outA, outB, outC)[p][l] = v
        square = square + v * v
    part_sum = square[0:8] + square[8:16] + square[16:24]
    tile = part_sum[:, 0:128]
    for n in range(1, 6):
        tile = tile + part_sum[:, n * 128:(n + 1) * 128]
    norm_sum = RowSum(link, nbuf)
    for n in range(4):
        norm_sum.send(tile)
        tile = norm_sum.total()
    norm_out[...] = tile
    link.drain()

def reduce_all(grads, gains):
    L = len(grads)
    sd = jax.ShapeDtypeStruct
    V = pltpu.VMEM
    vm = pl.BlockSpec(memory_space=pltpu.VMEM)
    flat = [g for layer in grads for g in layer]
    blk = lambda *lead: [V((L, *lead, 2, 144, 768), BF), V((L, *lead, 2, 48, 768), BF), V((L, *lead, 4, 4, 24, 768), BF), V((L, *lead, 4, 4, 24, 768), BF)]
    hblk = [V((L, 2, 1, 144, 768), BF), V((L, 2, 1, 48, 768), BF), V((L, 2, 2, 4, 24, 768), BF), V((L, 2, 2, 4, 24, 768), BF)]
    return pl.pallas_call(functools.partial(reduce_kernel, L),
        out_shape=(sd((L, 24, 768), F32),) * 3 + (sd(gains.shape, F32), sd((8, 128), F32)),
        in_specs=[pl.BlockSpec(memory_space=pl.ANY)] * len(flat) + [vm],
        out_specs=(vm,) * 5,
        scratch_shapes=blk(4) + blk(4) + hblk + blk(2) + [V((288, 768), F32), V((96, 768), F32), V((L, 3, 4, 4, 24, 768), BF),
            V((L, 3, 2, 2, 24, 768), BF), V((L, 3, 2, 4, 24, 768), BF), V((L, 3, 4, 24, 768), BF), V((L, 3, 3, 24, 768), BF),
            V((4, 4, 8, 768), F32), V((4, 4, 8, 128), F32),
            pltpu.SemaphoreType.DMA((L * 64 + 32,)), pltpu.SemaphoreType.DMA((L * 64 + 32,)), pltpu.SemaphoreType.DMA((L * 16,))],
        compiler_params=pltpu.CompilerParams(collective_id=1, has_side_effects=True, vmem_limit_bytes=60 << 20))(*flat, gains)


D = 768
HEADS = 12
HEAD_DIM = 64
LAYERS = 2
STEP = 5


highest = lax.Precision.HIGHEST
beta_first = 0.9
beta_second = 0.999
adam_epsilon = 1e-08
decay_matrix = 0.1
rate_matrix = 0.05
rate_gains = 0.25
clip_limit = 1.0
norm_epsilon = 1e-05
masked_value = -1e30


def layer_norm(features, gain_row, shift_row):
    mean_value = jnp.mean(features, axis=-1, keepdims=True)
    centred = features - mean_value
    variance = jnp.mean(centred * centred, axis=-1, keepdims=True)
    return centred * lax.rsqrt(variance + norm_epsilon) * gain_row + shift_row


def gelu_tanh(raised):
    return jax.nn.gelu(raised, approximate=True)


def adam_update(master, gradient, moment, square, rate, decay, clip_factor):
    clipped = gradient * clip_factor
    momentum = beta_first * moment + (1.0 - beta_first) * clipped
    variance = beta_second * square + (1.0 - beta_second) * clipped * clipped
    corrected_first = momentum / (1.0 - beta_first**STEP)
    corrected_second = variance / (1.0 - beta_second**STEP)
    updated = master - rate * (
        corrected_first / (jnp.sqrt(corrected_second) + adam_epsilon) + decay * master
    )
    return (updated, momentum, variance)


def split_heads(projected, offset):
    row_count = projected.shape[0]
    return projected[:, offset * D : (offset + 1) * D].reshape(row_count, HEADS, HEAD_DIM)


def attention_logits(query_rows, key_rows, masks):
    allowed, selectable, earlier = masks
    scores = jnp.einsum(
        "ihd,jhd->hij", query_rows, key_rows, preferred_element_type=jnp.float32
    ) * HEAD_DIM ** (-0.5)
    chosen = jnp.where(selectable, jax.nn.softplus(scores[0]), 0.0)
    forget = jnp.dot(earlier, chosen, precision=highest)
    logits = jnp.where(allowed[None], scores - forget[None], masked_value)
    return (scores, logits)


def rows_of(features, weight_rows):
    return jnp.einsum("te,ce->tc", features, weight_rows, preferred_element_type=jnp.float32)


def weight_grad(left, right):
    return jnp.einsum("tc,te->ce", left, right, preferred_element_type=jnp.float32).astype(BF)


def layer_forward(stream, weights, masks):
    joint_full, output_full, expand_full, shrink_full, gains_full = weights
    row_count = stream.shape[0]
    gains = gains_full.astype(jnp.float32)
    normed = layer_norm(stream, gains[0], gains[1]).astype(jnp.bfloat16)
    projected = rows_of(normed, joint_full).astype(jnp.bfloat16)
    query_rows = split_heads(projected, 0)
    key_rows = split_heads(projected, 1)
    value_rows = split_heads(projected, 2)
    scores, logits = attention_logits(query_rows, key_rows, masks)
    row_max = jnp.max(logits, axis=-1, keepdims=True)
    shifted = jnp.exp(logits - row_max)
    row_total = jnp.sum(shifted, axis=-1, keepdims=True)
    softmax_low = (shifted / row_total).astype(jnp.bfloat16)
    log_total = row_max + jnp.log(row_total)
    attended = jnp.einsum(
        "hij,jhd->ihd", softmax_low, value_rows, preferred_element_type=jnp.float32
    )
    attended = attended.reshape(row_count, D).astype(jnp.bfloat16)
    stream_mid = stream + rows_of(attended, output_full)
    normed_second = layer_norm(stream_mid, gains[2], gains[3]).astype(jnp.bfloat16)
    raised = rows_of(normed_second, expand_full)
    hidden = gelu_tanh(raised).astype(jnp.bfloat16)
    stream_next = stream_mid + jnp.dot(hidden, shrink_full, preferred_element_type=jnp.float32)
    saved = (
        stream,
        normed,
        projected,
        log_total,
        attended,
        stream_mid,
        normed_second,
        raised,
        hidden,
    )
    return (stream_next, saved)


def layer_backward(dstream, weights, saved, masks):
    joint_full, output_full, expand_full, shrink_full, gains_full = weights
    stream, normed, projected, log_total, attended, stream_mid, normed_second, raised, hidden = (
        saved
    )
    allowed, selectable, earlier = masks
    row_count = stream.shape[0]
    gains = gains_full.astype(jnp.float32)
    dbranch = dstream.astype(jnp.bfloat16)
    shrink_grad = weight_grad(hidden, dbranch)
    dhidden = jnp.einsum("td,fd->tf", dbranch, shrink_full, preferred_element_type=jnp.float32)
    gelu_value, gelu_pull = jax.vjp(gelu_tanh, raised)
    draised = gelu_pull(dhidden)[0].astype(jnp.bfloat16)
    expand_grad = weight_grad(draised, normed_second)
    dnormed_second = jnp.einsum(
        "tf,fe->te", draised, expand_full, preferred_element_type=jnp.float32
    )
    second_value, second_pull = jax.vjp(layer_norm, stream_mid, gains[2], gains[3])
    dmiddle, dgain_second, dshift_second = second_pull(dnormed_second)
    dstream_mid = dstream + dmiddle
    dattn = dstream_mid.astype(jnp.bfloat16)
    output_grad = weight_grad(dattn, attended)
    dattended = jnp.einsum("td,de->te", dattn, output_full, preferred_element_type=jnp.float32)
    dattended = dattended.astype(jnp.bfloat16).reshape(row_count, HEADS, HEAD_DIM)
    query_rows = split_heads(projected, 0)
    key_rows = split_heads(projected, 1)
    value_rows = split_heads(projected, 2)
    scores, logits = attention_logits(query_rows, key_rows, masks)
    softmax_full = jnp.exp(logits - log_total)
    softmax_low = softmax_full.astype(jnp.bfloat16)
    dsoft = jnp.einsum("ihd,jhd->hij", dattended, value_rows, preferred_element_type=jnp.float32)
    dvalues = jnp.einsum("hij,ihd->jhd", softmax_low, dattended, preferred_element_type=jnp.float32)
    dlogits = softmax_full * (dsoft - jnp.sum(softmax_full * dsoft, axis=-1, keepdims=True))
    dforget = -jnp.sum(dlogits, axis=0)
    dchosen = jnp.dot(earlier.T, dforget, precision=highest)
    slope = jax.nn.sigmoid(scores[0])
    head_zero = dlogits[0] + jnp.where(selectable, dchosen * slope, 0.0)
    dscores = jnp.concatenate([head_zero[None], dlogits[1:]], axis=0).astype(jnp.bfloat16)
    score_scale = HEAD_DIM ** (-0.5)
    dqueries = (
        jnp.einsum("hij,jhd->ihd", dscores, key_rows, preferred_element_type=jnp.float32)
        * score_scale
    )
    dkeys = (
        jnp.einsum("hij,ihd->jhd", dscores, query_rows, preferred_element_type=jnp.float32)
        * score_scale
    )
    dprojected = jnp.concatenate(
        [
            dqueries.reshape(row_count, D),
            dkeys.reshape(row_count, D),
            dvalues.reshape(row_count, D),
        ],
        axis=1,
    ).astype(jnp.bfloat16)
    joint_grad = weight_grad(dprojected, normed)
    dnormed = jnp.einsum("tc,ce->te", dprojected, joint_full, preferred_element_type=jnp.float32)
    first_value, first_pull = jax.vjp(layer_norm, stream, gains[0], gains[1])
    dinput, dgain_first, dshift_first = first_pull(dnormed)
    dstream_in = dstream_mid + dinput
    gains_grad = jnp.stack([dgain_first, dshift_first, dgain_second, dshift_second])
    return (dstream_in, (joint_grad, output_grad, expand_grad, shrink_grad, gains_grad))


def local(
    tokens,
    lengths,
    cotangent,
    joint_weight,
    output_weight,
    expand_weight,
    shrink_weight,
    layer_gains,
    joint_moment,
    output_moment,
    expand_moment,
    shrink_moment,
    gains_moment,
    joint_square,
    output_square,
    expand_square,
    shrink_square,
    gains_square,
):
    row_count = tokens.shape[0]
    positions = jnp.arange(row_count, dtype=jnp.int32)
    live_rows = positions < lengths[0]
    allowed = (positions[None, :] <= positions[:, None]) & live_rows[None, :]
    selectable = (
        (positions[None, :] > 0) & (positions[None, :] < positions[:, None]) & live_rows[:, None]
    )
    earlier = (positions[None, :] < positions[:, None]).astype(jnp.float32)
    masks = (allowed, selectable, earlier)
    swap = lambda a: a.transpose(0, 2, 1)
    rows_a = jnp.concatenate([swap(joint_weight), swap(output_weight)], axis=1).astype(BF)
    which_device = lax.axis_index("dp") * 8 + lax.axis_index("fsdp")
    gains_rows = lax.dynamic_update_slice(
        jnp.zeros((8, D), F32), layer_gains.astype(BF).astype(F32).reshape(8, 6), (0, which_device * 6)
    )
    joint_all, output_all, expand_all, shrink_all, gains_all = gather(
        rows_a, swap(expand_weight).astype(BF), shrink_weight.astype(BF), gains_rows
    )
    gains_all = gains_all.reshape(LAYERS, 4, D)
    weights = [
        (
            joint_all[l].reshape(3 * D, D),
            output_all[l].reshape(D, D),
            expand_all[l].reshape(4 * D, D),
            shrink_all[l].reshape(4 * D, D),
            gains_all[l],
        )
        for l in range(LAYERS)
    ]
    stream = tokens.astype(jnp.float32)
    saved_layers = []
    for l in range(LAYERS):
        stream, saved = layer_forward(stream, weights[l], masks)
        saved_layers.append(saved)
    layer_output = stream.astype(jnp.bfloat16)
    dstream = cotangent.astype(jnp.float32) * live_rows[:, None].astype(jnp.float32)
    gradients = [None] * LAYERS
    for l in reversed(range(LAYERS)):
        dstream, gradients[l] = layer_backward(dstream, weights[l], saved_layers[l], masks)
    blocks = [
        (
            g[0].reshape(4, 2, 2, 144, D),
            g[1].reshape(4, 2, 2, 48, D),
            g[2].reshape(2, 4, 4, 4, 24, D),
            g[3].reshape(2, 4, 4, 4, 24, D),
        )
        for g in gradients
    ]
    gains_grad = jnp.concatenate([g[4] for g in gradients], axis=0)
    sum_a, sum_b, sum_c, gains_sum, squares = reduce_all(blocks, gains_grad)
    gains_own = lax.dynamic_slice(gains_sum, (0, which_device * 6), (8, 6)).reshape(LAYERS, 4, 6)
    stacked = [swap(sum_a[:, :18]), swap(sum_a[:, 18:]), swap(sum_b), sum_c, gains_own]
    total_square = jnp.sum(squares) + jnp.sum(gains_sum * gains_sum)
    gradient_norm = jnp.sqrt(total_square)
    clip_factor = jnp.minimum(1.0, clip_limit / (gradient_norm + 1e-06))
    joint_new = adam_update(
        joint_weight, stacked[0], joint_moment, joint_square, rate_matrix, decay_matrix, clip_factor
    )
    output_new = adam_update(
        output_weight,
        stacked[1],
        output_moment,
        output_square,
        rate_matrix,
        decay_matrix,
        clip_factor,
    )
    expand_new = adam_update(
        expand_weight,
        stacked[2],
        expand_moment,
        expand_square,
        rate_matrix,
        decay_matrix,
        clip_factor,
    )
    shrink_new = adam_update(
        shrink_weight,
        stacked[3],
        shrink_moment,
        shrink_square,
        rate_matrix,
        decay_matrix,
        clip_factor,
    )
    gains_new = adam_update(
        layer_gains, stacked[4], gains_moment, gains_square, rate_gains, 0.0, clip_factor
    )
    return (
        layer_output,
        dstream,
        gradient_norm,
        joint_new[0],
        output_new[0],
        expand_new[0],
        shrink_new[0],
        gains_new[0],
        joint_new[1],
        output_new[1],
        expand_new[1],
        shrink_new[1],
        gains_new[1],
        joint_new[2],
        output_new[2],
        expand_new[2],
        shrink_new[2],
        gains_new[2],
    )


def solution(mesh):
    in_specs = (
        P(("dp", "fsdp"), None),
        P(("dp", "fsdp")),
        P(("dp", "fsdp"), None),
        P(None, None, ("dp", "fsdp")),
        P(None, None, ("dp", "fsdp")),
        P(None, None, ("dp", "fsdp")),
        P(None, ("dp", "fsdp"), None),
        P(None, None, ("dp", "fsdp")),
        P(None, None, ("dp", "fsdp")),
        P(None, None, ("dp", "fsdp")),
        P(None, None, ("dp", "fsdp")),
        P(None, ("dp", "fsdp"), None),
        P(None, None, ("dp", "fsdp")),
        P(None, None, ("dp", "fsdp")),
        P(None, None, ("dp", "fsdp")),
        P(None, None, ("dp", "fsdp")),
        P(None, ("dp", "fsdp"), None),
        P(None, None, ("dp", "fsdp")),
    )
    out_specs = (
        P(("dp", "fsdp"), None),
        P(("dp", "fsdp"), None),
        P(),
        P(None, None, ("dp", "fsdp")),
        P(None, None, ("dp", "fsdp")),
        P(None, None, ("dp", "fsdp")),
        P(None, ("dp", "fsdp"), None),
        P(None, None, ("dp", "fsdp")),
        P(None, None, ("dp", "fsdp")),
        P(None, None, ("dp", "fsdp")),
        P(None, None, ("dp", "fsdp")),
        P(None, ("dp", "fsdp"), None),
        P(None, None, ("dp", "fsdp")),
        P(None, None, ("dp", "fsdp")),
        P(None, None, ("dp", "fsdp")),
        P(None, None, ("dp", "fsdp")),
        P(None, ("dp", "fsdp"), None),
        P(None, None, ("dp", "fsdp")),
    )
    return jax.shard_map(local, mesh=mesh, in_specs=in_specs, out_specs=out_specs, check_vma=False)
```

```python
import jax
import jax.numpy as jnp
from jax import lax
from jax.experimental import pallas as pl
from jax.experimental.pallas import tpu as pltpu
from jax.sharding import PartitionSpec as P

MESH = pl.DeviceIdType.MESH
BF = jnp.bfloat16
F32 = jnp.float32

def place():
    dp = lax.axis_index("dp"); fs = lax.axis_index("fsdp")
    return (dp // 4, lax.rem(dp // 2, 2) * 2 + fs // 4, lax.rem(fs, 4), lax.rem(dp, 2))

def device_at(x, y, z, c):
    return ((x * 2 + y // 2) * 2 + c, lax.rem(y, 2) * 4 + z)

def moved(co, axis, k):
    n = 2 if axis == 3 else 4
    co = list(co)
    co[axis] = lax.rem(co[axis] + (k % n), n)
    return tuple(co)

def greet(co):
    bar = pltpu.get_barrier_semaphore()
    peers = [(a, k) for a in range(3) for k in (1, 2, 3)] + [(3, 1)]
    for a, k in peers:
        pl.semaphore_signal(bar, inc=1, device_id=device_at(*moved(co, a, k)), device_id_type=MESH)
    pl.semaphore_wait(bar, len(peers))

class Link:
    def __init__(self, co, ss, rs):
        self.co, self.ss, self.rs = co, ss, rs
        self.n = 0
        self.out = []
    def send(self, src, dst, axis, k):
        i = self.n
        self.n += 1
        cp = pltpu.make_async_remote_copy(src_ref=src, dst_ref=dst, send_sem=self.ss.at[i], recv_sem=self.rs.at[i],
            device_id=device_at(*moved(self.co, axis, k)), device_id_type=MESH)
        cp.start()
        self.out.append(cp)
        return cp
    def drain(self):
        for cp in self.out:
            cp.wait_send()

class Local:
    def __init__(self, sems):
        self.sems, self.n = sems, 0
    def copy(self, src, dst):
        cp = pltpu.make_async_copy(src, dst, self.sems.at[self.n])
        self.n += 1
        cp.start()
        return cp

class RowSum:
    def __init__(self, link, slots):
        self.link, self.slots, self.n = link, slots, 0

    def send(self, value):
        axis = (2, 1, 0, 3)[self.n]
        mine = self.slots.at[self.n, self.link.co[axis]]
        mine[...] = value
        self.going = [self.link.send(mine, mine, axis, k) for k in ((1, 3, 2) if axis < 3 else (1,))]

    def total(self):
        for cp in self.going:
            cp.wait_recv()
        count = 4 if self.n < 3 else 2
        value = self.slots[self.n, 0]
        for k in range(1, count):
            value = value + self.slots[self.n, k]
        self.n += 1
        return value


def acc(dst, srcs, lead):
    total = 1
    for d in lead:
        total *= d
    def body(t, carry):
        idx = []
        for d in reversed(lead):
            idx.append(lax.rem(t, d))
            t = t // d
        idx = tuple(reversed(idx))
        v = srcs[0][idx].astype(F32)
        for s in srcs[1:]:
            v = v + s[idx].astype(F32)
        dst[idx] = v.astype(dst.dtype)
        return carry
    lax.fori_loop(0, total, body, 0)


D = 768
LAYERS = 2
STEP = 5
beta_first = 0.9
beta_second = 0.999
adam_epsilon = 1e-08
decay_matrix = 0.1
rate_matrix = 0.05
rate_gains = 0.25
clip_limit = 1.0
HEADS = 12
HEAD_DIM = 64
T = 256
norm_epsilon = 1e-05
SQ = 0.7978845608028654
CUBE = 0.044715
highest = lax.Precision.HIGHEST


def dot_of(a, b, dims, **kw):
    return lax.dot_general(a, b, (dims, ((), ())), preferred_element_type=F32, **kw)


def dot_nt(a, b):
    return dot_of(a, b, ((1,), (1,)))


def dot_nn(a, b):
    return dot_of(a, b, ((1,), (0,)))


def dot_tn(a, b):
    return dot_of(a, b, ((0,), (0,)))


def loop(n, fn):
    def body(t, carry):
        fn(t)
        return carry
    lax.fori_loop(0, n, body, 0)


def tile(t, size):
    return pl.ds(pl.multiple_of(t * size, size), size)


def stats(v):
    centred = v - jnp.mean(v, axis=-1, keepdims=True)
    scale = lax.rsqrt(jnp.mean(centred * centred, axis=-1, keepdims=True) + norm_epsilon)
    return centred * scale, scale


def norm_rows(src, dst, gain, shift):
    def step(t):
        r = tile(t, 64)
        unit, _ = stats(src[r, :].astype(F32))
        dst[r, :] = (unit * gain + shift).astype(BF)
    loop(T // 64, step)


def norm_back(src, grad, base, dst, gain, low_dst):
    def step(t, carry):
        to_gain, to_shift = carry
        r = tile(t, 64)
        unit, scale = stats(src[r, :].astype(F32))
        g = grad[r, :]
        to_gain = to_gain + jnp.sum((g * unit).reshape(8, 8, D), axis=0)
        to_shift = to_shift + jnp.sum(g.reshape(8, 8, D), axis=0)
        g = g * gain
        out = base[r, :] + scale * (
            g - jnp.mean(g, axis=-1, keepdims=True) - unit * jnp.mean(g * unit, axis=-1, keepdims=True)
        )
        dst[r, :] = out
        if low_dst is not None:
            low_dst[r, :] = out.astype(BF)
        return (to_gain, to_shift)
    zero = jnp.zeros((8, D), F32)
    to_gain, to_shift = lax.fori_loop(0, T // 64, step, (zero, zero))
    return jnp.sum(to_gain, axis=0, keepdims=True), jnp.sum(to_shift, axis=0, keepdims=True)


def grids():
    return lax.broadcasted_iota(jnp.int32, (T, T), 0), lax.broadcasted_iota(jnp.int32, (T, T), 1)


def halves(pair):
    lane = lax.broadcasted_iota(jnp.int32, (T, 128), 1)
    zero = jnp.zeros_like(pair)
    return jnp.where(lane < HEAD_DIM, pair, zero), jnp.where(lane < HEAD_DIM, zero, pair)


SCALE = HEAD_DIM ** -0.5
FT = 384


def slots_at(ref, t):
    return ref[t // 4, lax.rem(t, 4)].reshape(FT, D)


def put_slots(ref, t, value):
    ref[t // 4, lax.rem(t, 4)] = value.reshape(4, 4, 24, D).astype(BF)


def first_scores(proj):
    q, _ = halves(proj[:, 0:128])
    return dot_nt(q * jnp.asarray(SCALE, BF), proj[:, D:D + 128])


def attention(proj, probs, attended, bias, length):
    row, col = grids()
    scores = first_scores(proj)
    chosen = jnp.maximum(scores, 0.0) + jnp.log(1.0 + jnp.exp(-jnp.abs(scores)))
    chosen = jnp.where((col > 0) & (col < row) & (row < length), chosen, 0.0)
    forget = dot_of((col < row).astype(F32), chosen, ((1,), (0,)), precision=highest)
    bias[...] = jnp.where((col <= row) & (col < length), forget, 1e30)

    def pair(p):
        at = tile(p, 128)
        q = halves(proj[:, at] * jnp.asarray(SCALE, BF))
        k = proj[:, tile(6 + p, 128)]
        v = halves(proj[:, tile(12 + p, 128)])
        total = None
        for h in range(2):
            logits = dot_nt(q[h], k) - bias[...]
            e = jnp.exp(logits - jnp.max(logits, axis=-1, keepdims=True))
            e = (e * (1.0 / jnp.sum(e, axis=-1, keepdims=True))).astype(BF)
            probs[2 * p + h] = e
            part = dot_nn(e, v[h])
            total = part if h == 0 else total + part
        attended[:, at] = total.astype(BF)
    loop(6, pair)


def forward_first(s, gains, length):
    norm_rows(s.stream, s.normed, gains[0:1], gains[1:2])
    s.need("wj")
    wj = s.wj.reshape(3 * D, D)
    def project(t):
        s.proj[:, tile(t, 256)] = dot_nt(s.normed[...], wj[tile(t, 256), :]).astype(BF)
    loop(9, project)
    attention(s.proj, s.probs, s.attended, s.bias, length)
    s.need("wo")
    wo = s.wo.reshape(D, D)
    def output(t):
        at = tile(t, 256)
        s.mid[:, at] = s.stream[:, at].astype(F32) + dot_nt(s.attended[...], wo[at, :])
    loop(3, output)


def forward_second(s, gains):
    norm_rows(s.mid, s.normed2, gains[2:3], gains[3:4])
    s.need("we")
    def raise_(t):
        at = tile(t, FT)
        r = dot_nt(s.normed2[...], slots_at(s.we, t))
        s.raised[:, at] = r
        s.hidden[:, at] = (0.5 * r * (1.0 + jnp.tanh(r * (SQ + SQ * CUBE * r * r)))).astype(BF)
    loop(4 * D // FT, raise_)
    s.need("ws")
    def lower(t):
        at = tile(t, 256)
        s.next[:, at] = s.mid[:, at] + dot_nn(s.hidden[...], s.ws[:, :, :, :, :, at].reshape(4 * D, 256))
    loop(3, lower)


def backward_second(s, gains):
    for name in ("dstream", "ws", "raised", "we", "normed2"):
        s.need(name)
    s.low[...] = s.dstream[...].astype(BF)
    s.acc[...] = jnp.zeros((T, D), F32)
    def step(t):
        at = tile(t, FT)
        dh = dot_nt(s.low[...], slots_at(s.ws, t))
        r = s.raised[:, at]
        th = jnp.tanh(r * (SQ + SQ * CUBE * r * r))
        hid = (0.5 * r * (1.0 + th)).astype(BF)
        slope = 0.5 * (1.0 + th) + 0.5 * r * (1.0 - th * th) * (SQ + 3.0 * SQ * CUBE * r * r)
        dr = (dh * slope).astype(BF)
        put_slots(s.ws, t, dot_tn(hid, s.low[...]))
        s.acc[...] += dot_nn(dr, slots_at(s.we, t))
        put_slots(s.we, t, dot_tn(dr, s.normed2[...]))
    pieces = 4 * D // FT // 2
    for piece in range(pieces):
        loop(2, lambda t: step(t + 2 * piece))
        if piece < pieces - 1:
            yield
    s.need("mid")
    s.sums += norm_back(s.mid, s.acc, s.dstream, s.dstream, gains[2:3], s.low)
    yield


def attention_back(proj, probs, dout, dproj, bias, keep, length):
    bias[...] = jnp.zeros((T, T), F32)

    def scores_of(p, h, do, v):
        prob = probs[2 * p + h]
        full = prob.astype(F32)
        dsoft = dot_nt(do, v)
        dl = full * (dsoft - jnp.sum(full * dsoft, axis=-1, keepdims=True))
        bias[...] += dl
        return prob, dl

    def pair(p):
        at, at_k, at_v = tile(p, 128), tile(6 + p, 128), tile(12 + p, 128)
        q = halves(proj[:, at] * jnp.asarray(SCALE, BF))
        k = halves(proj[:, at_k] * jnp.asarray(SCALE, BF))
        v = proj[:, at_v]
        do = halves(dout[:, at])
        dq = dk = dv = None
        for h in range(2):
            prob, dl = scores_of(p, h, do[h], v)
            ds = dl.astype(BF)
            parts = (dot_nn(ds, k[h]), dot_tn(ds, q[h]), dot_tn(prob, do[h]))
            dq, dk, dv = parts if h == 0 else (dq + parts[0], dk + parts[1], dv + parts[2])
        dproj[:, at] = dq.astype(BF)
        dproj[:, at_k] = dk.astype(BF)
        dproj[:, at_v] = dv.astype(BF)
    loop(2, lambda t: pair(t + 1))
    yield
    loop(3, lambda t: pair(t + 3))
    yield

    q = halves(proj[:, 0:128] * jnp.asarray(SCALE, BF))
    k = halves(proj[:, D:D + 128] * jnp.asarray(SCALE, BF))
    v = proj[:, 2 * D:2 * D + 128]
    do = halves(dout[:, 0:128])
    prob1, dl1 = scores_of(0, 1, do[1], v)
    prob0, dl0 = scores_of(0, 0, do[0], v)
    keep[...] = dl0
    row, col = grids()
    dchosen = -dot_of((col > row).astype(F32), bias[...], ((1,), (0,)), precision=highest)
    scores = first_scores(proj)
    slope = 1.0 / (1.0 + jnp.exp(-scores))
    extra = jnp.where((col > 0) & (col < row) & (row < length), dchosen * slope, 0.0)
    ds0 = (keep[...] + extra).astype(BF)
    ds1 = dl1.astype(BF)
    dproj[:, 0:128] = (dot_nn(ds0, k[0]) + dot_nn(ds1, k[1])).astype(BF)
    dproj[:, D:D + 128] = (dot_tn(ds0, q[0]) + dot_tn(ds1, q[1])).astype(BF)
    dproj[:, 2 * D:2 * D + 128] = (dot_tn(prob0, do[0]) + dot_tn(prob1, do[1])).astype(BF)


def backward_first(s, gains, length):
    for name in ("wo", "attended", "proj", "probs"):
        s.need(name)
    wo, wj = s.wo.reshape(D, D), s.wj.reshape(3 * D, D)
    def back(t):
        at = tile(t, 256)
        s.dout[:, at] = dot_nn(s.low[...], wo[:, at]).astype(BF)
    loop(3, back)
    def grad(t):
        at = tile(t, 256)
        wo[at, :] = dot_tn(s.low[:, at], s.attended[...]).astype(BF)
    loop(3, grad)
    yield
    yield from attention_back(s.proj, s.probs, s.dout, s.dproj, s.bias, s.keep, length)
    yield
    s.need("wj")
    s.need("normed")
    s.acc[...] = jnp.zeros((T, D), F32)
    def joint(t):
        at = tile(t, 256)
        d = s.dproj[:, at]
        s.acc[...] += dot_nn(d, wj[at, :])
        wj[at, :] = dot_tn(d, s.normed[...]).astype(BF)
    for piece in range(3):
        loop(3, lambda t: joint(t + 3 * piece))
        yield
    s.need("stream")
    s.sums += norm_back(s.stream, s.acc, s.dstream, s.dstream, gains[0:1], None)


class Names:
    def __init__(self, **kw):
        self.__dict__.update(kw)
        self.coming = {}
        self.sums = ()

    def need(self, name):
        for cp in self.coming.pop(name, ()):
            cp.wait()


WEIGHTS = dict(wj=((4, 2, 2, 144, D), BF), wo=((4, 2, 2, 48, D), BF), we=((2, 4, 4, 4, 24, D), BF), ws=((2, 4, 4, 4, 24, D), BF))
SAVED = dict(mid=((T, D), F32), normed=((T, D), BF), normed2=((T, D), BF), proj=((T, 3 * D), BF), probs=((HEADS, T, T), BF),
    attended=((T, D), BF), raised=((T, 4 * D), F32))
ONCE = dict(bias=((T, T), F32), hidden=((T, 4 * D), BF), next=((T, D), F32))
BACK = dict(bias=((T, T), F32), keep=((T, T), F32), dstream=((T, D), F32), low=((T, D), BF), acc=((T, D), F32), dout=((T, D), BF),
    dproj=((T, 3 * D), BF))


def fetch(ins, s, loc, names):
    for n in names:
        s.coming[n] = [loc.copy(ins[n], getattr(s, n))]


def run(pieces):
    for _ in pieces:
        pass


def gains_of(sums):
    gain2, shift2, gain1, shift1 = sums
    return jnp.concatenate([gain1, shift1, gain2, shift2], axis=0)


def live_rows(length):
    return lax.broadcasted_iota(jnp.int32, (T, D), 0) < length


def gather_forward_body(ins, out, s, loc, link, co):
    x, y, z, c = co
    lo, hi = pl.ds(0, 2), pl.ds(2, 2)
    W = [[getattr(s, k) for k in WEIGHTS], [out["next_" + k] for k in WEIGHTS]]
    parts = (1, 2, 0)
    first, second, third = (2, 0, 1), (1, 2, 0), (0, 1, 2)
    length = ins["length"][0]
    fetch(ins, s, loc, ("stream",))
    gain_sum = RowSum(link, s.gbuf)
    gain_sum.send(ins["gains"][...])
    own, ph1, ph2, ph2f, ph3, ph3f, sib = {}, {}, {}, {}, {}, {}, {0: [], 1: []}

    def slots(l, part):
        return (s.abuf.at[l], W[l][2].at[c], W[l][3].at[c])[part]

    def start(l):
        for part in parts:
            src = (ins["pa"], ins["pb"], ins["pc"])[part].at[l]
            to = slots(l, part)
            dst = to.at[y, z] if part == 0 else to.at[x, y, z]
            own[l, part] = loc.copy(src, dst)
            ph1[l, part] = [link.send(src, dst, first[part], k) for k in (1, 3, 2)]

    def widen(l):
        for part in parts:
            own[l, part].wait()
            for cp in ph1[l, part]:
                cp.wait_recv()
            to = slots(l, part)
            ref = (lambda: to.at[y], lambda: to.at[:, y, z], lambda: to.at[x, :, z])[part]()
            ph2[l, part] = [link.send(ref, ref, second[part], 1), link.send(ref, ref, second[part], 3)]

    def widen_on(l):
        for part in parts:
            ph2f[l, part] = []
            to = slots(l, part)
            for side, (back, half) in enumerate(((3, lo), (1, hi))):
                ph2[l, part][side].wait_recv()
                q = moved(co, second[part], back)
                ref = (lambda: to.at[q[1], half], lambda: to.at[half, y, q[2]], lambda: to.at[q[0], half, z])[part]()
                ph2f[l, part].append(link.send(ref, ref, second[part], (1, 3)[side]))

    def compact(l):
        for cp in ph2f[l, 0]:
            cp.wait_recv()
        for yy in range(4):
            for zz in range(4):
                v = s.abuf[l, yy, zz].astype(F32)
                at = (yy // 2) * 144 + ((yy % 2) * 4 + zz) * 18
                s.jf[at:at + 18] = v[:18]
                at = (yy // 2) * 48 + ((yy % 2) * 4 + zz) * 6
                s.of[at:at + 6] = v[18:24]
        for h in range(2):
            s.jst[l, h] = s.jf[h * 144:h * 144 + 144].astype(BF)
            s.ost[l, h] = s.of[h * 48:h * 48 + 48].astype(BF)
        mine = [(s.jst.at[l], W[l][0].at[x, :, c]), (s.ost.at[l], W[l][1].at[x, :, c])]
        own[l] = [loc.copy(a, b) for a, b in mine]
        return mine

    def spread(l):
        for part in parts:
            if part == 0:
                pairs = compact(l)
            else:
                for cp in ph2f[l, part]:
                    cp.wait_recv()
                to = slots(l, part)
                ref = to.at[:, y, :] if part == 1 else to.at[:, :, z]
                pairs = [(ref, ref)]
            ph3[l, part] = [[link.send(a, b, third[part], k) for a, b in pairs] for k in (1, 3)]
            sib[l] += [link.send(a, b, 3, 1) for a, b in pairs]

    def pieces(l, part, q, h):
        half = None if h is None else (lo, hi)[h]
        if part == 0:
            at = (q[0], slice(None) if h is None else h, c)
            return [W[l][0].at[at], W[l][1].at[at]]
        to = slots(l, part)
        whole = slice(None) if h is None else half
        return [to.at[whole, q[1], :] if part == 1 else to.at[whole, :, q[2]]]

    def spread_on(l):
        for part in parts:
            ph3f[l, part] = []
            for side, (back, h) in enumerate(((3, 0), (1, 1))):
                for cp in ph3[l, part][side]:
                    cp.wait_recv()
                q = moved(co, third[part], back)
                for ref in pieces(l, part, q, h):
                    ph3f[l, part].append((link.send(ref, ref, third[part], (1, 3)[side]), h))
                for ref in pieces(l, part, q, None):
                    sib[l].append(link.send(ref, ref, 3, 1))

    def finish(l):
        for part in parts:
            q = moved(co, third[part], 2)
            for n, (cp, h) in enumerate(ph3f[l, part]):
                cp.wait_recv()
                refs = pieces(l, part, q, h)
                ref = refs[n % len(refs)]
                sib[l].append(link.send(ref, ref, 3, 1))

    def settle(l):
        for cp in sib[l]:
            cp.wait_recv()
        for cp in own[l]:
            cp.wait()

    start(0)
    start(1)
    widen(0)
    gain_sum.send(gain_sum.total())
    widen(1)
    widen_on(0)
    gain_sum.send(gain_sum.total())
    spread(0)
    widen_on(1)
    gain_sum.send(gain_sum.total())
    spread_on(0)
    out["gains_all"][...] = gain_sum.total()
    spread(1)
    finish(0)
    settle(0)
    done = [loc.copy(getattr(s, k), out[k]) for k in WEIGHTS]
    gains = out["gains_all"][0:4]
    s.need("stream")
    forward_first(s, gains, length)
    done += [loc.copy(getattr(s, k), out[k]) for k in ("normed", "proj", "probs", "attended", "mid")]
    spread_on(1)
    forward_second(s, gains)
    done += [loc.copy(getattr(s, k), out[k]) for k in ("normed2", "raised", "next")]
    finish(1)
    settle(1)
    for cp in done:
        cp.wait()
    link.drain()


def layer1_body(ins, out, s, loc):
    fetch(ins, s, loc, ("stream", "wj", "wo", "we", "ws"))
    n = ins["length"][0]
    g = ins["gains"][4:8]
    s.need("stream")
    forward_first(s, g, n)
    forward_second(s, g)
    out["layer_output"][...] = s.next[...].astype(BF)
    s.dstream[...] = jnp.where(live_rows(n), ins["cotangent"][...].astype(F32), 0.0)
    run(backward_second(s, g))
    done = [loc.copy(s.we, out["we"]), loc.copy(s.ws, out["ws"])]
    run(backward_first(s, g, n))
    done += [loc.copy(s.wj, out["wj"]), loc.copy(s.wo, out["wo"]), loc.copy(s.dstream, out["dstream"])]
    out["gains_grad"][...] = gains_of(s.sums)
    for cp in done:
        cp.wait()


def backward_reduce_body(ins, out, s, loc, link, co):
    x, y, z, c = co
    first, second, third = (0, 1, 2), (1, 2, 0), (2, 0, 1)
    length = ins["length"][0]
    later = [ins["grad_" + k] for k in WEIGHTS]
    here = [getattr(s, k) for k in WEIGHTS]

    def cut(refs, part, q, cc):
        J, O, E, S = refs
        if part == 0:
            return [J.at[q, :, cc], O.at[q, :, cc]]
        return [E.at[cc, :, q]] if part == 1 else [S.at[cc, :, :, q]]

    def own_block(l, part, k):
        if l == 0:
            return cut(here, part, moved(co, first[part], k)[first[part]], c)
        return [r.at[k] for r in ((s.oJ, s.oO), (s.oE,), (s.oS,))[part]]

    def sib_block(part, k):
        return [r.at[k] for r in ((s.sJ, s.sO), (s.sE,), (s.sS,))[part]]

    def buf(name, l, part, side):
        return [getattr(s, name + k).at[l, side] for k in (("J", "O"), ("E",), ("S",))[part]]

    def half(refs, part, h):
        n = 1 if part == 0 else 2
        return [r.at[pl.ds(h * n, n)] for r in refs]

    def add(dsts, srcs, part, halved):
        lead = (1 if halved else 2,) if part == 0 else ((2 if halved else 4), 4)
        for n, d in enumerate(dsts):
            acc(d, [v[n] for v in srcs], lead)

    def send(srcs, dsts, axis, k):
        return [link.send(a, b, axis, k) for a, b in zip(srcs, dsts)]

    def reduce_part(l, p):
        arrive = {}
        for k in (2, 1, 3, 0):
            q = moved(co, first[p], k)[first[p]]
            src = later if l == 1 else here
            mine = [] if l == 0 else [loc.copy(a, b) for a, b in zip(cut(src, p, q, c), own_block(l, p, k))]
            arrive[k] = (mine, send(cut(src, p, q, 1 - c), sib_block(p, k), 3, 1))

        def join(k):
            mine, sibs = arrive[k]
            for cp in mine:
                cp.wait()
            for cp in sibs:
                cp.wait_recv()
            add(own_block(l, p, k), [own_block(l, p, k), sib_block(p, k)], p, False)

        yield
        a = first[p]
        join(2)
        o = own_block(l, p, 2)
        hop1 = (send(half(o, p, 0), buf("r1", l, p, 0), a, 1), send(half(o, p, 1), buf("r1", l, p, 1), a, 3))
        yield
        join(1)
        hop2 = send(half(own_block(l, p, 1), p, 1), half(buf("r2", l, p, 0), p, 1), a, 1)
        join(3)
        hop2 += send(half(own_block(l, p, 3), p, 0), half(buf("r2", l, p, 1), p, 0), a, 3)
        yield
        join(0)
        yield
        for side, k in ((0, 1), (1, 3)):
            for cp in hop1[side]:
                cp.wait_recv()
            o = half(own_block(l, p, k), p, side)
            add(o, [o, buf("r1", l, p, side)], p, True)
            hop2 += send(o, half(buf("r2", l, p, side), p, side), a, k)
        yield
        for cp in hop2:
            cp.wait_recv()
        o, left, right = own_block(l, p, 0), buf("r2", l, p, 0), buf("r2", l, p, 1)
        if p == 0:
            for h in range(2):
                for n, (f, rows) in enumerate(((s.fJ, 144), (s.fO, 48))):
                    f[h * rows:(h + 1) * rows] = o[n][h].astype(F32) + left[n][h].astype(F32) + right[n][h].astype(F32)
            for yy in range(4):
                for zz in range(4):
                    at = (yy // 2) * 144 + ((yy % 2) * 4 + zz) * 18
                    rows = s.fJ[at:at + 18]
                    at = (yy // 2) * 48 + ((yy % 2) * 4 + zz) * 6
                    s.r3[l, yy, zz] = jnp.concatenate([rows, s.fO[at:at + 6]], axis=0).astype(BF)
            block = s.r3.at[l]
        else:
            acc(o[0], [o[0], left[0], right[0]], (4, 4))
            block = o[0]
        ax = second[p]

        def blk(k, h=None):
            q = lax.rem(co[ax] + k, 4)
            part_of = slice(None) if h is None else pl.ds(2 * h, 2)
            return block.at[q, part_of] if p != 1 else block.at[part_of, q]

        hop1 = [link.send(blk(2, 0), s.t1.at[l, p, 0], ax, 1), link.send(blk(2, 1), s.t1.at[l, p, 1], ax, 3)]
        hop2 = [link.send(blk(1, 1), s.t2.at[l, p, 0, pl.ds(2, 2)], ax, 1), link.send(blk(3, 0), s.t2.at[l, p, 1, pl.ds(0, 2)], ax, 3)]
        yield
        for side, k in ((0, 1), (1, 3)):
            hop1[side].wait_recv()
            o = blk(k, side)
            acc(o, [o, s.t1.at[l, p, side]], (2,))
            hop2.append(link.send(o, s.t2.at[l, p, side, pl.ds(2 * side, 2)], ax, k))
        yield
        for cp in hop2:
            cp.wait_recv()
        acc(s.r4.at[l, p], [blk(0), s.t2.at[l, p, 0], s.t2.at[l, p, 1]], (4,))
        ax = third[p]
        me = co[ax]
        last = [link.send(s.r4.at[l, p, lax.rem(me + k, 4)], s.u1.at[l, p, k - 1], ax, k) for k in (1, 3, 2)]
        yield
        for cp in last:
            cp.wait_recv()
        v = s.r4[l, p, me].astype(F32)
        for k in range(3):
            v = v + s.u1[l, p, k].astype(F32)
        out["sum_" + "abc"[p]][l] = v
        yield

    STAGES = 9
    def stages(l, parts, going):
        for _ in range(STAGES - 1):
            for p in parts:
                next(going[l, p])
                yield
        for p in parts:
            run(going[l, p])
            yield

    going = {(l, p): reduce_part(l, p) for l in (1, 0) for p in range(3)}
    sibling = device_at(*moved(co, 3, 1))
    for p in (2, 1, 0):
        next(going[1, p])
    fetch(ins, s, loc, ("dstream", "ws", "raised", "we", "normed2", "mid", "wo", "attended", "proj", "probs", "wj", "normed", "stream"))
    g = ins["gains"][0:4]
    order = (2, 1, 0)
    one = stages(1, order, going)
    steps = [0]
    def advance(n):
        for _ in range(n):
            steps[0] += 1
            next(one, None)
    for _ in backward_second(s, g):
        advance(3)
    advance(max(0, 9 - steps[0]))
    pl.semaphore_signal(s.credit, inc=1, device_id=sibling, device_id_type=MESH)
    pl.semaphore_wait(s.credit, 1)
    next(going[0, 2])
    next(going[0, 1])
    ff = stages(0, (2, 1), going)
    for _ in backward_first(s, g, length):
        if steps[0] < 27:
            advance(3)
        else:
            next(ff, None)
            next(ff, None)
    next(going[0, 0])
    copies = [loc.copy(s.dstream, out["dstream"])]
    gain_sum = RowSum(link, s.gbuf)
    gain_sum.send(jnp.concatenate([gains_of(s.sums), ins["gains_later"][...]], axis=0))
    advance(max(0, 27 - steps[0]))
    joint = stages(0, (0,), going)
    rounds = 0
    while True:
        a, b, d = next(ff, 1), next(ff, 1), next(joint, 1)
        rounds += 1
        if rounds in (2, 4, 6):
            gain_sum.send(gain_sum.total())
        if a and b and d:
            break
    out["gains_sum"][...] = gain_sum.total()
    square = jnp.zeros((24, D), F32)
    for l in range(2):
        for p in range(3):
            v = out["sum_" + "abc"[p]][l]
            square = square + v * v
    part_sum = square[0:8] + square[8:16] + square[16:24]
    piece = part_sum[:, 0:128]
    for n in range(1, 6):
        piece = piece + part_sum[:, n * 128:(n + 1) * 128]
    norm_sum = RowSum(link, s.nbuf)
    for n in range(4):
        norm_sum.send(piece)
        piece = norm_sum.total()
    out["norm"][...] = piece
    for cp in copies:
        cp.wait()
    link.drain()


def call(body, inputs, outs, scratch, copies, remote=0, collective=None, credit=False, limit=60 << 20):
    in_names, out_names, names = list(inputs), list(outs), list(scratch)
    space = {"hbm": pl.ANY, "vmem": pltpu.VMEM, "smem": pltpu.SMEM}
    shapes = [pltpu.VMEM(*scratch[n]) for n in names] + [pltpu.SemaphoreType.DMA((copies,))]
    params = dict(vmem_limit_bytes=limit)
    if remote:
        shapes += [pltpu.SemaphoreType.DMA((remote,)), pltpu.SemaphoreType.DMA((remote,))]
        params.update(collective_id=collective, has_side_effects=True)
    if credit:
        shapes.append(pltpu.SemaphoreType.REGULAR)

    def kernel(*refs):
        ins = dict(zip(in_names, refs))
        out = dict(zip(out_names, refs[len(in_names):]))
        rest = refs[len(in_names) + len(out_names):]
        bufs = Names(**dict(zip(names, rest)))
        loc = Local(rest[len(names)])
        if not remote:
            body(ins, out, bufs, loc)
            return
        if credit:
            bufs.credit = rest[-1]
        co = place()
        greet(co)
        link = Link(co, *rest[len(names) + 1:len(names) + 3])
        body(ins, out, bufs, loc, link, co)

    result = pl.pallas_call(
        kernel,
        out_shape=tuple(jax.ShapeDtypeStruct(*outs[n][1:]) for n in out_names),
        in_specs=[pl.BlockSpec(memory_space=space[inputs[n][0]]) for n in in_names],
        out_specs=tuple(pl.BlockSpec(memory_space=space[outs[n][0]]) for n in out_names),
        scratch_shapes=shapes,
        compiler_params=pltpu.CompilerParams(**params),
    )(*[inputs[n][1] for n in in_names])
    return dict(zip(out_names, result))


def hbm(table, prefix=""):
    return {prefix + k: ("hbm", *v) for k, v in table.items()}


def gather_forward(rows_a, rows_b, rows_c, gains, tokens, length):
    ins = dict(pa=("hbm", rows_a), pb=("hbm", rows_b), pc=("hbm", rows_c), gains=("vmem", gains), stream=("hbm", tokens),
        length=("smem", length))
    outs = {**hbm(WEIGHTS), **hbm(WEIGHTS, "next_"), **hbm(SAVED), "next": ("hbm", (T, D), F32), "gains_all": ("vmem", (8, D), F32)}
    own = dict(stream=((T, D), BF), abuf=((2, 4, 4, 24, D), BF), jf=((288, D), F32), of=((96, D), F32), jst=((2, 2, 144, D), BF),
        ost=((2, 2, 48, D), BF), gbuf=((4, 4, 8, D), F32))
    return call(gather_forward_body, ins, outs, {**WEIGHTS, **SAVED, **ONCE, **own}, 40, remote=144, collective=0)


def layer1(stream, length, cotangent, weights, gains):
    ins = dict(stream=("hbm", stream), length=("smem", length), cotangent=("vmem", cotangent), gains=("vmem", gains),
        **{k: ("hbm", w) for k, w in weights.items()})
    outs = dict(layer_output=("vmem", (T, D), BF), dstream=("hbm", (T, D), F32), gains_grad=("vmem", (4, D), F32), **hbm(WEIGHTS))
    return call(layer1_body, ins, outs, {**WEIGHTS, **SAVED, **ONCE, **BACK, "stream": ((T, D), F32)}, 16)


def backward_reduce(tokens, length, dstream, weights, gains, saved, grads, gains_later):
    ins = dict(stream=("hbm", tokens), length=("smem", length), dstream=("hbm", dstream), gains=("vmem", gains),
        gains_later=("vmem", gains_later), **{k: ("hbm", w) for k, w in weights.items()}, **{k: ("hbm", saved[k]) for k in SAVED},
        **{"grad_" + k: ("hbm", w) for k, w in grads.items()})
    rows = ("vmem", (2, 24, D), F32)
    outs = dict(dstream=("hbm", (T, D), F32), sum_a=rows, sum_b=rows, sum_c=rows, gains_sum=("vmem", (8, D), F32),
        norm=("vmem", (8, 128), F32))
    own = {}
    for k, a, b in (("J", (2, 144), None), ("O", (2, 48), None), ("E", (4, 4, 24), None), ("S", (4, 4, 24), None)):
        halved = (a[0] // 2, *a[1:])
        own["o" + k] = ((4, *a, D), BF)
        own["s" + k] = ((4, *a, D), BF)
        own["r1" + k] = ((2, 2, *halved, D), BF)
        own["r2" + k] = ((2, 2, *a, D), BF)
    own.update(fJ=((288, D), F32), fO=((96, D), F32), r3=((2, 4, 4, 24, D), BF), t1=((2, 3, 2, 2, 24, D), BF),
        t2=((2, 3, 2, 4, 24, D), BF), r4=((2, 3, 4, 24, D), BF), u1=((2, 3, 3, 24, D), BF), gbuf=((4, 4, 8, D), F32),
        nbuf=((4, 4, 8, 128), F32))
    return call(backward_reduce_body, ins, outs, {**WEIGHTS, **SAVED, **BACK, "stream": ((T, D), BF), **own}, 40, remote=176,
        collective=1, credit=True)


def adam_update(master, gradient, moment, square, rate, decay, clip_factor):
    clipped = gradient * clip_factor
    momentum = beta_first * moment + (1.0 - beta_first) * clipped
    variance = beta_second * square + (1.0 - beta_second) * clipped * clipped
    corrected_first = momentum / (1.0 - beta_first**STEP)
    corrected_second = variance / (1.0 - beta_second**STEP)
    updated = master - rate * (
        corrected_first / (jnp.sqrt(corrected_second) + adam_epsilon) + decay * master
    )
    return (updated, momentum, variance)


def local(
    tokens,
    lengths,
    cotangent,
    joint_weight,
    output_weight,
    expand_weight,
    shrink_weight,
    layer_gains,
    joint_moment,
    output_moment,
    expand_moment,
    shrink_moment,
    gains_moment,
    joint_square,
    output_square,
    expand_square,
    shrink_square,
    gains_square,
):
    swap = lambda a: a.transpose(0, 2, 1)
    rows_a = jnp.concatenate([swap(joint_weight), swap(output_weight)], axis=1).astype(BF)
    which_device = lax.axis_index("dp") * 8 + lax.axis_index("fsdp")
    gains_rows = lax.dynamic_update_slice(
        jnp.zeros((8, D), F32), layer_gains.astype(BF).astype(F32).reshape(8, 6), (0, which_device * 6)
    )
    ahead = gather_forward(rows_a, swap(expand_weight).astype(BF), shrink_weight.astype(BF), gains_rows, tokens, lengths)
    gains = ahead["gains_all"]
    top = layer1(ahead["next"], lengths, cotangent, {k: ahead["next_" + k] for k in WEIGHTS}, gains)
    back = backward_reduce(tokens, lengths, top["dstream"], {k: ahead[k] for k in WEIGHTS}, gains, ahead,
        {k: top[k] for k in WEIGHTS}, top["gains_grad"])
    layer_output, dstream = top["layer_output"], back["dstream"]
    gains_sum, sum_a = back["gains_sum"], back["sum_a"]
    gains_own = lax.dynamic_slice(gains_sum, (0, which_device * 6), (8, 6)).reshape(LAYERS, 4, 6)
    stacked = [swap(sum_a[:, :18]), swap(sum_a[:, 18:]), swap(back["sum_b"]), back["sum_c"], gains_own]
    total_square = jnp.sum(back["norm"]) + jnp.sum(gains_sum * gains_sum)
    gradient_norm = jnp.sqrt(total_square)
    clip_factor = jnp.minimum(1.0, clip_limit / (gradient_norm + 1e-06))
    joint_new = adam_update(
        joint_weight, stacked[0], joint_moment, joint_square, rate_matrix, decay_matrix, clip_factor
    )
    output_new = adam_update(
        output_weight,
        stacked[1],
        output_moment,
        output_square,
        rate_matrix,
        decay_matrix,
        clip_factor,
    )
    expand_new = adam_update(
        expand_weight,
        stacked[2],
        expand_moment,
        expand_square,
        rate_matrix,
        decay_matrix,
        clip_factor,
    )
    shrink_new = adam_update(
        shrink_weight,
        stacked[3],
        shrink_moment,
        shrink_square,
        rate_matrix,
        decay_matrix,
        clip_factor,
    )
    gains_new = adam_update(
        layer_gains, stacked[4], gains_moment, gains_square, rate_gains, 0.0, clip_factor
    )
    return (
        layer_output,
        dstream,
        gradient_norm,
        joint_new[0],
        output_new[0],
        expand_new[0],
        shrink_new[0],
        gains_new[0],
        joint_new[1],
        output_new[1],
        expand_new[1],
        shrink_new[1],
        gains_new[1],
        joint_new[2],
        output_new[2],
        expand_new[2],
        shrink_new[2],
        gains_new[2],
    )


def solution(mesh):
    in_specs = (
        P(("dp", "fsdp"), None),
        P(("dp", "fsdp")),
        P(("dp", "fsdp"), None),
        P(None, None, ("dp", "fsdp")),
        P(None, None, ("dp", "fsdp")),
        P(None, None, ("dp", "fsdp")),
        P(None, ("dp", "fsdp"), None),
        P(None, None, ("dp", "fsdp")),
        P(None, None, ("dp", "fsdp")),
        P(None, None, ("dp", "fsdp")),
        P(None, None, ("dp", "fsdp")),
        P(None, ("dp", "fsdp"), None),
        P(None, None, ("dp", "fsdp")),
        P(None, None, ("dp", "fsdp")),
        P(None, None, ("dp", "fsdp")),
        P(None, None, ("dp", "fsdp")),
        P(None, ("dp", "fsdp"), None),
        P(None, None, ("dp", "fsdp")),
    )
    out_specs = (
        P(("dp", "fsdp"), None),
        P(("dp", "fsdp"), None),
        P(),
        P(None, None, ("dp", "fsdp")),
        P(None, None, ("dp", "fsdp")),
        P(None, None, ("dp", "fsdp")),
        P(None, ("dp", "fsdp"), None),
        P(None, None, ("dp", "fsdp")),
        P(None, None, ("dp", "fsdp")),
        P(None, None, ("dp", "fsdp")),
        P(None, None, ("dp", "fsdp")),
        P(None, ("dp", "fsdp"), None),
        P(None, None, ("dp", "fsdp")),
        P(None, None, ("dp", "fsdp")),
        P(None, None, ("dp", "fsdp")),
        P(None, None, ("dp", "fsdp")),
        P(None, ("dp", "fsdp"), None),
        P(None, None, ("dp", "fsdp")),
    )
    return jax.shard_map(local, mesh=mesh, in_specs=in_specs, out_specs=out_specs, check_vma=False)
```

```python
import jax
import jax.numpy as jnp
import numpy as np
from jax import lax
from jax.experimental import pallas as pl
from jax.experimental.pallas import tpu as pltpu
from jax.sharding import PartitionSpec as P

MESH = pl.DeviceIdType.MESH
BF = jnp.bfloat16
F32 = jnp.float32
ANY, VMEM, SMEM = pl.ANY, pltpu.VMEM, pltpu.SMEM

def place():
    dp = lax.axis_index("dp"); fs = lax.axis_index("fsdp")
    return (dp // 4, lax.rem(dp // 2, 2) * 2 + fs // 4, lax.rem(fs, 4), lax.rem(dp, 2))

def device_at(x, y, z, c):
    return ((x * 2 + y // 2) * 2 + c, lax.rem(y, 2) * 4 + z)

def moved(co, axis, k):
    n = 2 if axis == 3 else 4
    co = list(co)
    co[axis] = lax.rem(co[axis] + (k % n), n)
    return tuple(co)

PLANES = ((1, 2), (0, 2), (0, 1))
RINGS = ((1, 2), (2, 0), (0, 1))
CORNERS = [(a, b) for a in range(4) for b in range(4) if (a, b) != (0, 0)]


def greet(co, planes):
    steps = {(0, 0, k, 1) for k in range(4)}
    for k in (1, 2, 3):
        steps |= {(k, 0, 0, 0), (0, k, 0, 0), (0, 0, k, 0)}
    for axes in planes:
        for corner in CORNERS:
            step = [0, 0, 0, 0]
            step[axes[0]], step[axes[1]] = corner
            steps.add(tuple(step))
    bar = pltpu.get_barrier_semaphore()
    for step in sorted(steps):
        pl.semaphore_signal(bar, inc=1, device_id=device_at(*stepped(co, step)), device_id_type=MESH)
    return lambda: pl.semaphore_wait(bar, len(steps))


def stepped(co, step):
    for axis, k in enumerate(step):
        if k:
            co = moved(co, axis, k)
    return co


class Link:
    def __init__(self, co, ss, rs):
        self.co, self.ss, self.rs = co, ss, rs
        self.n = 0
        self.out = []
    def send(self, src, dst, axis, k):
        i = self.n
        self.n += 1
        cp = pltpu.make_async_remote_copy(src_ref=src, dst_ref=dst, send_sem=self.ss.at[i], recv_sem=self.rs.at[i],
            device_id=device_at(*moved(self.co, axis, k)), device_id_type=MESH)
        cp.start()
        self.out.append(cp)
        return cp
    def step(self, src, dst, step):
        i = self.n
        self.n += 1
        cp = pltpu.make_async_remote_copy(src_ref=src, dst_ref=dst, send_sem=self.ss.at[i], recv_sem=self.rs.at[i],
            device_id=device_at(*stepped(self.co, step)), device_id_type=MESH)
        cp.start()
        self.out.append(cp)
        return cp

    def plane(self, axes, src_of, dst_of):
        going = []
        for a, b in CORNERS:
            step = [0, 0, 0, 0]
            step[axes[0]], step[axes[1]] = a, b
            going.append(self.step(src_of(a, b), dst_of(a, b), step))
        return going

    def plane_at_once(self, axes, src_of, landing):
        i = self.n
        self.n += 1
        for n, (a, b) in enumerate(CORNERS):
            step = [0, 0, 0, 0]
            step[axes[0]], step[axes[1]] = a, b
            pltpu.make_async_remote_copy(src_ref=src_of(a, b), dst_ref=landing.at[n], send_sem=self.ss.at[i], recv_sem=self.rs.at[i],
                device_id=device_at(*stepped(self.co, step)), device_id_type=MESH).start()
        whole = pltpu.make_async_remote_copy(src_ref=landing, dst_ref=landing, send_sem=self.ss.at[i], recv_sem=self.rs.at[i],
            device_id=device_at(*moved(self.co, 3, 1)), device_id_type=MESH)
        self.out.append(whole)
        return whole

    def sent(self, copies):
        for cp in copies:
            cp.wait_send()
        self.out = [o for o in self.out if all(o is not cp for cp in copies)]

    def drain(self):
        for cp in self.out:
            cp.wait_send()

class Local:
    def __init__(self, sems):
        self.sems, self.n = sems, 0
    def copy(self, src, dst):
        cp = pltpu.make_async_copy(src, dst, self.sems.at[self.n])
        self.n += 1
        cp.start()
        return cp

class WideSum:
    def __init__(self, link, wide, deep):
        self.link, self.wide, self.deep = link, wide, deep

    def first(self, value):
        x, y, z, c = self.link.co
        mine = self.wide.at[x, y]
        mine[...] = value
        self.going = self.link.plane((0, 1), lambda a, b: mine, lambda a, b: mine)

    def second(self):
        x, y, z, c = self.link.co
        for cp in self.going:
            cp.wait_recv()
        value = None
        for i in range(4):
            for j in range(4):
                v = self.wide[i, j]
                value = v if value is None else value + v
        mine = self.deep.at[z, c]
        mine[...] = value
        self.going = [self.link.step(mine, mine, (0, 0, a, b)) for a in range(4) for b in range(2) if a or b]

    def total(self):
        for cp in self.going:
            cp.wait_recv()
        value = None
        for i in range(4):
            for j in range(2):
                v = self.deep[i, j]
                value = v if value is None else value + v
        return value


def acc(dst, srcs, lead):
    lead = lead[:-1]
    total = 1
    for d in lead:
        total *= d

    def body(t, carry):
        idx = []
        for d in reversed(lead):
            idx.append(lax.rem(t, d))
            t = t // d
        idx = tuple(reversed(idx))
        v = srcs[0][idx].astype(F32)
        for src in srcs[1:]:
            v = v + src[idx].astype(F32)
        dst[idx] = v.astype(dst.dtype)
        return carry

    lax.fori_loop(0, total, body, 0)


D = 768
LAYERS = 2
STEP = 5
beta_first = 0.9
beta_second = 0.999
adam_epsilon = 1e-08
clip_limit = 1.0
HEADS = 12
HEAD_DIM = 64
T = 256
norm_epsilon = 1e-05
SQ = 0.7978845608028654
CUBE = 0.044715
highest = lax.Precision.HIGHEST


def dot_of(a, b, dims, **kw):
    return lax.dot_general(a, b, (dims, ((), ())), preferred_element_type=F32, **kw)


def dot_nt(a, b):
    return dot_of(a, b, ((1,), (1,)))


def dot_nn(a, b):
    return dot_of(a, b, ((1,), (0,)))


def dot_tn(a, b):
    return dot_of(a, b, ((0,), (0,)))


def loop(n, fn):
    def body(t, carry):
        fn(t)
        return carry
    lax.fori_loop(0, n, body, 0)


def tile(t, size):
    return pl.ds(pl.multiple_of(t * size, size), size)


def stats(v):
    centred = v - jnp.mean(v, axis=-1, keepdims=True)
    scale = lax.rsqrt(jnp.mean(centred * centred, axis=-1, keepdims=True) + norm_epsilon)
    return centred * scale, scale


def norm_rows(src, dst, gain, shift):
    def step(t):
        r = tile(t, 64)
        unit, _ = stats(src[r, :].astype(F32))
        dst[r, :] = (unit * gain + shift).astype(BF)
    loop(T // 64, step)


def norm_back(src, grad, base, dst, gain, low_dst):
    def step(t, carry):
        to_gain, to_shift = carry
        r = tile(t, 64)
        unit, scale = stats(src[r, :].astype(F32))
        g = grad[r, :]
        to_gain = to_gain + jnp.sum((g * unit).reshape(8, 8, D), axis=0)
        to_shift = to_shift + jnp.sum(g.reshape(8, 8, D), axis=0)
        g = g * gain
        out = base[r, :] + scale * (
            g - jnp.mean(g, axis=-1, keepdims=True) - unit * jnp.mean(g * unit, axis=-1, keepdims=True)
        )
        dst[r, :] = out
        if low_dst is not None:
            low_dst[r, :] = out.astype(BF)
        return (to_gain, to_shift)
    zero = jnp.zeros((8, D), F32)
    to_gain, to_shift = lax.fori_loop(0, T // 64, step, (zero, zero))
    return jnp.sum(to_gain, axis=0, keepdims=True), jnp.sum(to_shift, axis=0, keepdims=True)


def grids():
    return lax.broadcasted_iota(jnp.int32, (T, T), 0), lax.broadcasted_iota(jnp.int32, (T, T), 1)


def halves(pair):
    lane = lax.broadcasted_iota(jnp.int32, (T, 128), 1)
    zero = jnp.zeros_like(pair)
    return jnp.where(lane < HEAD_DIM, pair, zero), jnp.where(lane < HEAD_DIM, zero, pair)


SCALE = HEAD_DIM ** -0.5
FT = 384


def slots_at(ref, t, f):
    return ref[t, f // 4, lax.rem(f, 4)].reshape(FT, 256)


def put_slots(ref, f, value):
    for t in range(3):
        ref[t, f // 4, lax.rem(f, 4)] = value[:, 256 * t:256 * t + 256].reshape(4, 4, 24, 256).astype(BF)


def first_scores(proj):
    q, _ = halves(proj[:, 0:128])
    return dot_nt(q * jnp.asarray(SCALE, BF), proj[:, D:D + 128])


def attention(proj, probs, attended, bias, length):
    row, col = grids()
    scores = first_scores(proj)
    chosen = jnp.maximum(scores, 0.0) + jnp.log(1.0 + jnp.exp(-jnp.abs(scores)))
    chosen = jnp.where((col > 0) & (col < row) & (row < length), chosen, 0.0)
    forget = dot_of((col < row).astype(F32), chosen, ((1,), (0,)), precision=highest)
    bias[...] = jnp.where((col <= row) & (col < length), forget, 1e30)

    def pair(p):
        at = tile(p, 128)
        q = halves(proj[:, at] * jnp.asarray(SCALE, BF))
        k = proj[:, tile(6 + p, 128)]
        v = halves(proj[:, tile(12 + p, 128)])
        total = None
        for h in range(2):
            logits = dot_nt(q[h], k) - bias[...]
            e = jnp.exp(logits - jnp.max(logits, axis=-1, keepdims=True))
            e = (e * (1.0 / jnp.sum(e, axis=-1, keepdims=True))).astype(BF)
            probs[2 * p + h] = e
            part = dot_nn(e, v[h])
            total = part if h == 0 else total + part
        attended[:, at] = total.astype(BF)
    loop(6, pair)


def forward_first(s, gains, length):
    norm_rows(s.stream, s.normed, gains[0:1], gains[1:2])
    wj = s.wj.reshape(3 * D, D)
    def project(t):
        s.proj[:, tile(t, 256)] = dot_nt(s.normed[...], wj[tile(t, 256), :]).astype(BF)
    loop(9, project)
    yield
    attention(s.proj, s.probs, s.attended, s.bias, length)
    yield
    wo = s.wo.reshape(D, D)
    def output(t):
        at = tile(t, 256)
        s.mid[:, at] = s.stream[:, at].astype(F32) + dot_nt(s.attended[...], wo[at, :])
    loop(3, output)


def third(t):
    return slice(256 * t, 256 * t + 256)


def forward_second(s, gains):
    norm_rows(s.mid, s.normed2, gains[2:3], gains[3:4])
    s.need("we")
    def raise_(f):
        at = tile(f, FT)
        r = dot_nt(s.normed2[:, third(0)], slots_at(s.we, 0, f))
        for t in (1, 2):
            r = r + dot_nt(s.normed2[:, third(t)], slots_at(s.we, t, f))
        s.raised[:, at] = r
        s.hidden[:, at] = (0.5 * r * (1.0 + jnp.tanh(r * (SQ + SQ * CUBE * r * r)))).astype(BF)
    loop(4 * D // FT, raise_)
    yield
    s.need("ws")
    for t in range(3):
        s.next[:, third(t)] = s.mid[:, third(t)] + dot_nn(s.hidden[...], s.ws[t].reshape(4 * D, 256))


def backward_second(s, gains):
    for name in ("dstream", "ws", "raised", "we", "normed2"):
        s.need(name)
    s.low[...] = s.dstream[...].astype(BF)
    s.acc[...] = jnp.zeros((T, D), F32)
    def step(t):
        at = tile(t, FT)
        dh = dot_nt(s.low[:, third(0)], slots_at(s.ws, 0, t))
        for n in (1, 2):
            dh = dh + dot_nt(s.low[:, third(n)], slots_at(s.ws, n, t))
        r = s.raised[:, at]
        th = jnp.tanh(r * (SQ + SQ * CUBE * r * r))
        hid = (0.5 * r * (1.0 + th)).astype(BF)
        slope = 0.5 * (1.0 + th) + 0.5 * r * (1.0 - th * th) * (SQ + 3.0 * SQ * CUBE * r * r)
        dr = (dh * slope).astype(BF)
        put_slots(s.ws, t, dot_tn(hid, s.low[...]))
        for n in range(3):
            s.acc[:, third(n)] += dot_nn(dr, slots_at(s.we, n, t))
        put_slots(s.we, t, dot_tn(dr, s.normed2[...]))
    pieces = 4 * D // FT // 2
    for piece in range(pieces):
        loop(2, lambda t: step(t + 2 * piece))
        if piece < pieces - 1:
            yield
    s.need("mid")
    s.sums += norm_back(s.mid, s.acc, s.dstream, s.dstream, gains[2:3], s.low)
    yield


def attention_back(proj, probs, dout, dproj, bias, keep, length):
    bias[...] = jnp.zeros((T, T), F32)

    def scores_of(p, h, do, v):
        prob = probs[2 * p + h]
        full = prob.astype(F32)
        dsoft = dot_nt(do, v)
        dl = full * (dsoft - jnp.sum(full * dsoft, axis=-1, keepdims=True))
        bias[...] += dl
        return prob, dl

    def pair(p):
        at, at_k, at_v = tile(p, 128), tile(6 + p, 128), tile(12 + p, 128)
        q = halves(proj[:, at] * jnp.asarray(SCALE, BF))
        k = halves(proj[:, at_k] * jnp.asarray(SCALE, BF))
        v = proj[:, at_v]
        do = halves(dout[:, at])
        dq = dk = dv = None
        for h in range(2):
            prob, dl = scores_of(p, h, do[h], v)
            ds = dl.astype(BF)
            parts = (dot_nn(ds, k[h]), dot_tn(ds, q[h]), dot_tn(prob, do[h]))
            dq, dk, dv = parts if h == 0 else (dq + parts[0], dk + parts[1], dv + parts[2])
        dproj[:, at] = dq.astype(BF)
        dproj[:, at_k] = dk.astype(BF)
        dproj[:, at_v] = dv.astype(BF)
    loop(2, lambda t: pair(t + 1))
    yield
    loop(3, lambda t: pair(t + 3))
    yield

    q = halves(proj[:, 0:128] * jnp.asarray(SCALE, BF))
    k = halves(proj[:, D:D + 128] * jnp.asarray(SCALE, BF))
    v = proj[:, 2 * D:2 * D + 128]
    do = halves(dout[:, 0:128])
    prob1, dl1 = scores_of(0, 1, do[1], v)
    prob0, dl0 = scores_of(0, 0, do[0], v)
    keep[...] = dl0
    row, col = grids()
    dchosen = -dot_of((col > row).astype(F32), bias[...], ((1,), (0,)), precision=highest)
    scores = first_scores(proj)
    slope = 1.0 / (1.0 + jnp.exp(-scores))
    extra = jnp.where((col > 0) & (col < row) & (row < length), dchosen * slope, 0.0)
    ds0 = (keep[...] + extra).astype(BF)
    ds1 = dl1.astype(BF)
    dproj[:, 0:128] = (dot_nn(ds0, k[0]) + dot_nn(ds1, k[1])).astype(BF)
    dproj[:, D:D + 128] = (dot_tn(ds0, q[0]) + dot_tn(ds1, q[1])).astype(BF)
    dproj[:, 2 * D:2 * D + 128] = (dot_tn(prob0, do[0]) + dot_tn(prob1, do[1])).astype(BF)


def backward_first(s, gains, length):
    for name in ("wo", "attended", "proj", "probs"):
        s.need(name)
    wo, wj = s.wo.reshape(D, D), s.wj.reshape(3 * D, D)
    def back(t):
        at = tile(t, 256)
        s.dout[:, at] = dot_nn(s.low[...], wo[:, at]).astype(BF)
    loop(3, back)
    def grad(t):
        at = tile(t, 256)
        wo[at, :] = dot_tn(s.low[:, at], s.attended[...]).astype(BF)
    loop(3, grad)
    yield
    yield from attention_back(s.proj, s.probs, s.dout, s.dproj, s.bias, s.keep, length)
    yield
    s.need("wj")
    s.need("normed")
    s.acc[...] = jnp.zeros((T, D), F32)
    def joint(t):
        at = tile(t, 384)
        d = s.dproj[:, at]
        s.acc[...] += dot_nn(d, wj[at, :])
        wj[at, :] = dot_tn(d, s.normed[...]).astype(BF)
    for piece in range(2):
        loop(3, lambda t: joint(t + 3 * piece))
        yield
    s.need("stream")
    s.sums += norm_back(s.stream, s.acc, s.dstream, s.dstream, gains[0:1], None)


class Names:
    def __init__(self, **kw):
        self.__dict__.update(kw)
        self.coming = {}
        self.sums = ()

    def need(self, name):
        for cp in self.coming.pop(name, ()):
            cp.wait()


WEIGHTS = dict(wj=((4, 2, 2, 144, D), BF), wo=((4, 2, 2, 48, D), BF), we=((3, 2, 4, 4, 4, 24, 256), BF), ws=((3, 2, 4, 4, 4, 24, 256), BF))
SAVED = dict(mid=((T, D), F32), normed=((T, D), BF), normed2=((T, D), BF), proj=((T, 3 * D), BF), probs=((HEADS, T, T), BF),
    attended=((T, D), BF), raised=((T, 4 * D), F32))
ONCE = dict(bias=((T, T), F32), hidden=((T, 4 * D), BF), next=((T, D), F32))
BACK = dict(bias=((T, T), F32), keep=((T, T), F32), dstream=((T, D), F32), low=((T, D), BF), acc=((T, D), F32), dout=((T, D), BF),
    dproj=((T, 3 * D), BF))


def fetch(ins, s, loc, names):
    for n in names:
        s.coming[n] = [loc.copy(getattr(ins, n), getattr(s, n))]


def run(pieces):
    for _ in pieces:
        pass


def gains_of(sums):
    gain2, shift2, gain1, shift1 = sums
    return jnp.concatenate([gain1, shift1, gain2, shift2], axis=0)


def live_rows(length):
    return lax.broadcasted_iota(jnp.int32, (T, D), 0) < length


def own_columns(which):
    lane = lax.broadcasted_iota(jnp.int32, (1, D), 1)
    return [(lane == which * 6 + j).astype(F32) for j in range(6)]


OWN = ((3, 4, 4, 4, 24, 256), BF)
SIBLING = dict(sib_wj=((4, 2, 144, D), BF), sib_wo=((4, 2, 48, D), BF), sib_we=OWN, sib_ws=OWN)


def side_of(ref, name, core, at=slice(None)):
    return ref.at[at, :, core] if name in ("wj", "wo") else ref.at[:, core]


class Pair:
    def __init__(self, s, link, c):
        self.s, self.link, self.c = s, link, c
        self.going, self.copies = {}, {}

    def send(self, name, at=slice(None)):
        src, dst = side_of(getattr(self.s, name), name, 1 - self.c, at), getattr(self.s, "sib_" + name)
        cp = self.link.send(src, dst.at[at] if name == "wj" else dst, 3, 1)
        self.going.setdefault(name, []).append(cp)
        self.copies.setdefault(name, []).append(cp)

    def arrived(self, name):
        for cp in self.going.pop(name):
            cp.wait_recv()

    def join(self, name):
        self.arrived(name)
        mine, other = side_of(getattr(self.s, name), name, self.c), getattr(self.s, "sib_" + name)
        acc(mine, [mine, other], (3, 4, 4))

    def join_rows(self, perm):
        self.arrived("wj")
        self.arrived("wo")
        s = self.s
        def step(n):
            x, h = n // 2, lax.rem(n, 2)
            j = s.wj[x, h, self.c].astype(F32) + s.sib_wj[x, h].astype(F32)
            o = s.wo[x, h, self.c].astype(F32) + s.sib_wo[x, h].astype(F32)
            rows = jnp.concatenate([j.astype(BF), o.astype(BF)], axis=0)
            slots = dot_tn(perm, rows)
            for t in range(3):
                s.ga[t, x, pl.ds(2 * h, 2)] = slots[:, 256 * t:256 * t + 256].reshape(2, 4, 24, 256).astype(BF)
        loop(8, step)


def compact(slots, wj, wo, perm):
    def step(n):
        x, h, c = n // 4, lax.rem(n // 2, 2), lax.rem(n, 2)
        for t in range(3):
            rows = dot_nn(perm, slots[t, c, x, pl.ds(2 * h, 2)].reshape(192, 256)).astype(BF)
            wj[x, h, c, :, third(t)] = rows[:144]
            wo[x, h, c, :, third(t)] = rows[144:]
    loop(16, step)


class Gather:
    def __init__(self, link, loc, piece, dst):
        self.link, self.loc, self.piece, self.dst = link, loc, piece, dst
        self.co = link.co

    def slots(self, t, sel):
        return self.dst.at[(t, self.co[3], *sel)]

    def small(self):
        self.own, self.one = [], []
        for t in range(3):
            src, dst = self.piece.at[:, third(t)], self.slots(t, self.co[:3])
            self.own.append(self.loc.copy(src, dst))
            self.one.append([self.link.send(src, dst, RINGS[t][0], k) for k in (1, 3, 2)])

    def slab(self):
        self.two = []
        for t in range(3):
            self.own[t].wait()
            for cp in self.one[t]:
                cp.wait_recv()
            u, v = RINGS[t]
            sel = list(self.co[:3])
            sel[u] = slice(None)
            ref = self.slots(t, sel)
            self.two.append([self.link.send(ref, ref, v, k) for k in (1, 3)])

    def slab_on(self):
        self.three = []
        for t in range(3):
            u, v = RINGS[t]
            for side, back, on in ((0, 3, 1), (1, 1, 3)):
                self.two[t][side].wait_recv()
                sel = list(moved(self.co, v, back)[:3])
                sel[u] = pl.ds(2 * side, 2)
                ref = self.slots(t, sel)
                self.three.append(self.link.send(ref, ref, v, on))

    def block(self):
        for cp in self.three:
            cp.wait_recv()
        self.four = []
        for t in range(3):
            sel = [slice(None)] * 3
            sel[t] = self.co[t]
            ref = self.slots(t, sel)
            self.four.append([self.link.send(ref, ref, t, k) for k in (1, 3)])

    def block_on(self):
        self.five = []
        for t in range(3):
            u, v = RINGS[t]
            for side, back, on in ((0, 3, 1), (1, 1, 3)):
                self.four[t][side].wait_recv()
                sel = [slice(None)] * 3
                sel[t] = moved(self.co, t, back)[t]
                sel[u] = pl.ds(2 * side, 2)
                ref = self.slots(t, sel)
                self.five.append(self.link.send(ref, ref, t, on))

    def across(self):
        for cp in self.five:
            cp.wait_recv()
        c = self.co[3]
        self.six = [self.link.send(self.dst.at[t, c], self.dst.at[t, c], 3, 1) for t in range(3)]

    def sent(self):
        groups = (*self.one, *self.two, self.three, *self.four, self.five, self.six)
        self.link.sent([cp for g in groups for cp in g])

    def ready(self):
        for cp in self.six:
            cp.wait_recv()


def first_body(ins, out, s, loc, link, co):
    x, y, z, c = co
    length = ins.length[0]
    fetch(ins, s, loc, ("stream",))
    targets = [[s.slots.at[0], s.we, s.ws], [s.slots.at[1], out.top_we, out.top_ws]]
    items = []
    for l in range(2):
        rows = jnp.concatenate([ins.joint[:, l, :], ins.output[:, l, :]], axis=0)
        for w, value in enumerate((rows, ins.expand[l], ins.shrink[l])):
            s.piece[l, w] = value.astype(BF)
            items.append(Gather(link, loc, s.piece.at[l, w], targets[l][w]))
    s.met()
    for item in items:
        item.small()
    which = ((x * 2 + y // 2) * 2 + c) * 8 + lax.rem(y, 2) * 4 + z
    masks = own_columns(which)
    placed = []
    for l in range(2):
        rows = ins.layer_gains[l].astype(BF).astype(F32)
        total = rows[:, 0:1] * masks[0]
        for j in range(1, 6):
            total = total + rows[:, j:j + 1] * masks[j]
        placed.append(total)
    gain_sum = WideSum(link, s.gwide, s.gdeep)
    gain_sum.first(jnp.concatenate(placed, axis=0))

    done = []
    perm = ins.perm

    def step(k):
        if k + 2 < 6:
            items[k + 2].block()
        if 0 < k < 7:
            items[k - 1].across()
        if k < 6:
            items[k].block_on()

    def save(*names, prefix=""):
        for n in names:
            done.append(loc.copy(getattr(s, n), getattr(out, prefix + n)))

    for name in ("slab", "slab_on"):
        for item in items:
            getattr(item, name)()
        if name == "slab":
            gain_sum.second()
    items[0].block()
    items[1].block()
    out.gains_all[...] = gain_sum.total()
    gains = out.gains_all[0:4]
    step(0)
    step(1)
    items[0].ready()
    compact(s.slots.at[0], s.wj, s.wo, perm[...])
    step(2)
    save("wj", "wo")
    s.need("stream")
    first = forward_first(s, gains, length)
    next(first)
    next(first)
    step(3)
    run(first)
    items[1].ready()
    second = forward_second(s, gains)
    next(second)
    step(4)
    items[2].ready()
    save("normed", "proj", "probs", "attended", "mid", "normed2", "raised")
    run(second)
    s.second[...] = s.next[...]
    for cp in done:
        cp.wait()
    done.clear()
    save("we", "ws")
    done.append(loc.copy(s.second, out.top_stream))
    top = Names(**{k: v for k, v in s.__dict__.items() if k not in ("coming", "sums", "stream", "met")}, stream=s.second)
    gains = out.gains_all[4:8]
    items[3].ready()
    compact(s.slots.at[1], s.wj, s.wo, perm[...])
    save("wj", "wo", prefix="top_")
    step(5)
    first = forward_first(top, gains, length)
    next(first)
    step(6)
    items[4].ready()
    items[1].sent()
    for cp in done:
        cp.wait()
    done.clear()
    top.coming["we"] = [loc.copy(out.top_we, s.we)]
    next(first)
    run(first)
    save("normed", "proj", "probs", "attended", "mid", prefix="top_")
    second = forward_second(top, gains)
    next(second)
    save("normed2", "raised", prefix="top_")
    items[5].ready()
    items[2].sent()
    top.coming["ws"] = [loc.copy(out.top_ws, s.ws)]
    run(second)
    out.layer_output[...] = s.next[...].astype(BF)
    for cp in done:
        cp.wait()
    link.drain()


class Reduce:
    def __init__(self, link, s, l, w, source):
        self.link, self.s, self.l, self.w, self.source, self.co = link, s, l, w, source, link.co

    def at(self, t, k):
        sel = [slice(None)] * 3
        sel[t] = moved(self.co, t, k)[t]
        return self.source.at[(t, *sel)]

    def half(self, ref, h):
        return ref.at[pl.ds(2 * h, 2)]

    def r1(self, t, side):
        return self.s.r1.at[self.l, self.w, t, side]

    def r2(self, t, side):
        return self.s.r2.at[self.l, t, side, :, :, self.w]

    def far(self):
        self.hop1 = [[self.link.send(self.half(self.at(t, 2), side), self.r1(t, side), t, k) for side, k in ((0, 1), (1, 3))]
            for t in range(3)]

    def near(self):
        self.hop2 = [[self.link.send(self.half(self.at(t, k), 1 - side), self.half(self.r2(t, side), 1 - side), t, k)
            for side, k in ((0, 1), (1, 3))] for t in range(3)]

    def onward(self):
        for t in range(3):
            for side, k in ((0, 1), (1, 3)):
                self.hop1[t][side].wait_recv()
                o = self.half(self.at(t, k), side)
                acc(o, [o, self.r1(t, side)], (2, 4))
                self.hop2[t].append(self.link.send(o, self.half(self.r2(t, side), side), t, k))

    def collect(self):
        for t in range(3):
            for cp in self.hop2[t]:
                cp.wait_recv()
            acc(self.r2(t, 0), [self.at(t, 0), self.r2(t, 0), self.r2(t, 1)], (4, 4))

    def sent(self):
        self.link.sent([cp for t in range(3) for cp in (*self.hop1[t], *self.hop2[t])])


class Settle:
    def __init__(self, link, s, l, first, count):
        self.link, self.s, self.l, self.first, self.count = link, s, l, first, count
        self.which = pl.ds(first, count)

    def send(self):
        co, self.going = self.link.co, []
        for t in range(3):
            u, v = PLANES[t]
            block = self.s.r2.at[self.l, t, 0]
            pick = lambda a, b: block.at[lax.rem(co[u] + a, 4), lax.rem(co[v] + b, 4), self.which]
            self.going.append(self.link.plane_at_once(PLANES[t], pick, self.s.u1.at[self.l, t, :, self.which]))

    def final(self, square):
        co = self.link.co
        for t in range(3):
            u, v = PLANES[t]
            self.going[t].wait_recv()
            for w in range(self.first, self.first + self.count):
                g = self.s.r2[self.l, t, 0, co[u], co[v], w].astype(F32)
                for k in range(15):
                    g = g + self.s.u1[self.l, t, k, w].astype(F32)
                self.s.grads[self.l, w, :, third(t)] = g
                g = g * g
                g = g[0:8] + g[8:16] + g[16:24]
                g = g[:, 0:128] + g[:, 128:256]
                square = g if square is None else square + g
        return square


def second_body(ins, out, s, loc, link, co):
    x, y, z, c = co
    length = ins.length[0]
    shared = {k: v for k, v in s.__dict__.items() if k not in ("coming", "sums", "met")}
    base = Names(**shared)
    top = Names(**{**shared, **{k: getattr(s, "top_" + k) for k in ("we", "ws", "stream")}})
    layers = (base, top)
    pairs = [Pair(n, link, c) for n in layers]
    sums = [[Reduce(link, s, l, w, (n.ga, n.we.at[:, c], n.ws.at[:, c])[w]) for w in range(3)] for l, n in enumerate(layers)]
    low, up = sums
    top_end, ff_end, row_end = Settle(link, s, 1, 0, 3), Settle(link, s, 0, 1, 2), Settle(link, s, 0, 0, 1)
    perm = ins.perm

    def bring(n, prefix, *names):
        for name in names:
            n.coming[name] = [loc.copy(getattr(ins, prefix + name), getattr(n, name))]

    bring(top, "top_", "ws", "raised", "we", "normed2", "mid", "wo", "attended", "proj", "probs", "wj", "normed", "stream")
    bring(base, "", "we", "ws", "stream")
    s.dstream[...] = jnp.where(live_rows(length), ins.cotangent[...].astype(F32), 0.0)
    g = ins.gains[4:8]
    run(backward_second(top, g))
    s.met()
    pairs[1].send("ws")
    bring(base, "", "raised", "normed2", "mid")
    for k, _ in enumerate(backward_first(top, g, length)):
        if k == 0:
            pairs[1].send("we")
            pairs[1].send("wo")
        if k == 1:
            pairs[1].join("ws")
            up[2].far()
            up[2].near()
        if k == 2:
            pairs[1].join("we")
            up[1].far()
            up[1].near()
        if k == 3:
            bring(base, "", "attended", "proj", "probs")
        if k == 4:
            pairs[1].send("wj", pl.ds(0, 2))
            up[2].onward()
        if k == 5:
            pairs[1].send("wj", pl.ds(2, 2))
    up[1].onward()
    bring(base, "", "normed")
    square = None
    base.coming["dstream"] = []
    g = ins.gains[0:4]
    for k, _ in enumerate(backward_second(base, g)):
        if k == 0:
            pairs[1].join_rows(perm[...])
            up[0].far()
            up[0].near()
            link.sent(pairs[1].copies["wj"] + pairs[1].copies["wo"])
            bring(base, "", "wj", "wo")
            pl.semaphore_signal(s.credit, inc=1, device_id=device_at(*moved(co, 3, 1)), device_id_type=MESH)
            up[2].collect()
        if k == 1:
            up[1].collect()
        if k == 2:
            up[0].onward()
    pl.semaphore_wait(s.credit, 1)
    pairs[0].send("ws")
    for k, _ in enumerate(backward_first(base, g, length)):
        if k == 0:
            pairs[0].send("we")
            pairs[0].send("wo")
            up[0].collect()
            top_end.send()
        if k == 1:
            pairs[0].join("ws")
            low[2].far()
            low[2].near()
        if k == 2:
            pairs[0].join("we")
            low[1].far()
            low[1].near()
        if k == 3:
            square = top_end.final(square)
            up[0].sent()
        if k == 4:
            pairs[0].send("wj", pl.ds(0, 2))
            low[2].onward()
        if k == 5:
            pairs[0].send("wj", pl.ds(2, 2))
            low[1].onward()
    gain_sum = WideSum(link, s.gwide, s.gdeep)
    gain_sum.first(jnp.concatenate([gains_of(base.sums), gains_of(top.sums)], axis=0))
    copies = [loc.copy(s.dstream, out.dstream)]
    low[2].collect()
    pairs[0].join_rows(perm[...])
    low[0].far()
    low[0].near()
    low[1].collect()
    ff_end.send()
    low[0].onward()
    gain_sum.second()
    square = ff_end.final(square)
    low[0].collect()
    row_end.send()
    gains_sum = gain_sum.total()
    out.gains_sum[...] = gains_sum
    square = row_end.final(square)
    copies.append(loc.copy(s.grads, out.grads))
    norm_sum = WideSum(link, s.nwide, s.ndeep)
    norm_sum.first(square)
    norm_sum.second()
    whole = norm_sum.total()
    norm = jnp.sqrt(jnp.sum(jnp.sum(whole, axis=0, keepdims=True), axis=1, keepdims=True)
        + jnp.sum(jnp.sum(gains_sum * gains_sum, axis=0, keepdims=True), axis=1, keepdims=True))
    out.norm[...] = jnp.broadcast_to(norm, (8, 128))
    for cp in copies:
        cp.wait()
    link.drain()


RATES = dict(matrix=(0.05, 0.1), gains=(0.25, 0.0))


def adam(master, gradient, moment, square, kind, clip):
    rate, decay = RATES[kind]
    clipped = gradient * clip
    momentum = beta_first * moment + (1.0 - beta_first) * clipped
    variance = beta_second * square + (1.0 - beta_second) * clipped * clipped
    corrected_first = momentum / (1.0 - beta_first**STEP)
    corrected_second = variance / (1.0 - beta_second**STEP)
    updated = master - rate * (corrected_first / (jnp.sqrt(corrected_second) + adam_epsilon) + decay * master)
    return updated, momentum, variance


def update_body(ins, out, s, loc, link, co):
    x, y, z, c = co
    out.input_gradient[...] = ins.dstream[...]
    out.layer_output[...] = ins.low_output[...]
    which = ((x * 2 + y // 2) * 2 + c) * 8 + lax.rem(y, 2) * 4 + z
    columns = [jnp.sum(ins.gains_sum[...] * m, axis=-1, keepdims=True) for m in own_columns(which)]
    lane = lax.broadcasted_iota(jnp.int32, (8, 6), 1)
    own_gains = jnp.zeros((8, 6), F32)
    for j in range(6):
        own_gains = own_gains + jnp.where(lane == j, columns[j], 0.0)
    norm = ins.norm[0:1, 0:1]
    out.gradient_norm[...] = norm
    clip = jnp.minimum(1.0, clip_limit / (norm + 1e-06))
    for l in range(2):
        for name, w, rows in (("joint", 0, slice(0, 18)), ("output", 0, slice(18, 24)), ("expand", 1, slice(0, 24)), ("shrink", 2, slice(0, 24))):
            at = (slice(None), l, slice(None)) if w == 0 else (l, slice(None), slice(None))
            new = adam(getattr(ins, name)[at], ins.grads[l, w, rows, :], getattr(ins, name + "_moment")[at], getattr(ins, name + "_square")[at], "matrix", clip)
            for kind, v in zip(("master", "momentum", "variance"), new):
                getattr(out, name + "_" + kind)[at] = v
        new = adam(ins.layer_gains[l], own_gains[4 * l:4 * l + 4], ins.gains_moment[l], ins.gains_square[l], "gains", clip)
        for kind, v in zip(("master", "momentum", "variance"), new):
            getattr(out, "gains_" + kind)[l] = v


def call(body, inputs, outs, scratch, copies, remote=0, collective=None, planes=(), credit=False, limit=63 << 20):
    in_names, out_names, names = list(inputs), list(outs), list(scratch)
    shapes = [pltpu.VMEM(*scratch[n]) for n in names] + [pltpu.SemaphoreType.DMA((copies,))]
    params = dict(vmem_limit_bytes=limit)
    if remote:
        shapes += [pltpu.SemaphoreType.DMA((remote,)), pltpu.SemaphoreType.DMA((remote,))]
        params.update(collective_id=collective, has_side_effects=True)
    if credit:
        shapes.append(pltpu.SemaphoreType.REGULAR)

    def kernel(*refs):
        ins = Names(**dict(zip(in_names, refs)))
        out = Names(**dict(zip(out_names, refs[len(in_names):])))
        rest = refs[len(in_names) + len(out_names):]
        bufs = Names(**dict(zip(names, rest)))
        loc = Local(rest[len(names)])
        co = place()
        if not remote:
            body(ins, out, bufs, loc, None, co)
            return
        if credit:
            bufs.credit = rest[-1]
        bufs.met = greet(co, planes)
        link = Link(co, *rest[len(names) + 1:len(names) + 3])
        body(ins, out, bufs, loc, link, co)

    result = pl.pallas_call(
        kernel,
        out_shape=tuple(jax.ShapeDtypeStruct(*outs[n][1:]) for n in out_names),
        in_specs=[pl.BlockSpec(memory_space=inputs[n][0]) for n in in_names],
        out_specs=tuple(pl.BlockSpec(memory_space=outs[n][0]) for n in out_names),
        scratch_shapes=shapes,
        compiler_params=pltpu.CompilerParams(**params),
    )(*[inputs[n][1] for n in in_names])
    return Names(**dict(zip(out_names, result)))


def hbm(table, prefix=""):
    return {prefix + k: (ANY, *v) for k, v in table.items()}


ROWS = dict(joint=((18, 2, D), F32), output=((6, 2, D), F32), expand=((2, 24, D), F32), shrink=((2, 24, D), F32))
SUMS = dict(gwide=((4, 4, 8, D), F32), gdeep=((4, 2, 8, D), F32))


def slot_order():
    order = np.zeros((192, 192), np.float32)
    for f in range(8):
        for r in range(18):
            order[18 * f + r, 24 * f + r] = 1
        for r in range(6):
            order[144 + 6 * f + r, 24 * f + 18 + r] = 1
    return jnp.asarray(order, BF)


def first_kernel(shards, layer_gains, tokens, length, perm):
    ins = dict(layer_gains=(VMEM, layer_gains), stream=(ANY, tokens), length=(SMEM, length), perm=(VMEM, perm),
        **{k: (VMEM, v) for k, v in shards.items()})
    row = ((T, D), F32)
    outs = {**hbm(WEIGHTS), **hbm(SAVED), **hbm(WEIGHTS, "top_"), **hbm(SAVED, "top_"), "top_stream": (ANY, *row),
        "gains_all": (VMEM, (8, D), F32), "layer_output": (VMEM, (T, D), BF)}
    own = dict(stream=((T, D), BF), second=row, piece=((2, 3, 24, D), BF), slots=((2, 3, 2, 4, 4, 4, 24, 256), BF))
    return call(first_body, ins, outs, {**WEIGHTS, **SAVED, **ONCE, **own, **SUMS}, 64, 272, 0, ((0, 1),))


def second_kernel(tokens, length, cotangent, ahead, perm):
    names = (*WEIGHTS, *SAVED)
    ins = dict(stream=(ANY, tokens), length=(SMEM, length), perm=(VMEM, perm), cotangent=(VMEM, cotangent),
        gains=(VMEM, ahead.gains_all), top_stream=(ANY, ahead.top_stream), **{k: (ANY, getattr(ahead, k)) for k in names},
        **{"top_" + k: (ANY, getattr(ahead, "top_" + k)) for k in names})
    outs = dict(dstream=(ANY, (T, D), F32), norm=(VMEM, (8, 128), F32), grads=(ANY, (2, 3, 24, D), F32),
        gains_sum=(VMEM, (8, D), F32))
    own = dict(stream=((T, D), BF), top_stream=((T, D), F32), ga=OWN, r1=((2, 3, 3, 2, 2, 4, 24, 256), BF),
        r2=((2, 3, 2, 4, 4, 3, 24, 256), BF), u1=((2, 3, 15, 3, 24, 256), BF), grads=((2, 3, 24, D), F32),
        nwide=((4, 4, 8, 128), F32), ndeep=((4, 2, 8, 128), F32))
    weights = {"top_" + k: WEIGHTS[k] for k in ("we", "ws")}
    return call(second_body, ins, outs, {**WEIGHTS, **weights, **SAVED, **BACK, **own, **SUMS, **SIBLING}, 64, 200, 1, PLANES,
        credit=True)


def update(state, ahead, back):
    ins = dict(dstream=(VMEM, back.dstream), low_output=(VMEM, ahead.layer_output), norm=(VMEM, back.norm),
        grads=(VMEM, back.grads), gains_sum=(VMEM, back.gains_sum), **{k: (VMEM, v) for k, v in state.items()})
    outs = dict(input_gradient=(VMEM, (T, D), F32), layer_output=(VMEM, (T, D), BF), gradient_norm=(VMEM, (1, 1), F32))
    for kind in ("master", "momentum", "variance"):
        for name, v in {**ROWS, "gains": ((2, 4, 6), F32)}.items():
            outs[name + "_" + kind] = (VMEM, *v)
    return call(update_body, ins, outs, {}, 1)


def local(
    tokens,
    lengths,
    cotangent,
    joint_weight,
    output_weight,
    expand_weight,
    shrink_weight,
    layer_gains,
    joint_moment,
    output_moment,
    expand_moment,
    shrink_moment,
    gains_moment,
    joint_square,
    output_square,
    expand_square,
    shrink_square,
    gains_square,
):
    front = lambda a: a.transpose(2, 0, 1)
    swap = lambda a: a.transpose(0, 2, 1)
    shards = dict(joint=front(joint_weight), output=front(output_weight), expand=swap(expand_weight), shrink=shrink_weight)
    perm = slot_order()
    ahead = first_kernel(shards, layer_gains, tokens, lengths, perm)
    back = second_kernel(tokens, lengths, cotangent, ahead, perm)
    state = dict(
        shards,
        joint_moment=front(joint_moment),
        output_moment=front(output_moment),
        expand_moment=swap(expand_moment),
        shrink_moment=shrink_moment,
        joint_square=front(joint_square),
        output_square=front(output_square),
        expand_square=swap(expand_square),
        shrink_square=shrink_square,
        layer_gains=layer_gains,
        gains_moment=gains_moment,
        gains_square=gains_square,
    )
    new = update(state, ahead, back)
    results = [new.layer_output, new.input_gradient, new.gradient_norm.reshape(())]
    for kind in ("master", "momentum", "variance"):
        results += [
            getattr(new, "joint_" + kind).transpose(1, 2, 0),
            getattr(new, "output_" + kind).transpose(1, 2, 0),
            swap(getattr(new, "expand_" + kind)),
            getattr(new, "shrink_" + kind),
            getattr(new, "gains_" + kind),
        ]
    return tuple(results)


AXES = ("dp", "fsdp")


def solution(mesh):
    in_specs = (
        P(AXES, None),
        P(AXES),
        P(AXES, None),
        P(None, None, AXES),
        P(None, None, AXES),
        P(None, None, AXES),
        P(None, AXES, None),
        P(None, None, AXES),
        P(None, None, AXES),
        P(None, None, AXES),
        P(None, None, AXES),
        P(None, AXES, None),
        P(None, None, AXES),
        P(None, None, AXES),
        P(None, None, AXES),
        P(None, None, AXES),
        P(None, AXES, None),
        P(None, None, AXES),
    )
    out_specs = (
        P(AXES, None),
        P(AXES, None),
        P(),
        P(None, None, AXES),
        P(None, None, AXES),
        P(None, None, AXES),
        P(None, AXES, None),
        P(None, None, AXES),
        P(None, None, AXES),
        P(None, None, AXES),
        P(None, None, AXES),
        P(None, AXES, None),
        P(None, None, AXES),
        P(None, None, AXES),
        P(None, None, AXES),
        P(None, None, AXES),
        P(None, AXES, None),
        P(None, None, AXES),
    )
    return jax.shard_map(local, mesh=mesh, in_specs=in_specs, out_specs=out_specs, check_vma=False)
```

```python
import jax
import jax.numpy as jnp
import numpy as np
from jax import lax
from jax.experimental import pallas as pl
from jax.experimental.pallas import tpu as pltpu
from jax.sharding import PartitionSpec as P

MESH = pl.DeviceIdType.MESH
BF = jnp.bfloat16
F32 = jnp.float32
ANY, VMEM, SMEM = pl.ANY, pltpu.VMEM, pltpu.SMEM

def place():
    dp = lax.axis_index("dp"); fs = lax.axis_index("fsdp")
    return (dp // 4, lax.rem(dp // 2, 2) * 2 + fs // 4, lax.rem(fs, 4), lax.rem(dp, 2))

def device_at(x, y, z, c):
    return ((x * 2 + y // 2) * 2 + c, lax.rem(y, 2) * 4 + z)

def moved(co, axis, k):
    n = 2 if axis == 3 else 4
    co = list(co)
    co[axis] = lax.rem(co[axis] + (k % n), n)
    return tuple(co)

PLANES = ((1, 2), (0, 2), (0, 1))
RINGS = ((1, 2), (2, 0), (0, 1))
CORNERS = [(a, b) for a in range(4) for b in range(4) if (a, b) != (0, 0)]


def greet(co, planes):
    steps = {(0, 0, k, 1) for k in range(4)}
    for k in (1, 2, 3):
        steps |= {(k, 0, 0, 0), (0, k, 0, 0), (0, 0, k, 0)}
    for axes in planes:
        for corner in CORNERS:
            step = [0, 0, 0, 0]
            step[axes[0]], step[axes[1]] = corner
            steps.add(tuple(step))
    bar = pltpu.get_barrier_semaphore()
    for step in sorted(steps):
        pl.semaphore_signal(bar, inc=1, device_id=device_at(*stepped(co, step)), device_id_type=MESH)
    return lambda: pl.semaphore_wait(bar, len(steps))


def stepped(co, step):
    for axis, k in enumerate(step):
        if k:
            co = moved(co, axis, k)
    return co


class Link:
    def __init__(self, co, ss, rs):
        self.co, self.ss, self.rs = co, ss, rs
        self.n = 0
        self.out = []
    def send(self, src, dst, axis, k):
        i = self.n
        self.n += 1
        cp = pltpu.make_async_remote_copy(src_ref=src, dst_ref=dst, send_sem=self.ss.at[i], recv_sem=self.rs.at[i],
            device_id=device_at(*moved(self.co, axis, k)), device_id_type=MESH)
        cp.start()
        self.out.append(cp)
        return cp
    def step(self, src, dst, step):
        i = self.n
        self.n += 1
        cp = pltpu.make_async_remote_copy(src_ref=src, dst_ref=dst, send_sem=self.ss.at[i], recv_sem=self.rs.at[i],
            device_id=device_at(*stepped(self.co, step)), device_id_type=MESH)
        cp.start()
        self.out.append(cp)
        return cp

    def plane(self, axes, src_of, dst_of):
        going = []
        for a, b in CORNERS:
            step = [0, 0, 0, 0]
            step[axes[0]], step[axes[1]] = a, b
            going.append(self.step(src_of(a, b), dst_of(a, b), step))
        return going

    def sent(self, copies):
        for cp in copies:
            cp.wait_send()
        self.out = [o for o in self.out if all(o is not cp for cp in copies)]

    def drain(self):
        for cp in self.out:
            cp.wait_send()
        self.out = []

class Local:
    def __init__(self, sems):
        self.sems, self.n = sems, 0
    def copy(self, src, dst):
        cp = pltpu.make_async_copy(src, dst, self.sems.at[self.n])
        self.n += 1
        cp.start()
        return cp

class WideSum:
    def __init__(self, link, wide, deep):
        self.link, self.wide, self.deep = link, wide, deep

    def first(self, value):
        x, y, z, c = self.link.co
        mine = self.wide.at[x, y]
        mine[...] = value
        self.going = self.link.plane((0, 1), lambda a, b: mine, lambda a, b: mine)

    def second(self):
        x, y, z, c = self.link.co
        for cp in self.going:
            cp.wait_recv()
        value = None
        for i in range(4):
            for j in range(4):
                v = self.wide[i, j]
                value = v if value is None else value + v
        mine = self.deep.at[z, c]
        mine[...] = value
        self.going = [self.link.step(mine, mine, (0, 0, a, b)) for a in range(4) for b in range(2) if a or b]

    def total(self):
        for cp in self.going:
            cp.wait_recv()
        value = None
        for i in range(4):
            for j in range(2):
                v = self.deep[i, j]
                value = v if value is None else value + v
        return value


def acc(dst, srcs, lead):
    lead = lead[:-1]
    total = 1
    for d in lead:
        total *= d

    def body(t, carry):
        idx = []
        for d in reversed(lead):
            idx.append(lax.rem(t, d))
            t = t // d
        idx = tuple(reversed(idx))
        v = srcs[0][idx].astype(F32)
        for src in srcs[1:]:
            v = v + src[idx].astype(F32)
        dst[idx] = v.astype(dst.dtype)
        return carry

    lax.fori_loop(0, total, body, 0)


D = 768
LAYERS = 2
STEP = 5
beta_first = 0.9
beta_second = 0.999
adam_epsilon = 1e-08
clip_limit = 1.0
HEADS = 12
HEAD_DIM = 64
T = 256
norm_epsilon = 1e-05
SQ = 0.7978845608028654
CUBE = 0.044715
highest = lax.Precision.HIGHEST


def dot_of(a, b, dims, **kw):
    return lax.dot_general(a, b, (dims, ((), ())), preferred_element_type=F32, **kw)


def dot_nt(a, b):
    return dot_of(a, b, ((1,), (1,)))


def dot_nn(a, b):
    return dot_of(a, b, ((1,), (0,)))


def dot_tn(a, b):
    return dot_of(a, b, ((0,), (0,)))


def loop(n, fn):
    def body(t, carry):
        fn(t)
        return carry
    lax.fori_loop(0, n, body, 0)


def tile(t, size):
    return pl.ds(pl.multiple_of(t * size, size), size)


def stats(v):
    centred = v - jnp.mean(v, axis=-1, keepdims=True)
    scale = lax.rsqrt(jnp.mean(centred * centred, axis=-1, keepdims=True) + norm_epsilon)
    return centred * scale, scale


def norm_rows(src, dst, gain, shift):
    def step(t):
        r = tile(t, 64)
        unit, _ = stats(src[r, :].astype(F32))
        dst[r, :] = (unit * gain + shift).astype(BF)
    loop(T // 64, step)


def norm_back(src, grad, base, dst, gain, low_dst):
    def step(t, carry):
        to_gain, to_shift = carry
        r = tile(t, 64)
        unit, scale = stats(src[r, :].astype(F32))
        g = grad[r, :]
        to_gain = to_gain + jnp.sum((g * unit).reshape(8, 8, D), axis=0)
        to_shift = to_shift + jnp.sum(g.reshape(8, 8, D), axis=0)
        g = g * gain
        out = base[r, :] + scale * (
            g - jnp.mean(g, axis=-1, keepdims=True) - unit * jnp.mean(g * unit, axis=-1, keepdims=True)
        )
        dst[r, :] = out
        if low_dst is not None:
            low_dst[r, :] = out.astype(BF)
        return (to_gain, to_shift)
    zero = jnp.zeros((8, D), F32)
    to_gain, to_shift = lax.fori_loop(0, T // 64, step, (zero, zero))
    return jnp.sum(to_gain, axis=0, keepdims=True), jnp.sum(to_shift, axis=0, keepdims=True)


def grids():
    return lax.broadcasted_iota(jnp.int32, (T, T), 0), lax.broadcasted_iota(jnp.int32, (T, T), 1)


def halves(pair):
    lane = lax.broadcasted_iota(jnp.int32, (T, 128), 1)
    zero = jnp.zeros_like(pair)
    return jnp.where(lane < HEAD_DIM, pair, zero), jnp.where(lane < HEAD_DIM, zero, pair)


SCALE = HEAD_DIM ** -0.5
FT = 384


def slots_at(ref, t, f):
    return ref[t, f // 4, lax.rem(f, 4)].reshape(FT, 256)


def put_slots(ref, f, value):
    for t in range(3):
        ref[t, f // 4, lax.rem(f, 4)] = value[:, 256 * t:256 * t + 256].reshape(4, 4, 24, 256).astype(BF)


def first_scores(proj):
    q, _ = halves(proj[:, 0:128])
    return dot_nt(q * jnp.asarray(SCALE, BF), proj[:, D:D + 128])


def attention(proj, probs, attended, bias, length):
    row, col = grids()
    scores = first_scores(proj)
    chosen = jnp.maximum(scores, 0.0) + jnp.log(1.0 + jnp.exp(-jnp.abs(scores)))
    chosen = jnp.where((col > 0) & (col < row) & (row < length), chosen, 0.0)
    forget = dot_of((col < row).astype(F32), chosen, ((1,), (0,)), precision=highest)
    bias[...] = jnp.where((col <= row) & (col < length), forget, 1e30)

    def pair(p):
        at = tile(p, 128)
        q = halves(proj[:, at] * jnp.asarray(SCALE, BF))
        k = proj[:, tile(6 + p, 128)]
        v = halves(proj[:, tile(12 + p, 128)])
        total = None
        for h in range(2):
            logits = dot_nt(q[h], k) - bias[...]
            e = jnp.exp(logits - jnp.max(logits, axis=-1, keepdims=True))
            e = (e * (1.0 / jnp.sum(e, axis=-1, keepdims=True))).astype(BF)
            probs[2 * p + h] = e
            part = dot_nn(e, v[h])
            total = part if h == 0 else total + part
        attended[:, at] = total.astype(BF)
    loop(6, pair)


def forward_first(s, gains, length):
    norm_rows(s.stream, s.normed, gains[0:1], gains[1:2])
    wj = s.wj.reshape(3 * D, D)
    def project(t):
        s.proj[:, tile(t, 256)] = dot_nt(s.normed[...], wj[tile(t, 256), :]).astype(BF)
    loop(9, project)
    yield
    attention(s.proj, s.probs, s.attended, s.bias, length)
    yield
    wo = s.wo.reshape(D, D)
    def output(t):
        at = tile(t, 256)
        s.mid[:, at] = s.stream[:, at].astype(F32) + dot_nt(s.attended[...], wo[at, :])
    loop(3, output)


def third(t):
    return slice(256 * t, 256 * t + 256)


def forward_second(s, gains):
    norm_rows(s.mid, s.normed2, gains[2:3], gains[3:4])
    s.need("we")
    def raise_(f):
        at = tile(f, FT)
        r = dot_nt(s.normed2[:, third(0)], slots_at(s.we, 0, f))
        for t in (1, 2):
            r = r + dot_nt(s.normed2[:, third(t)], slots_at(s.we, t, f))
        s.raised[:, at] = r
        s.hidden[:, at] = (0.5 * r * (1.0 + jnp.tanh(r * (SQ + SQ * CUBE * r * r)))).astype(BF)
    loop(4 * D // FT, raise_)
    yield
    s.need("ws")
    for t in range(3):
        s.next[:, third(t)] = s.mid[:, third(t)] + dot_nn(s.hidden[...], s.ws[t].reshape(4 * D, 256))


def backward_second(s, gains):
    for name in ("dstream", "ws", "raised", "we", "normed2"):
        s.need(name)

    s.low[...] = s.dstream[...].astype(BF)
    s.acc[...] = jnp.zeros((T, D), F32)
    def step(t):
        at = tile(t, FT)
        dh = dot_nt(s.low[:, third(0)], slots_at(s.ws, 0, t))
        for n in (1, 2):
            dh = dh + dot_nt(s.low[:, third(n)], slots_at(s.ws, n, t))
        r = s.raised[:, at]
        th = jnp.tanh(r * (SQ + SQ * CUBE * r * r))
        hid = (0.5 * r * (1.0 + th)).astype(BF)
        slope = 0.5 * (1.0 + th) + 0.5 * r * (1.0 - th * th) * (SQ + 3.0 * SQ * CUBE * r * r)
        dr = (dh * slope).astype(BF)
        put_slots(s.ws, t, dot_tn(hid, s.low[...]))
        for n in range(3):
            s.acc[:, third(n)] += dot_nn(dr, slots_at(s.we, n, t))
        put_slots(s.we, t, dot_tn(dr, s.normed2[...]))
    pieces = 4 * D // FT // 2
    for piece in range(pieces):
        loop(2, lambda t: step(t + 2 * piece))
        if piece < pieces - 1:
            yield
    s.need("mid")
    s.sums += norm_back(s.mid, s.acc, s.dstream, s.dstream, gains[2:3], s.low)
    yield


def attention_back(proj, probs, dout, dproj, bias, keep, length):
    bias[...] = jnp.zeros((T, T), F32)

    def scores_of(p, h, do, v):
        prob = probs[2 * p + h]
        full = prob.astype(F32)
        dsoft = dot_nt(do, v)
        dl = full * (dsoft - jnp.sum(full * dsoft, axis=-1, keepdims=True))
        bias[...] += dl
        return prob, dl

    def pair(p):
        at, at_k, at_v = tile(p, 128), tile(6 + p, 128), tile(12 + p, 128)
        q = halves(proj[:, at] * jnp.asarray(SCALE, BF))
        k = halves(proj[:, at_k] * jnp.asarray(SCALE, BF))
        v = proj[:, at_v]
        do = halves(dout[:, at])
        dq = dk = dv = None
        for h in range(2):
            prob, dl = scores_of(p, h, do[h], v)
            ds = dl.astype(BF)
            parts = (dot_nn(ds, k[h]), dot_tn(ds, q[h]), dot_tn(prob, do[h]))
            dq, dk, dv = parts if h == 0 else (dq + parts[0], dk + parts[1], dv + parts[2])
        dproj[:, at] = dq.astype(BF)
        dproj[:, at_k] = dk.astype(BF)
        dproj[:, at_v] = dv.astype(BF)
    loop(2, lambda t: pair(t + 1))
    yield
    loop(3, lambda t: pair(t + 3))
    yield

    q = halves(proj[:, 0:128] * jnp.asarray(SCALE, BF))
    k = halves(proj[:, D:D + 128] * jnp.asarray(SCALE, BF))
    v = proj[:, 2 * D:2 * D + 128]
    do = halves(dout[:, 0:128])
    prob1, dl1 = scores_of(0, 1, do[1], v)
    prob0, dl0 = scores_of(0, 0, do[0], v)
    keep[...] = dl0
    row, col = grids()
    dchosen = -dot_of((col > row).astype(F32), bias[...], ((1,), (0,)), precision=highest)
    scores = first_scores(proj)
    slope = 1.0 / (1.0 + jnp.exp(-scores))
    extra = jnp.where((col > 0) & (col < row) & (row < length), dchosen * slope, 0.0)
    ds0 = (keep[...] + extra).astype(BF)
    ds1 = dl1.astype(BF)
    dproj[:, 0:128] = (dot_nn(ds0, k[0]) + dot_nn(ds1, k[1])).astype(BF)
    dproj[:, D:D + 128] = (dot_tn(ds0, q[0]) + dot_tn(ds1, q[1])).astype(BF)
    dproj[:, 2 * D:2 * D + 128] = (dot_tn(prob0, do[0]) + dot_tn(prob1, do[1])).astype(BF)


def backward_first(s, gains, length):
    for name in ("wo", "attended", "proj", "probs"):
        s.need(name)
    wo, wj = s.wo.reshape(D, D), s.wj.reshape(3 * D, D)
    def back(t):
        at = tile(t, 256)
        s.dout[:, at] = dot_nn(s.low[...], wo[:, at]).astype(BF)
    loop(3, back)
    def grad(t):
        at = tile(t, 256)
        wo[at, :] = dot_tn(s.low[:, at], s.attended[...]).astype(BF)
    loop(3, grad)
    yield
    yield from attention_back(s.proj, s.probs, s.dout, s.dproj, s.bias, s.keep, length)
    yield
    s.need("wj")
    s.need("normed")
    s.acc[...] = jnp.zeros((T, D), F32)
    def joint(t):
        at = tile(t, 384)
        d = s.dproj[:, at]
        s.acc[...] += dot_nn(d, wj[at, :])
        wj[at, :] = dot_tn(d, s.normed[...]).astype(BF)
    for piece in range(2):
        loop(3, lambda t: joint(t + 3 * piece))
        yield
    s.need("stream")
    s.sums += norm_back(s.stream, s.acc, s.dstream, s.dstream, gains[0:1], None)


class Names:
    def __init__(self, **kw):
        self.__dict__.update(kw)
        self.coming = {}
        self.sums = ()

    def need(self, name):
        for cp in self.coming.pop(name, ()):
            cp.wait()


WEIGHTS = dict(wj=((4, 2, 2, 144, D), BF), wo=((4, 2, 2, 48, D), BF), we=((3, 2, 4, 4, 4, 24, 256), BF), ws=((3, 2, 4, 4, 4, 24, 256), BF))
SAVED = dict(mid=((T, D), F32), normed=((T, D), BF), normed2=((T, D), BF), proj=((T, 3 * D), BF), probs=((HEADS, T, T), BF),
    attended=((T, D), BF), raised=((T, 4 * D), F32))
ONCE = dict(bias=((T, T), F32), hidden=((T, 4 * D), BF), next=((T, D), F32))
BACK = dict(bias=((T, T), F32), keep=((T, T), F32), dstream=((T, D), F32), low=((T, D), BF), acc=((T, D), F32), dout=((T, D), BF),
    dproj=((T, 3 * D), BF))


def fetch(ins, s, loc, names):
    for n in names:
        s.coming[n] = [loc.copy(getattr(ins, n), getattr(s, n))]


def run(pieces):
    for _ in pieces:
        pass


def gains_of(sums):
    gain2, shift2, gain1, shift1 = sums
    return jnp.concatenate([gain1, shift1, gain2, shift2], axis=0)


def live_rows(length):
    return lax.broadcasted_iota(jnp.int32, (T, D), 0) < length


def own_columns(which):
    lane = lax.broadcasted_iota(jnp.int32, (1, D), 1)
    return [(lane == which * 6 + j).astype(F32) for j in range(6)]


OWN = ((3, 4, 4, 4, 24, 256), BF)
SIBLING = dict(sib_wj=((4, 2, 144, D), BF), sib_wo=((4, 2, 48, D), BF), sib_we=OWN, sib_ws=OWN)


def side_of(ref, name, core, at=slice(None)):
    return ref.at[at, :, core] if name in ("wj", "wo") else ref.at[:, core]


class Pair:
    def __init__(self, s, link, c):
        self.s, self.link, self.c = s, link, c
        self.going, self.copies = {}, {}

    def send(self, name, at=slice(None)):
        src, dst = side_of(getattr(self.s, name), name, 1 - self.c, at), getattr(self.s, "sib_" + name)
        cp = self.link.send(src, dst.at[at] if name == "wj" else dst, 3, 1)
        self.going.setdefault(name, []).append(cp)
        self.copies.setdefault(name, []).append(cp)

    def arrived(self, name):
        for cp in self.going.pop(name):
            cp.wait_recv()

    def join(self, name):
        self.arrived(name)
        mine, other = side_of(getattr(self.s, name), name, self.c), getattr(self.s, "sib_" + name)
        acc(mine, [mine, other], (3, 4, 4))

    def join_rows(self, perm):
        self.arrived("wj")
        self.arrived("wo")
        s = self.s
        def step(n):
            x, h = n // 2, lax.rem(n, 2)
            j = s.wj[x, h, self.c].astype(F32) + s.sib_wj[x, h].astype(F32)
            o = s.wo[x, h, self.c].astype(F32) + s.sib_wo[x, h].astype(F32)
            rows = jnp.concatenate([j.astype(BF), o.astype(BF)], axis=0)
            slots = dot_tn(perm, rows)
            for t in range(3):
                s.ga[t, x, pl.ds(2 * h, 2)] = slots[:, 256 * t:256 * t + 256].reshape(2, 4, 24, 256).astype(BF)
        loop(8, step)


def compact(slots, wj, wo, perm):
    def step(n):
        x, h, c = n // 4, lax.rem(n // 2, 2), lax.rem(n, 2)
        for t in range(3):
            rows = dot_nn(perm, slots[t, c, x, pl.ds(2 * h, 2)].reshape(192, 256)).astype(BF)
            wj[x, h, c, :, third(t)] = rows[:144]
            wo[x, h, c, :, third(t)] = rows[144:]
    loop(16, step)


class Gather:
    def __init__(self, link, loc, piece, dst):
        self.link, self.loc, self.piece, self.dst = link, loc, piece, dst
        self.co = link.co

    def slots(self, t, sel):
        return self.dst.at[(t, self.co[3], *sel)]

    def small(self):
        self.own, self.one = [], []
        for t in range(3):
            src, dst = self.piece.at[:, third(t)], self.slots(t, self.co[:3])
            self.own.append(self.loc.copy(src, dst))
            self.one.append([self.link.send(src, dst, RINGS[t][0], k) for k in (1, 3, 2)])

    def slab(self):
        self.two = []
        for t in range(3):
            self.own[t].wait()
            for cp in self.one[t]:
                cp.wait_recv()
            u, v = RINGS[t]
            sel = list(self.co[:3])
            sel[u] = slice(None)
            ref = self.slots(t, sel)
            self.two.append([self.link.send(ref, ref, v, k) for k in (1, 3)])

    def slab_on(self):
        self.three = []
        for t in range(3):
            u, v = RINGS[t]
            for side, back, on in ((0, 3, 1), (1, 1, 3)):
                self.two[t][side].wait_recv()
                sel = list(moved(self.co, v, back)[:3])
                sel[u] = pl.ds(2 * side, 2)
                ref = self.slots(t, sel)
                self.three.append(self.link.send(ref, ref, v, on))

    def block(self):
        for cp in self.three:
            cp.wait_recv()
        self.four = []
        for t in range(3):
            sel = [slice(None)] * 3
            sel[t] = self.co[t]
            ref = self.slots(t, sel)
            self.four.append([self.link.send(ref, ref, t, k) for k in (1, 3)])

    def block_on(self):
        self.five = []
        for t in range(3):
            u, v = RINGS[t]
            for side, back, on in ((0, 3, 1), (1, 1, 3)):
                self.four[t][side].wait_recv()
                sel = [slice(None)] * 3
                sel[t] = moved(self.co, t, back)[t]
                sel[u] = pl.ds(2 * side, 2)
                ref = self.slots(t, sel)
                self.five.append(self.link.send(ref, ref, t, on))

    def across(self):
        for cp in self.five:
            cp.wait_recv()
        c = self.co[3]
        self.six = [self.link.send(self.dst.at[t, c], self.dst.at[t, c], 3, 1) for t in range(3)]

    def ready(self):
        for cp in self.six:
            cp.wait_recv()


def first_body(ins, out, s, loc, link, co):
    x, y, z, c = co
    length = ins.length[0]
    fetch(ins, s, loc, ("stream",))
    targets = [[s.slots.at[0], s.we, s.ws], [s.slots.at[1], s.later_we, s.later_ws]]
    items = []
    for l in range(2):
        rows = jnp.concatenate([ins.joint[:, l, :], ins.output[:, l, :]], axis=0)
        for w, value in enumerate((rows, ins.expand[l], ins.shrink[l])):
            s.piece[l, w] = value.astype(BF)
            items.append(Gather(link, loc, s.piece.at[l, w], targets[l][w]))
    s.met()
    for item in items:
        item.small()
    which = ((x * 2 + y // 2) * 2 + c) * 8 + lax.rem(y, 2) * 4 + z
    masks = own_columns(which)
    placed = []
    for l in range(2):
        rows = ins.layer_gains[l].astype(BF).astype(F32)
        total = rows[:, 0:1] * masks[0]
        for j in range(1, 6):
            total = total + rows[:, j:j + 1] * masks[j]
        placed.append(total)
    gain_sum = WideSum(link, s.gwide, s.gdeep)
    gain_sum.first(jnp.concatenate(placed, axis=0))

    done = []
    perm = ins.perm

    def step(k):
        if k + 2 < 6:
            items[k + 2].block()
        if 0 < k < 7:
            items[k - 1].across()
        if k < 6:
            items[k].block_on()

    def save(*names, prefix=""):
        for n in names:
            done.append(loc.copy(getattr(s, n), getattr(out, prefix + n)))

    for item in items:
        item.slab()
    gain_sum.second()
    for item in items[:3]:
        item.slab_on()
    items[0].block()
    for item in items[3:]:
        item.slab_on()
    items[1].block()
    out.gains_all[...] = gain_sum.total()
    gains = out.gains_all[0:4]
    step(0)
    step(1)
    items[0].ready()
    compact(s.slots.at[0], s.wj, s.wo, perm[...])
    step(2)
    save("wj", "wo")
    s.need("stream")
    first = forward_first(s, gains, length)
    next(first)
    step(3)
    next(first)
    run(first)
    step(4)
    items[1].ready()
    second = forward_second(s, gains)
    next(second)
    items[2].ready()
    save("normed", "proj", "probs", "attended", "mid", "normed2", "raised")
    run(second)
    s.second[...] = s.next[...]
    for cp in done:
        cp.wait()
    done.clear()
    save("we", "ws")
    done.append(loc.copy(s.second, out.top_stream))
    top = Names(**{k: v for k, v in s.__dict__.items() if k not in ("coming", "sums", "stream", "met", "we", "ws")}, stream=s.second, we=s.later_we,
        ws=s.later_ws)
    gains = out.gains_all[4:8]
    step(5)
    items[3].ready()
    compact(s.slots.at[1], s.wj, s.wo, perm[...])
    save("wj", "wo", prefix="top_")
    first = forward_first(top, gains, length)
    next(first)
    step(6)
    items[4].ready()
    done.append(loc.copy(s.later_we, out.top_we))
    next(first)
    run(first)
    save("normed", "proj", "probs", "attended", "mid", prefix="top_")
    second = forward_second(top, gains)
    next(second)
    save("normed2", "raised", prefix="top_")
    link.drain()
    items[5].ready()
    done.append(loc.copy(s.later_ws, out.top_ws))
    run(second)
    out.layer_output[...] = s.next[...].astype(BF)
    for cp in done:
        cp.wait()
    link.drain()


class Reduce:
    def __init__(self, link, s, l, w, source):
        self.link, self.s, self.l, self.w, self.source, self.co = link, s, l, w, source, link.co

    def at(self, t, k):
        sel = [slice(None)] * 3
        sel[t] = moved(self.co, t, k)[t]
        return self.source.at[(t, *sel)]

    def half(self, ref, h):
        return ref.at[pl.ds(2 * h, 2)]

    def r1(self, t, side):
        return self.s.r1.at[self.l, self.w, t, side]

    def r2(self, t, side):
        return self.s.r2.at[self.l, t, side, :, :, self.w]

    def far(self):
        self.hop1 = [[self.link.send(self.half(self.at(t, 2), side), self.r1(t, side), t, k) for side, k in ((0, 1), (1, 3))]
            for t in range(3)]

    def near(self):
        self.hop2 = [[self.link.send(self.half(self.at(t, k), 1 - side), self.half(self.r2(t, side), 1 - side), t, k)
            for side, k in ((0, 1), (1, 3))] for t in range(3)]

    def onward(self):
        for t in range(3):
            for side, k in ((0, 1), (1, 3)):
                self.hop1[t][side].wait_recv()
                o = self.half(self.at(t, k), side)
                acc(o, [o, self.r1(t, side)], (2, 4))
                self.hop2[t].append(self.link.send(o, self.half(self.r2(t, side), side), t, k))

    def collect(self):
        for t in range(3):
            for cp in self.hop2[t]:
                cp.wait_recv()
            acc(self.r2(t, 0), [self.at(t, 0), self.r2(t, 0), self.r2(t, 1)], (4, 4))

    def sent(self):
        self.link.sent([cp for t in range(3) for cp in (*self.hop1[t], *self.hop2[t])])


class Settle:
    def __init__(self, link, s, l, first, count):
        self.link, self.s, self.l, self.first, self.count = link, s, l, first, count
        self.which = pl.ds(first, count)

    def row(self, t, q):
        block = self.s.r2.at[self.l, t, 0]
        return block.at[:, q, self.which] if RINGS[t][1] == PLANES[t][1] else block.at[q, :, self.which]

    def send(self):
        co, self.going = self.link.co, []
        for t in range(3):
            v = RINGS[t][1]
            self.going.append([self.link.send(self.row(t, moved(co, v, k)[v]), self.s.m1.at[self.l, t, k - 1, :, self.which], v, k)
                for k in (2, 1, 3)])

    def cross(self):
        co, self.last = self.link.co, []
        for t in range(3):
            for cp in self.going[t]:
                cp.wait_recv()
            u, v = RINGS[t]
            got = [self.s.m1.at[self.l, t, k, :, self.which] for k in range(3)]
            acc(got[0], [self.row(t, co[v])] + got, (4, self.count))
            self.last.append([self.link.send(self.s.m1.at[self.l, t, 0, moved(co, u, k)[u], self.which],
                self.s.u2.at[self.l, t, k - 1, self.which], u, k) for k in (2, 1, 3)])

    def final(self, square):
        co = self.link.co
        for t in range(3):
            for cp in self.last[t]:
                cp.wait_recv()
            u = RINGS[t][0]
            for w in range(self.first, self.first + self.count):
                g = self.s.m1[self.l, t, 0, co[u], w].astype(F32)
                for k in range(3):
                    g = g + self.s.u2[self.l, t, k, w].astype(F32)
                self.s.grads[self.l, w, :, third(t)] = g
                g = g * g
                g = g[0:8] + g[8:16] + g[16:24]
                g = g[:, 0:128] + g[:, 128:256]
                square = g if square is None else square + g
        return square


def second_body(ins, out, s, loc, link, co):
    x, y, z, c = co
    length = ins.length[0]
    shared = {k: v for k, v in s.__dict__.items() if k not in ("coming", "sums", "met")}
    base = Names(**shared)
    top = Names(**{**shared, **{k: getattr(s, "top_" + k) for k in ("we", "ws", "stream")}})
    layers = (base, top)
    pairs = [Pair(n, link, c) for n in layers]
    sums = [[Reduce(link, s, l, w, (n.ga, n.we.at[:, c], n.ws.at[:, c])[w]) for w in range(3)] for l, n in enumerate(layers)]
    low, up = sums
    top_end, ff_end, row_end = Settle(link, s, 1, 0, 3), Settle(link, s, 0, 1, 2), Settle(link, s, 0, 0, 1)
    perm = ins.perm

    def bring(n, prefix, *names):
        for name in names:
            n.coming[name] = [loc.copy(getattr(ins, prefix + name), getattr(n, name))]

    bring(top, "top_", "ws", "raised", "we", "normed2", "mid", "wo", "attended", "proj", "probs", "wj", "normed", "stream")
    bring(base, "", "we", "ws", "stream")
    s.dstream[...] = jnp.where(live_rows(length), ins.cotangent[...].astype(F32), 0.0)
    g = ins.gains[4:8]
    run(backward_second(top, g))
    s.met()
    pairs[1].send("ws")
    pairs[1].send("we")
    bring(base, "", "raised", "normed2", "mid")
    for k, _ in enumerate(backward_first(top, g, length)):
        if k == 0:
            pairs[1].send("wo")
        if k == 3:
            bring(base, "", "attended", "proj", "probs")
            pairs[1].join("ws")
            up[2].far()
            up[2].near()
        if k == 4:
            pairs[1].send("wj", pl.ds(0, 2))
        if k == 5:
            pairs[1].send("wj", pl.ds(2, 2))
    bring(base, "", "normed")
    pairs[1].join("we")
    up[1].far()
    up[1].near()
    square = None
    base.coming["dstream"] = []
    g = ins.gains[0:4]
    for k, _ in enumerate(backward_second(base, g)):
        if k == 0:
            up[2].onward()
        if k == 1:
            pairs[1].join_rows(perm[...])
            up[0].far()
            up[0].near()
            link.sent(pairs[1].copies["wj"] + pairs[1].copies["wo"])
            bring(base, "", "wj", "wo")
            pl.semaphore_signal(s.credit, inc=1, device_id=device_at(*moved(co, 3, 1)), device_id_type=MESH)
            up[1].onward()
    pl.semaphore_wait(s.credit, 1)
    pairs[0].send("ws")
    pairs[0].send("we")
    up[2].collect()
    for k, _ in enumerate(backward_first(base, g, length)):
        if k == 0:
            pairs[0].send("wo")
            up[0].onward()
        if k == 1:
            up[1].collect()
        if k == 3:
            pairs[0].join("ws")
            low[2].far()
            low[2].near()
            up[0].collect()
            top_end.send()
        if k == 4:
            pairs[0].send("wj", pl.ds(0, 2))
        if k == 5:
            pairs[0].send("wj", pl.ds(2, 2))
            pairs[0].join("we")
            low[1].far()
            low[1].near()
            top_end.cross()
    gain_sum = WideSum(link, s.gwide, s.gdeep)
    gain_sum.first(jnp.concatenate([gains_of(base.sums), gains_of(top.sums)], axis=0))
    copies = [loc.copy(s.dstream, out.dstream)]
    low[2].onward()
    up[0].sent()
    pairs[0].join_rows(perm[...])
    low[0].far()
    low[0].near()
    low[1].onward()
    low[2].collect()
    gain_sum.second()
    low[0].onward()
    low[1].collect()
    ff_end.send()
    square = top_end.final(square)
    low[0].collect()
    row_end.send()
    ff_end.cross()
    gains_sum = gain_sum.total()
    out.gains_sum[...] = gains_sum
    row_end.cross()
    square = ff_end.final(square)
    square = row_end.final(square)
    copies.append(loc.copy(s.grads, out.grads))
    norm_sum = WideSum(link, s.nwide, s.ndeep)
    norm_sum.first(square)
    link.drain()
    norm_sum.second()
    whole = norm_sum.total()
    norm = jnp.sqrt(jnp.sum(jnp.sum(whole, axis=0, keepdims=True), axis=1, keepdims=True)
        + jnp.sum(jnp.sum(gains_sum * gains_sum, axis=0, keepdims=True), axis=1, keepdims=True))
    out.norm[...] = jnp.broadcast_to(norm, (8, 128))
    for cp in copies:
        cp.wait()
    link.drain()


RATES = dict(matrix=(0.05, 0.1), gains=(0.25, 0.0))


def adam(master, gradient, moment, square, kind, clip):
    rate, decay = RATES[kind]
    clipped = gradient * clip
    momentum = beta_first * moment + (1.0 - beta_first) * clipped
    variance = beta_second * square + (1.0 - beta_second) * clipped * clipped
    corrected_first = momentum / (1.0 - beta_first**STEP)
    corrected_second = variance / (1.0 - beta_second**STEP)
    updated = master - rate * (corrected_first / (jnp.sqrt(corrected_second) + adam_epsilon) + decay * master)
    return updated, momentum, variance


def update_body(ins, out, s, loc, link, co):
    x, y, z, c = co
    out.input_gradient[...] = ins.dstream[...]
    out.layer_output[...] = ins.low_output[...]
    which = ((x * 2 + y // 2) * 2 + c) * 8 + lax.rem(y, 2) * 4 + z
    columns = [jnp.sum(ins.gains_sum[...] * m, axis=-1, keepdims=True) for m in own_columns(which)]
    lane = lax.broadcasted_iota(jnp.int32, (8, 6), 1)
    own_gains = jnp.zeros((8, 6), F32)
    for j in range(6):
        own_gains = own_gains + jnp.where(lane == j, columns[j], 0.0)
    norm = ins.norm[0:1, 0:1]
    out.gradient_norm[...] = norm
    clip = jnp.minimum(1.0, clip_limit / (norm + 1e-06))
    for l in range(2):
        for name, w, rows in (("joint", 0, slice(0, 18)), ("output", 0, slice(18, 24)), ("expand", 1, slice(0, 24)), ("shrink", 2, slice(0, 24))):
            at = (slice(None), l, slice(None)) if w == 0 else (l, slice(None), slice(None))
            new = adam(getattr(ins, name)[at], ins.grads[l, w, rows, :], getattr(ins, name + "_moment")[at], getattr(ins, name + "_square")[at], "matrix", clip)
            for kind, v in zip(("master", "momentum", "variance"), new):
                getattr(out, name + "_" + kind)[at] = v
        new = adam(ins.layer_gains[l], own_gains[4 * l:4 * l + 4], ins.gains_moment[l], ins.gains_square[l], "gains", clip)
        for kind, v in zip(("master", "momentum", "variance"), new):
            getattr(out, "gains_" + kind)[l] = v


def call(body, inputs, outs, scratch, copies, remote=0, collective=None, planes=(), credit=False, limit=63 << 20):
    in_names, out_names, names = list(inputs), list(outs), list(scratch)
    shapes = [pltpu.VMEM(*scratch[n]) for n in names] + [pltpu.SemaphoreType.DMA((copies,))]
    params = dict(vmem_limit_bytes=limit)
    if remote:
        shapes += [pltpu.SemaphoreType.DMA((remote,)), pltpu.SemaphoreType.DMA((remote,))]
        params.update(collective_id=collective, has_side_effects=True)
    if credit:
        shapes.append(pltpu.SemaphoreType.REGULAR)

    def kernel(*refs):
        ins = Names(**dict(zip(in_names, refs)))
        out = Names(**dict(zip(out_names, refs[len(in_names):])))
        rest = refs[len(in_names) + len(out_names):]
        bufs = Names(**dict(zip(names, rest)))
        loc = Local(rest[len(names)])
        co = place()
        if not remote:
            body(ins, out, bufs, loc, None, co)
            return
        if credit:
            bufs.credit = rest[-1]
        bufs.met = greet(co, planes)
        link = Link(co, *rest[len(names) + 1:len(names) + 3])
        body(ins, out, bufs, loc, link, co)

    result = pl.pallas_call(
        kernel,
        out_shape=tuple(jax.ShapeDtypeStruct(*outs[n][1:]) for n in out_names),
        in_specs=[pl.BlockSpec(memory_space=inputs[n][0]) for n in in_names],
        out_specs=tuple(pl.BlockSpec(memory_space=outs[n][0]) for n in out_names),
        scratch_shapes=shapes,
        compiler_params=pltpu.CompilerParams(**params),
    )(*[inputs[n][1] for n in in_names])
    return Names(**dict(zip(out_names, result)))


def hbm(table, prefix=""):
    return {prefix + k: (ANY, *v) for k, v in table.items()}


ROWS = dict(joint=((18, 2, D), F32), output=((6, 2, D), F32), expand=((2, 24, D), F32), shrink=((2, 24, D), F32))
SUMS = dict(gwide=((4, 4, 8, D), F32), gdeep=((4, 2, 8, D), F32))


def slot_order():
    order = np.zeros((192, 192), np.float32)
    for f in range(8):
        for r in range(18):
            order[18 * f + r, 24 * f + r] = 1
        for r in range(6):
            order[144 + 6 * f + r, 24 * f + 18 + r] = 1
    return jnp.asarray(order, BF)


def first_kernel(shards, layer_gains, tokens, length, perm):
    ins = dict(layer_gains=(VMEM, layer_gains), stream=(ANY, tokens), length=(SMEM, length), perm=(VMEM, perm),
        **{k: (VMEM, v) for k, v in shards.items()})
    row = ((T, D), F32)
    outs = {**hbm(WEIGHTS), **hbm(SAVED), **hbm(WEIGHTS, "top_"), **hbm(SAVED, "top_"), "top_stream": (ANY, *row),
        "gains_all": (VMEM, (8, D), F32), "layer_output": (VMEM, (T, D), BF)}
    own = dict(stream=((T, D), BF), second=row, piece=((2, 3, 24, D), BF), slots=((2, 3, 2, 4, 4, 4, 24, 256), BF), later_we=WEIGHTS["we"],
        later_ws=WEIGHTS["ws"])
    return call(first_body, ins, outs, {**WEIGHTS, **SAVED, **ONCE, **own, **SUMS}, 64, 272, 0, ((0, 1),))


def second_kernel(tokens, length, cotangent, ahead, perm):
    names = (*WEIGHTS, *SAVED)
    ins = dict(stream=(ANY, tokens), length=(SMEM, length), perm=(VMEM, perm), cotangent=(VMEM, cotangent),
        gains=(VMEM, ahead.gains_all), top_stream=(ANY, ahead.top_stream), **{k: (ANY, getattr(ahead, k)) for k in names},
        **{"top_" + k: (ANY, getattr(ahead, "top_" + k)) for k in names})
    outs = dict(dstream=(ANY, (T, D), F32), norm=(VMEM, (8, 128), F32), grads=(ANY, (2, 3, 24, D), F32),
        gains_sum=(VMEM, (8, D), F32))
    own = dict(stream=((T, D), BF), top_stream=((T, D), F32), ga=OWN, r1=((2, 3, 3, 2, 2, 4, 24, 256), BF),
        r2=((2, 3, 2, 4, 4, 3, 24, 256), BF), m1=((2, 3, 3, 4, 3, 24, 256), BF), u2=((2, 3, 3, 3, 24, 256), BF), grads=((2, 3, 24, D), F32),
        nwide=((4, 4, 8, 128), F32), ndeep=((4, 2, 8, 128), F32))
    weights = {"top_" + k: WEIGHTS[k] for k in ("we", "ws")}
    return call(second_body, ins, outs, {**WEIGHTS, **weights, **SAVED, **BACK, **own, **SUMS, **SIBLING}, 64, 240, 1, ((0, 1),),
        credit=True)


def update(state, ahead, back):
    ins = dict(dstream=(VMEM, back.dstream), low_output=(VMEM, ahead.layer_output), norm=(VMEM, back.norm),
        grads=(VMEM, back.grads), gains_sum=(VMEM, back.gains_sum), **{k: (VMEM, v) for k, v in state.items()})
    outs = dict(input_gradient=(VMEM, (T, D), F32), layer_output=(VMEM, (T, D), BF), gradient_norm=(VMEM, (1, 1), F32))
    for kind in ("master", "momentum", "variance"):
        for name, v in {**ROWS, "gains": ((2, 4, 6), F32)}.items():
            outs[name + "_" + kind] = (VMEM, *v)
    return call(update_body, ins, outs, {}, 1)


def local(
    tokens,
    lengths,
    cotangent,
    joint_weight,
    output_weight,
    expand_weight,
    shrink_weight,
    layer_gains,
    joint_moment,
    output_moment,
    expand_moment,
    shrink_moment,
    gains_moment,
    joint_square,
    output_square,
    expand_square,
    shrink_square,
    gains_square,
):
    front = lambda a: a.transpose(2, 0, 1)
    swap = lambda a: a.transpose(0, 2, 1)
    shards = dict(joint=front(joint_weight), output=front(output_weight), expand=swap(expand_weight), shrink=shrink_weight)
    perm = slot_order()
    ahead = first_kernel(shards, layer_gains, tokens, lengths, perm)
    back = second_kernel(tokens, lengths, cotangent, ahead, perm)
    state = dict(
        shards,
        joint_moment=front(joint_moment),
        output_moment=front(output_moment),
        expand_moment=swap(expand_moment),
        shrink_moment=shrink_moment,
        joint_square=front(joint_square),
        output_square=front(output_square),
        expand_square=swap(expand_square),
        shrink_square=shrink_square,
        layer_gains=layer_gains,
        gains_moment=gains_moment,
        gains_square=gains_square,
    )
    new = update(state, ahead, back)
    results = [new.layer_output, new.input_gradient, new.gradient_norm.reshape(())]
    for kind in ("master", "momentum", "variance"):
        results += [
            getattr(new, "joint_" + kind).transpose(1, 2, 0),
            getattr(new, "output_" + kind).transpose(1, 2, 0),
            swap(getattr(new, "expand_" + kind)),
            getattr(new, "shrink_" + kind),
            getattr(new, "gains_" + kind),
        ]
    return tuple(results)


AXES = ("dp", "fsdp")


def solution(mesh):
    in_specs = (
        P(AXES, None),
        P(AXES),
        P(AXES, None),
        P(None, None, AXES),
        P(None, None, AXES),
        P(None, None, AXES),
        P(None, AXES, None),
        P(None, None, AXES),
        P(None, None, AXES),
        P(None, None, AXES),
        P(None, None, AXES),
        P(None, AXES, None),
        P(None, None, AXES),
        P(None, None, AXES),
        P(None, None, AXES),
        P(None, None, AXES),
        P(None, AXES, None),
        P(None, None, AXES),
    )
    out_specs = (
        P(AXES, None),
        P(AXES, None),
        P(),
        P(None, None, AXES),
        P(None, None, AXES),
        P(None, None, AXES),
        P(None, AXES, None),
        P(None, None, AXES),
        P(None, None, AXES),
        P(None, None, AXES),
        P(None, None, AXES),
        P(None, AXES, None),
        P(None, None, AXES),
        P(None, None, AXES),
        P(None, None, AXES),
        P(None, None, AXES),
        P(None, AXES, None),
        P(None, None, AXES),
    )
    return jax.shard_map(local, mesh=mesh, in_specs=in_specs, out_specs=out_specs, check_vma=False)
```

```python
import jax
import jax.numpy as jnp
import numpy as np
from jax import lax
from jax.experimental import pallas as pl
from jax.experimental.pallas import tpu as pltpu
from jax.sharding import PartitionSpec as P

MESH = pl.DeviceIdType.MESH
BF = jnp.bfloat16
F32 = jnp.float32
ANY, VMEM, SMEM = pl.ANY, pltpu.VMEM, pltpu.SMEM

def place():
    dp = lax.axis_index("dp"); fs = lax.axis_index("fsdp")
    return (dp // 4, lax.rem(dp // 2, 2) * 2 + fs // 4, lax.rem(fs, 4), lax.rem(dp, 2))

def device_at(x, y, z, c):
    return ((x * 2 + y // 2) * 2 + c, lax.rem(y, 2) * 4 + z)

def moved(co, axis, k):
    n = 2 if axis == 3 else 4
    co = list(co)
    co[axis] = lax.rem(co[axis] + (k % n), n)
    return tuple(co)

PLANES = ((1, 2), (0, 2), (0, 1))
RINGS = ((1, 2), (2, 0), (0, 1))
CORNERS = [(a, b) for a in range(4) for b in range(4) if (a, b) != (0, 0)]


def greet(co, planes):
    steps = {(0, 0, k, 1) for k in range(4)}
    for k in (1, 2, 3):
        steps |= {(k, 0, 0, 0), (0, k, 0, 0), (0, 0, k, 0)}
    for axes in planes:
        for corner in CORNERS:
            step = [0, 0, 0, 0]
            step[axes[0]], step[axes[1]] = corner
            steps.add(tuple(step))
    bar = pltpu.get_barrier_semaphore()
    for step in sorted(steps):
        pl.semaphore_signal(bar, inc=1, device_id=device_at(*stepped(co, step)), device_id_type=MESH)
    return lambda: pl.semaphore_wait(bar, len(steps))


def stepped(co, step):
    for axis, k in enumerate(step):
        if k:
            co = moved(co, axis, k)
    return co


class Link:
    def __init__(self, co, ss, rs):
        self.co, self.ss, self.rs = co, ss, rs
        self.n = 0
        self.out = []
    def send(self, src, dst, axis, k):
        i = self.n
        self.n += 1
        cp = pltpu.make_async_remote_copy(src_ref=src, dst_ref=dst, send_sem=self.ss.at[i], recv_sem=self.rs.at[i],
            device_id=device_at(*moved(self.co, axis, k)), device_id_type=MESH)
        cp.start()
        self.out.append(cp)
        return cp
    def step(self, src, dst, step):
        i = self.n
        self.n += 1
        cp = pltpu.make_async_remote_copy(src_ref=src, dst_ref=dst, send_sem=self.ss.at[i], recv_sem=self.rs.at[i],
            device_id=device_at(*stepped(self.co, step)), device_id_type=MESH)
        cp.start()
        self.out.append(cp)
        return cp

    def plane(self, axes, src_of, dst_of):
        going = []
        for a, b in CORNERS:
            step = [0, 0, 0, 0]
            step[axes[0]], step[axes[1]] = a, b
            going.append(self.step(src_of(a, b), dst_of(a, b), step))
        return going

    def sent(self, copies):
        for cp in copies:
            cp.wait_send()
        self.out = [o for o in self.out if all(o is not cp for cp in copies)]

    def drain(self):
        for cp in self.out:
            cp.wait_send()
        self.out = []

class Local:
    def __init__(self, sems):
        self.sems, self.n = sems, 0
    def copy(self, src, dst):
        cp = pltpu.make_async_copy(src, dst, self.sems.at[self.n])
        self.n += 1
        cp.start()
        return cp

class WideSum:
    def __init__(self, link, wide, deep):
        self.link, self.wide, self.deep = link, wide, deep

    def first(self, value):
        x, y, z, c = self.link.co
        mine = self.wide.at[x, y]
        mine[...] = value
        self.going = self.link.plane((0, 1), lambda a, b: mine, lambda a, b: mine)

    def second(self):
        x, y, z, c = self.link.co
        for cp in self.going:
            cp.wait_recv()
        value = None
        for i in range(4):
            for j in range(4):
                v = self.wide[i, j]
                value = v if value is None else value + v
        mine = self.deep.at[z, c]
        mine[...] = value
        self.going = [self.link.step(mine, mine, (0, 0, a, b)) for a in range(4) for b in range(2) if a or b]

    def total(self):
        for cp in self.going:
            cp.wait_recv()
        value = None
        for i in range(4):
            for j in range(2):
                v = self.deep[i, j]
                value = v if value is None else value + v
        return value


def acc(dst, srcs, lead):
    lead = lead[:-1]
    total = 1
    for d in lead:
        total *= d

    def body(t, carry):
        idx = []
        for d in reversed(lead):
            idx.append(lax.rem(t, d))
            t = t // d
        idx = tuple(reversed(idx))
        v = srcs[0][idx].astype(F32)
        for src in srcs[1:]:
            v = v + src[idx].astype(F32)
        dst[idx] = v.astype(dst.dtype)
        return carry

    lax.fori_loop(0, total, body, 0)


D = 768
LAYERS = 2
STEP = 5
beta_first = 0.9
beta_second = 0.999
adam_epsilon = 1e-08
clip_limit = 1.0
HEADS = 12
HEAD_DIM = 64
T = 256
norm_epsilon = 1e-05
SQ = 0.7978845608028654
CUBE = 0.044715
highest = lax.Precision.HIGHEST


def dot_of(a, b, dims, **kw):
    return lax.dot_general(a, b, (dims, ((), ())), preferred_element_type=F32, **kw)


def dot_nt(a, b):
    return dot_of(a, b, ((1,), (1,)))


def dot_nn(a, b):
    return dot_of(a, b, ((1,), (0,)))


def dot_tn(a, b):
    return dot_of(a, b, ((0,), (0,)))


def loop(n, fn):
    def body(t, carry):
        fn(t)
        return carry
    lax.fori_loop(0, n, body, 0)


def tile(t, size):
    return pl.ds(pl.multiple_of(t * size, size), size)


def stats(v):
    centred = v - jnp.mean(v, axis=-1, keepdims=True)
    scale = lax.rsqrt(jnp.mean(centred * centred, axis=-1, keepdims=True) + norm_epsilon)
    return centred * scale, scale


def norm_rows(src, dst, gain, shift):
    def step(t):
        r = tile(t, 64)
        unit, _ = stats(src[r, :].astype(F32))
        dst[r, :] = (unit * gain + shift).astype(BF)
    loop(T // 64, step)


def norm_back(src, grad, base, dst, gain, low_dst):
    def step(t, carry):
        to_gain, to_shift = carry
        r = tile(t, 64)
        unit, scale = stats(src[r, :].astype(F32))
        g = grad[r, :]
        to_gain = to_gain + jnp.sum((g * unit).reshape(8, 8, D), axis=0)
        to_shift = to_shift + jnp.sum(g.reshape(8, 8, D), axis=0)
        g = g * gain
        out = base[r, :] + scale * (
            g - jnp.mean(g, axis=-1, keepdims=True) - unit * jnp.mean(g * unit, axis=-1, keepdims=True)
        )
        dst[r, :] = out
        if low_dst is not None:
            low_dst[r, :] = out.astype(BF)
        return (to_gain, to_shift)
    zero = jnp.zeros((8, D), F32)
    to_gain, to_shift = lax.fori_loop(0, T // 64, step, (zero, zero))
    return jnp.sum(to_gain, axis=0, keepdims=True), jnp.sum(to_shift, axis=0, keepdims=True)


def grids():
    return lax.broadcasted_iota(jnp.int32, (T, T), 0), lax.broadcasted_iota(jnp.int32, (T, T), 1)


def halves(pair):
    lane = lax.broadcasted_iota(jnp.int32, (T, 128), 1)
    zero = jnp.zeros_like(pair)
    return jnp.where(lane < HEAD_DIM, pair, zero), jnp.where(lane < HEAD_DIM, zero, pair)


SCALE = HEAD_DIM ** -0.5
FT = 384


def slots_at(ref, t, f):
    return ref[t, f // 4, lax.rem(f, 4)].reshape(FT, 256)


def put_slots(ref, f, value):
    for t in range(3):
        ref[t, f // 4, lax.rem(f, 4)] = value[:, 256 * t:256 * t + 256].reshape(4, 4, 24, 256).astype(BF)


def first_scores(proj):
    q, _ = halves(proj[:, 0:128])
    return dot_nt(q * jnp.asarray(SCALE, BF), proj[:, D:D + 128])


def attention(proj, probs, attended, bias, length):
    row, col = grids()
    scores = first_scores(proj)
    chosen = jnp.maximum(scores, 0.0) + jnp.log(1.0 + jnp.exp(-jnp.abs(scores)))
    chosen = jnp.where((col > 0) & (col < row) & (row < length), chosen, 0.0)
    forget = dot_of((col < row).astype(F32), chosen, ((1,), (0,)), precision=highest)
    bias[...] = jnp.where((col <= row) & (col < length), forget, 1e30)

    def pair(p):
        at = tile(p, 128)
        q = halves(proj[:, at] * jnp.asarray(SCALE, BF))
        k = proj[:, tile(6 + p, 128)]
        v = halves(proj[:, tile(12 + p, 128)])
        total = None
        for h in range(2):
            logits = dot_nt(q[h], k) - bias[...]
            e = jnp.exp(logits - jnp.max(logits, axis=-1, keepdims=True))
            e = (e * (1.0 / jnp.sum(e, axis=-1, keepdims=True))).astype(BF)
            probs[2 * p + h] = e
            part = dot_nn(e, v[h])
            total = part if h == 0 else total + part
        attended[:, at] = total.astype(BF)
    loop(6, pair)


def forward_first(s, gains, length):
    norm_rows(s.stream, s.normed, gains[0:1], gains[1:2])
    wj = s.wj.reshape(3 * D, D)
    def project(t):
        s.proj[:, tile(t, 256)] = dot_nt(s.normed[...], wj[tile(t, 256), :]).astype(BF)
    loop(9, project)
    yield
    attention(s.proj, s.probs, s.attended, s.bias, length)
    yield
    wo = s.wo.reshape(D, D)
    def output(t):
        at = tile(t, 256)
        s.mid[:, at] = s.stream[:, at].astype(F32) + dot_nt(s.attended[...], wo[at, :])
    loop(3, output)


def third(t):
    return slice(256 * t, 256 * t + 256)


def forward_second(s, gains):
    norm_rows(s.mid, s.normed2, gains[2:3], gains[3:4])
    s.need("we")
    def raise_(f):
        at = tile(f, FT)
        r = dot_nt(s.normed2[:, third(0)], slots_at(s.we, 0, f))
        for t in (1, 2):
            r = r + dot_nt(s.normed2[:, third(t)], slots_at(s.we, t, f))
        s.raised[:, at] = r
        s.hidden[:, at] = (0.5 * r * (1.0 + jnp.tanh(r * (SQ + SQ * CUBE * r * r)))).astype(BF)
    loop(4 * D // FT, raise_)
    yield
    s.need("ws")
    for t in range(3):
        s.next[:, third(t)] = s.mid[:, third(t)] + dot_nn(s.hidden[...], s.ws[t].reshape(4 * D, 256))


def backward_second(s, gains):
    for name in ("dstream", "ws", "raised", "we", "normed2"):
        s.need(name)

    s.low[...] = s.dstream[...].astype(BF)
    s.acc[...] = jnp.zeros((T, D), F32)
    def step(t):
        t = lax.rem(t + s.flip, 8)
        at = tile(t, FT)
        dh = dot_nt(s.low[:, third(0)], slots_at(s.ws, 0, t))
        for n in (1, 2):
            dh = dh + dot_nt(s.low[:, third(n)], slots_at(s.ws, n, t))
        r = s.raised[:, at]
        th = jnp.tanh(r * (SQ + SQ * CUBE * r * r))
        hid = (0.5 * r * (1.0 + th)).astype(BF)
        slope = 0.5 * (1.0 + th) + 0.5 * r * (1.0 - th * th) * (SQ + 3.0 * SQ * CUBE * r * r)
        dr = (dh * slope).astype(BF)
        put_slots(s.ws, t, dot_tn(hid, s.low[...]))
        for n in range(3):
            s.acc[:, third(n)] += dot_nn(dr, slots_at(s.we, n, t))
        put_slots(s.we, t, dot_tn(dr, s.normed2[...]))
    pieces = 4 * D // FT // 2
    for piece in range(pieces):
        if piece == pieces // 2:
            for name in ("ws_later", "raised_later", "we_later"):
                s.need(name)
        loop(2, lambda t: step(t + 2 * piece))
        if piece < pieces - 1:
            yield
    s.need("mid")
    s.sums += norm_back(s.mid, s.acc, s.dstream, s.dstream, gains[2:3], s.low)
    yield


def attention_back(proj, probs, dout, dproj, bias, keep, length):
    bias[...] = jnp.zeros((T, T), F32)

    def scores_of(p, h, do, v):
        prob = probs[2 * p + h]
        full = prob.astype(F32)
        dsoft = dot_nt(do, v)
        dl = full * (dsoft - jnp.sum(full * dsoft, axis=-1, keepdims=True))
        bias[...] += dl
        return prob, dl

    def pair(p):
        at, at_k, at_v = tile(p, 128), tile(6 + p, 128), tile(12 + p, 128)
        q = halves(proj[:, at] * jnp.asarray(SCALE, BF))
        k = halves(proj[:, at_k] * jnp.asarray(SCALE, BF))
        v = proj[:, at_v]
        do = halves(dout[:, at])
        dq = dk = dv = None
        for h in range(2):
            prob, dl = scores_of(p, h, do[h], v)
            ds = dl.astype(BF)
            parts = (dot_nn(ds, k[h]), dot_tn(ds, q[h]), dot_tn(prob, do[h]))
            dq, dk, dv = parts if h == 0 else (dq + parts[0], dk + parts[1], dv + parts[2])
        dproj[:, at] = dq.astype(BF)
        dproj[:, at_k] = dk.astype(BF)
        dproj[:, at_v] = dv.astype(BF)
    loop(2, lambda t: pair(t + 1))
    yield
    loop(3, lambda t: pair(t + 3))
    yield

    q = halves(proj[:, 0:128] * jnp.asarray(SCALE, BF))
    k = halves(proj[:, D:D + 128] * jnp.asarray(SCALE, BF))
    v = proj[:, 2 * D:2 * D + 128]
    do = halves(dout[:, 0:128])
    prob1, dl1 = scores_of(0, 1, do[1], v)
    prob0, dl0 = scores_of(0, 0, do[0], v)
    keep[...] = dl0
    row, col = grids()
    dchosen = -dot_of((col > row).astype(F32), bias[...], ((1,), (0,)), precision=highest)
    scores = first_scores(proj)
    slope = 1.0 / (1.0 + jnp.exp(-scores))
    extra = jnp.where((col > 0) & (col < row) & (row < length), dchosen * slope, 0.0)
    ds0 = (keep[...] + extra).astype(BF)
    ds1 = dl1.astype(BF)
    dproj[:, 0:128] = (dot_nn(ds0, k[0]) + dot_nn(ds1, k[1])).astype(BF)
    dproj[:, D:D + 128] = (dot_tn(ds0, q[0]) + dot_tn(ds1, q[1])).astype(BF)
    dproj[:, 2 * D:2 * D + 128] = (dot_tn(prob0, do[0]) + dot_tn(prob1, do[1])).astype(BF)


def backward_first(s, gains, length):
    for name in ("wo", "attended", "proj", "probs"):
        s.need(name)
    wo, wj = s.wo.reshape(D, D), s.wj.reshape(3 * D, D)
    def back(t):
        at = tile(t, 256)
        s.dout[:, at] = dot_nn(s.low[...], wo[:, at]).astype(BF)
    loop(3, back)
    def grad(t):
        at = tile(t, 256)
        wo[at, :] = dot_tn(s.low[:, at], s.attended[...]).astype(BF)
    loop(3, grad)
    yield
    yield from attention_back(s.proj, s.probs, s.dout, s.dproj, s.bias, s.keep, length)
    yield
    s.need("wj")
    s.need("normed")
    s.acc[...] = jnp.zeros((T, D), F32)
    def joint(t):
        at = tile(t, 384)
        d = s.dproj[:, at]
        s.acc[...] += dot_nn(d, wj[at, :])
        wj[at, :] = dot_tn(d, s.normed[...]).astype(BF)
    for piece in range(2):
        loop(3, lambda t: joint(t + 3 * piece))
        yield
    s.need("stream")
    s.sums += norm_back(s.stream, s.acc, s.dstream, s.dstream, gains[0:1], None)


class Names:
    def __init__(self, **kw):
        self.__dict__.update(kw)
        self.coming = {}
        self.sums = ()

    def need(self, name):
        for cp in self.coming.pop(name, ()):
            cp.wait()


WEIGHTS = dict(wj=((4, 2, 2, 144, D), BF), wo=((4, 2, 2, 48, D), BF), we=((3, 2, 4, 4, 4, 24, 256), BF), ws=((3, 2, 4, 4, 4, 24, 256), BF))
SAVED = dict(mid=((T, D), F32), normed=((T, D), BF), normed2=((T, D), BF), proj=((T, 3 * D), BF), probs=((HEADS, T, T), BF),
    attended=((T, D), BF), raised=((T, 4 * D), F32))
ONCE = dict(bias=((T, T), F32), hidden=((T, 4 * D), BF), next=((T, D), F32))
BACK = dict(bias=((T, T), F32), keep=((T, T), F32), dstream=((T, D), F32), low=((T, D), BF), acc=((T, D), F32), dout=((T, D), BF),
    dproj=((T, 3 * D), BF))


def fetch(ins, s, loc, names):
    for n in names:
        s.coming[n] = [loc.copy(getattr(ins, n), getattr(s, n))]


def run(pieces):
    for _ in pieces:
        pass


def gains_of(sums):
    gain2, shift2, gain1, shift1 = sums
    return jnp.concatenate([gain1, shift1, gain2, shift2], axis=0)


def live_rows(length):
    return lax.broadcasted_iota(jnp.int32, (T, D), 0) < length


def own_columns(which):
    lane = lax.broadcasted_iota(jnp.int32, (1, D), 1)
    return [(lane == which * 6 + j).astype(F32) for j in range(6)]


OWN = ((3, 4, 4, 4, 24, 256), BF)
SIBLING = dict(sib_wj=((4, 2, 144, D), BF), sib_wo=((4, 2, 48, D), BF), sib_we=OWN, sib_ws=OWN)


def side_of(ref, name, core, at=slice(None)):
    return ref.at[at, :, core] if name in ("wj", "wo") else ref.at[:, core]


class Pair:
    def __init__(self, s, link, c):
        self.s, self.link, self.c = s, link, c
        self.going, self.copies = {}, {}

    def send(self, name, at=slice(None)):
        src, dst = side_of(getattr(self.s, name), name, 1 - self.c, at), getattr(self.s, "sib_" + name)
        cp = self.link.send(src, dst.at[at] if name == "wj" else dst, 3, 1)
        self.going.setdefault(name, []).append(cp)
        self.copies.setdefault(name, []).append(cp)

    def arrived(self, name):
        for cp in self.going.pop(name):
            cp.wait_recv()

    def join(self, name):
        self.arrived(name)
        mine, other = side_of(getattr(self.s, name), name, self.c), getattr(self.s, "sib_" + name)
        acc(mine, [mine, other], (3, 4, 4))

    def join_rows(self, perm):
        self.arrived("wj")
        self.arrived("wo")
        s = self.s
        def step(n):
            x, h = n // 2, lax.rem(n, 2)
            j = s.wj[x, h, self.c].astype(F32) + s.sib_wj[x, h].astype(F32)
            o = s.wo[x, h, self.c].astype(F32) + s.sib_wo[x, h].astype(F32)
            rows = jnp.concatenate([j.astype(BF), o.astype(BF)], axis=0)
            slots = dot_tn(perm, rows)
            for t in range(3):
                s.ga[t, x, pl.ds(2 * h, 2)] = slots[:, 256 * t:256 * t + 256].reshape(2, 4, 24, 256).astype(BF)
        loop(8, step)


def compact(slots, wj, wo, perm):
    def step(n):
        x, h, c = n // 4, lax.rem(n // 2, 2), lax.rem(n, 2)
        for t in range(3):
            rows = dot_nn(perm, slots[t, c, x, pl.ds(2 * h, 2)].reshape(192, 256)).astype(BF)
            wj[x, h, c, :, third(t)] = rows[:144]
            wo[x, h, c, :, third(t)] = rows[144:]
    loop(16, step)


class Gather:
    def __init__(self, link, loc, piece, dst):
        self.link, self.loc, self.piece, self.dst = link, loc, piece, dst
        self.co = link.co

    def slots(self, t, sel):
        return self.dst.at[(t, self.co[3], *sel)]

    def small(self):
        self.own, self.one = [], []
        for t in range(3):
            src, dst = self.piece.at[:, third(t)], self.slots(t, self.co[:3])
            self.own.append(self.loc.copy(src, dst))
            self.one.append([self.link.send(src, dst, RINGS[t][0], k) for k in (1, 3, 2)])

    def slab(self):
        self.two = []
        for t in range(3):
            self.own[t].wait()
            for cp in self.one[t]:
                cp.wait_recv()
            u, v = RINGS[t]
            sel = list(self.co[:3])
            sel[u] = slice(None)
            ref = self.slots(t, sel)
            self.two.append([self.link.send(ref, ref, v, k) for k in (1, 3)])

    def slab_on(self):
        self.three = []
        for t in range(3):
            u, v = RINGS[t]
            for side, back, on in ((0, 3, 1), (1, 1, 3)):
                self.two[t][side].wait_recv()
                sel = list(moved(self.co, v, back)[:3])
                sel[u] = pl.ds(2 * side, 2)
                ref = self.slots(t, sel)
                self.three.append(self.link.send(ref, ref, v, on))

    def block(self):
        for cp in self.three:
            cp.wait_recv()
        self.four = []
        for t in range(3):
            sel = [slice(None)] * 3
            sel[t] = self.co[t]
            ref = self.slots(t, sel)
            self.four.append([self.link.send(ref, ref, t, k) for k in (1, 3)])

    def block_on(self):
        self.five = []
        for t in range(3):
            u, v = RINGS[t]
            for side, back, on in ((0, 3, 1), (1, 1, 3)):
                self.four[t][side].wait_recv()
                sel = [slice(None)] * 3
                sel[t] = moved(self.co, t, back)[t]
                sel[u] = pl.ds(2 * side, 2)
                ref = self.slots(t, sel)
                self.five.append(self.link.send(ref, ref, t, on))

    def across(self):
        for cp in self.five:
            cp.wait_recv()
        c = self.co[3]
        self.six = [self.link.send(self.dst.at[t, c], self.dst.at[t, c], 3, 1) for t in range(3)]

    def ready(self):
        for cp in self.six:
            cp.wait_recv()


def first_body(ins, out, s, loc, link, co):
    x, y, z, c = co
    length = ins.length[0]
    fetch(ins, s, loc, ("stream",))
    targets = [[s.slots.at[0], s.we, s.ws], [s.slots.at[1], s.later_we, s.later_ws]]
    items = []
    for l in range(2):
        rows = jnp.concatenate([ins.joint[:, l, :], ins.output[:, l, :]], axis=0)
        for w, value in enumerate((rows, ins.expand[l], ins.shrink[l])):
            s.piece[l, w] = value.astype(BF)
            items.append(Gather(link, loc, s.piece.at[l, w], targets[l][w]))
    s.met()
    for item in items:
        item.small()
    which = ((x * 2 + y // 2) * 2 + c) * 8 + lax.rem(y, 2) * 4 + z
    masks = own_columns(which)
    placed = []
    for l in range(2):
        rows = ins.layer_gains[l].astype(BF).astype(F32)
        total = rows[:, 0:1] * masks[0]
        for j in range(1, 6):
            total = total + rows[:, j:j + 1] * masks[j]
        placed.append(total)
    gain_sum = WideSum(link, s.gwide, s.gdeep)
    gain_sum.first(jnp.concatenate(placed, axis=0))

    done = []
    perm = ins.perm

    def step(k):
        if k + 2 < 6:
            items[k + 2].block()
        if 0 < k < 7:
            items[k - 1].across()
        if k < 6:
            items[k].block_on()

    def save(*names, prefix=""):
        for n in names:
            done.append(loc.copy(getattr(s, n), getattr(out, prefix + n)))

    for item in items:
        item.slab()
    gain_sum.second()
    for item in items[:3]:
        item.slab_on()
    items[0].block()
    for item in items[3:]:
        item.slab_on()
    items[1].block()
    out.gains_all[...] = gain_sum.total()
    gains = out.gains_all[0:4]
    step(0)
    step(1)
    items[0].ready()
    compact(s.slots.at[0], s.wj, s.wo, perm[...])
    step(2)
    save("wj", "wo")
    s.need("stream")
    first = forward_first(s, gains, length)
    next(first)
    step(3)
    next(first)
    run(first)
    step(4)
    items[1].ready()
    second = forward_second(s, gains)
    next(second)
    items[2].ready()
    save("normed", "proj", "probs", "attended", "mid", "normed2", "raised")
    run(second)
    s.second[...] = s.next[...]
    for cp in done:
        cp.wait()
    done.clear()
    save("we", "ws")
    done.append(loc.copy(s.second, out.top_stream))
    top = Names(**{k: v for k, v in s.__dict__.items() if k not in ("coming", "sums", "stream", "met", "we", "ws")}, stream=s.second, we=s.later_we,
        ws=s.later_ws)
    gains = out.gains_all[4:8]
    step(5)
    items[3].ready()
    compact(s.slots.at[1], s.wj, s.wo, perm[...])
    save("wj", "wo", prefix="top_")
    first = forward_first(top, gains, length)
    next(first)
    step(6)
    items[4].ready()
    done.append(loc.copy(s.later_we, out.top_we))
    next(first)
    run(first)
    save("normed", "proj", "probs", "attended", "mid", prefix="top_")
    second = forward_second(top, gains)
    next(second)
    save("normed2", "raised", prefix="top_")
    link.drain()
    items[5].ready()
    done.append(loc.copy(s.later_ws, out.top_ws))
    run(second)
    out.layer_output[...] = s.next[...].astype(BF)
    for cp in done:
        cp.wait()
    link.drain()


class Reduce:
    def __init__(self, link, s, l, w, source):
        self.link, self.s, self.l, self.w, self.source, self.co = link, s, l, w, source, link.co

    def at(self, t, k):
        sel = [slice(None)] * 3
        sel[t] = moved(self.co, t, k)[t]
        return self.source.at[(t, *sel)]

    def half(self, ref, h):
        return ref.at[pl.ds(2 * h, 2)]

    def r1(self, t, side):
        return self.s.r1.at[self.l, self.w, t, side]

    def r2(self, t, side):
        return self.s.r2.at[self.l, t, side, :, :, self.w]

    def far(self):
        self.hop1 = [[self.link.send(self.half(self.at(t, 2), side), self.r1(t, side), t, k) for side, k in ((0, 1), (1, 3))]
            for t in range(3)]

    def near(self):
        self.hop2 = [[self.link.send(self.half(self.at(t, k), 1 - side), self.half(self.r2(t, side), 1 - side), t, k)
            for side, k in ((0, 1), (1, 3))] for t in range(3)]

    def onward(self):
        for t in range(3):
            for side, k in ((0, 1), (1, 3)):
                self.hop1[t][side].wait_recv()
                o = self.half(self.at(t, k), side)
                acc(o, [o, self.r1(t, side)], (2, 4))
                self.hop2[t].append(self.link.send(o, self.half(self.r2(t, side), side), t, k))

    def collect(self):
        for t in range(3):
            for cp in self.hop2[t]:
                cp.wait_recv()
            acc(self.r2(t, 0), [self.at(t, 0), self.r2(t, 0), self.r2(t, 1)], (4, 4))

    def sent(self):
        self.link.sent([cp for t in range(3) for cp in (*self.hop1[t], *self.hop2[t])])


class Settle:
    def __init__(self, link, s, l, first, count):
        self.link, self.s, self.l, self.first, self.count = link, s, l, first, count
        self.which = pl.ds(first, count)

    def row(self, t, q):
        block = self.s.r2.at[self.l, t, 0]
        return block.at[:, q, self.which] if RINGS[t][1] == PLANES[t][1] else block.at[q, :, self.which]

    def send(self):
        co, self.going = self.link.co, []
        for t in range(3):
            v = RINGS[t][1]
            self.going.append([self.link.send(self.row(t, moved(co, v, k)[v]), self.s.m1.at[self.l, t, k - 1, :, self.which], v, k)
                for k in (2, 1, 3)])

    def cross(self):
        co, self.last = self.link.co, []
        for t in range(3):
            for cp in self.going[t]:
                cp.wait_recv()
            u, v = RINGS[t]
            got = [self.s.m1.at[self.l, t, k, :, self.which] for k in range(3)]
            acc(got[0], [self.row(t, co[v])] + got, (4, self.count))
            self.last.append([self.link.send(self.s.m1.at[self.l, t, 0, moved(co, u, k)[u], self.which],
                self.s.u2.at[self.l, t, k - 1, self.which], u, k) for k in (2, 1, 3)])

    def final(self, square):
        co = self.link.co
        for t in range(3):
            for cp in self.last[t]:
                cp.wait_recv()
            u = RINGS[t][0]
            for w in range(self.first, self.first + self.count):
                g = self.s.m1[self.l, t, 0, co[u], w].astype(F32)
                for k in range(3):
                    g = g + self.s.u2[self.l, t, k, w].astype(F32)
                self.s.grads[self.l, w, :, third(t)] = g
                g = g * g
                g = g[0:8] + g[8:16] + g[16:24]
                g = g[:, 0:128] + g[:, 128:256]
                square = g if square is None else square + g
        return square


def second_body(ins, out, s, loc, link, co):
    x, y, z, c = co
    length = ins.length[0]
    shared = {k: v for k, v in s.__dict__.items() if k not in ("coming", "sums", "met")}
    base = Names(**shared)
    top = Names(**{**shared, **{k: getattr(s, "top_" + k) for k in ("we", "ws", "stream")}})
    layers = (base, top)
    base.flip = top.flip = 4 * (1 - c)
    pairs = [Pair(n, link, c) for n in layers]
    sums = [[Reduce(link, s, l, w, (n.ga, n.we.at[:, c], n.ws.at[:, c])[w]) for w in range(3)] for l, n in enumerate(layers)]
    low, up = sums
    top_end, ff_end, row_end = Settle(link, s, 1, 0, 3), Settle(link, s, 0, 1, 2), Settle(link, s, 0, 0, 1)
    perm = ins.perm

    def bring(n, prefix, *names):
        for name in names:
            n.coming[name] = [loc.copy(getattr(ins, prefix + name), getattr(n, name))]

    def bring_half(n, prefix, h, *names):
        for name in names:
            half = 1 - c if h == 0 else c
            at = (slice(None), tile(half, 2 * D) if name == "raised" else half)
            n.coming[name + "_later" * h] = [loc.copy(getattr(ins, prefix + name).at[at], getattr(n, name).at[at])]

    bring_half(top, "top_", 0, "ws", "raised", "we")
    bring(top, "top_", "normed2")
    bring_half(top, "top_", 1, "ws", "raised", "we")
    bring(top, "top_", "mid", "wo", "attended", "proj", "probs", "wj", "normed", "stream")
    bring(base, "", "we", "ws", "stream")
    s.dstream[...] = jnp.where(live_rows(length), ins.cotangent[...].astype(F32), 0.0)
    g = ins.gains[4:8]
    for k, _ in enumerate(backward_second(top, g)):
        if k == 1:
            s.met()
            pairs[1].send("ws")
            pairs[1].send("we")
    bring(base, "", "raised", "normed2", "mid")
    for k, _ in enumerate(backward_first(top, g, length)):
        if k == 0:
            pairs[1].send("wo")
        if k == 1:
            pairs[1].join("ws")
            up[2].far()
            up[2].near()
        if k == 3:
            bring(base, "", "attended", "proj", "probs")
            pairs[1].join("we")
            up[1].far()
            up[1].near()
        if k == 4:
            pairs[1].send("wj", pl.ds(0, 2))
        if k == 5:
            pairs[1].send("wj", pl.ds(2, 2))
    bring(base, "", "normed")
    square = None
    base.coming["dstream"] = []
    g = ins.gains[0:4]
    for k, _ in enumerate(backward_second(base, g)):
        if k == 0:
            up[2].onward()
        if k == 1:
            pairs[1].join_rows(perm[...])
            up[0].far()
            up[0].near()
            link.sent(pairs[1].copies["wj"] + pairs[1].copies["wo"])
            bring(base, "", "wj", "wo")
            pl.semaphore_signal(s.credit, inc=1, device_id=device_at(*moved(co, 3, 1)), device_id_type=MESH)
            up[1].onward()
        if k == 2:
            pl.semaphore_wait(s.credit, 1)
            pairs[0].send("ws")
            pairs[0].send("we")
    up[2].collect()
    for k, _ in enumerate(backward_first(base, g, length)):
        if k == 0:
            pairs[0].send("wo")
            up[0].onward()
        if k == 1:
            up[1].collect()
            pairs[0].join("ws")
            low[2].far()
            low[2].near()
        if k == 3:
            up[0].collect()
            top_end.send()
            pairs[0].join("we")
            low[1].far()
            low[1].near()
        if k == 4:
            pairs[0].send("wj", pl.ds(0, 2))
        if k == 5:
            pairs[0].send("wj", pl.ds(2, 2))
            low[2].onward()
    gain_sum = WideSum(link, s.gwide, s.gdeep)
    gain_sum.first(jnp.concatenate([gains_of(base.sums), gains_of(top.sums)], axis=0))
    copies = [loc.copy(s.dstream, out.dstream)]
    up[0].sent()
    pairs[0].join_rows(perm[...])
    low[0].far()
    low[0].near()
    low[1].onward()
    top_end.cross()
    low[2].collect()
    gain_sum.second()
    low[0].onward()
    low[1].collect()
    ff_end.send()
    square = top_end.final(square)
    low[0].collect()
    row_end.send()
    ff_end.cross()
    gains_sum = gain_sum.total()
    out.gains_sum[...] = gains_sum
    row_end.cross()
    square = ff_end.final(square)
    square = row_end.final(square)
    copies.append(loc.copy(s.grads, out.grads))
    norm_sum = WideSum(link, s.nwide, s.ndeep)
    norm_sum.first(square)
    link.drain()
    norm_sum.second()
    whole = norm_sum.total()
    norm = jnp.sqrt(jnp.sum(jnp.sum(whole, axis=0, keepdims=True), axis=1, keepdims=True)
        + jnp.sum(jnp.sum(gains_sum * gains_sum, axis=0, keepdims=True), axis=1, keepdims=True))
    out.norm[...] = jnp.broadcast_to(norm, (8, 128))
    for cp in copies:
        cp.wait()
    link.drain()


RATES = dict(matrix=(0.05, 0.1), gains=(0.25, 0.0))


def adam(master, gradient, moment, square, kind, clip):
    rate, decay = RATES[kind]
    clipped = gradient * clip
    momentum = beta_first * moment + (1.0 - beta_first) * clipped
    variance = beta_second * square + (1.0 - beta_second) * clipped * clipped
    corrected_first = momentum / (1.0 - beta_first**STEP)
    corrected_second = variance / (1.0 - beta_second**STEP)
    updated = master - rate * (corrected_first / (jnp.sqrt(corrected_second) + adam_epsilon) + decay * master)
    return updated, momentum, variance


def update_body(ins, out, s, loc, link, co):
    x, y, z, c = co
    out.input_gradient[...] = ins.dstream[...]
    out.layer_output[...] = ins.low_output[...]
    which = ((x * 2 + y // 2) * 2 + c) * 8 + lax.rem(y, 2) * 4 + z
    columns = [jnp.sum(ins.gains_sum[...] * m, axis=-1, keepdims=True) for m in own_columns(which)]
    lane = lax.broadcasted_iota(jnp.int32, (8, 6), 1)
    own_gains = jnp.zeros((8, 6), F32)
    for j in range(6):
        own_gains = own_gains + jnp.where(lane == j, columns[j], 0.0)
    norm = ins.norm[0:1, 0:1]
    out.gradient_norm[...] = norm
    clip = jnp.minimum(1.0, clip_limit / (norm + 1e-06))
    for l in range(2):
        for name, w, rows in (("joint", 0, slice(0, 18)), ("output", 0, slice(18, 24)), ("expand", 1, slice(0, 24)), ("shrink", 2, slice(0, 24))):
            at = (slice(None), l, slice(None)) if w == 0 else (l, slice(None), slice(None))
            new = adam(getattr(ins, name)[at], ins.grads[l, w, rows, :], getattr(ins, name + "_moment")[at], getattr(ins, name + "_square")[at], "matrix", clip)
            for kind, v in zip(("master", "momentum", "variance"), new):
                getattr(out, name + "_" + kind)[at] = v
        new = adam(ins.layer_gains[l], own_gains[4 * l:4 * l + 4], ins.gains_moment[l], ins.gains_square[l], "gains", clip)
        for kind, v in zip(("master", "momentum", "variance"), new):
            getattr(out, "gains_" + kind)[l] = v


def call(body, inputs, outs, scratch, copies, remote=0, collective=None, planes=(), credit=False, limit=63 << 20):
    in_names, out_names, names = list(inputs), list(outs), list(scratch)
    shapes = [pltpu.VMEM(*scratch[n]) for n in names] + [pltpu.SemaphoreType.DMA((copies,))]
    params = dict(vmem_limit_bytes=limit)
    if remote:
        shapes += [pltpu.SemaphoreType.DMA((remote,)), pltpu.SemaphoreType.DMA((remote,))]
        params.update(collective_id=collective, has_side_effects=True)
    if credit:
        shapes.append(pltpu.SemaphoreType.REGULAR)

    def kernel(*refs):
        ins = Names(**dict(zip(in_names, refs)))
        out = Names(**dict(zip(out_names, refs[len(in_names):])))
        rest = refs[len(in_names) + len(out_names):]
        bufs = Names(**dict(zip(names, rest)))
        loc = Local(rest[len(names)])
        co = place()
        if not remote:
            body(ins, out, bufs, loc, None, co)
            return
        if credit:
            bufs.credit = rest[-1]
        bufs.met = greet(co, planes)
        link = Link(co, *rest[len(names) + 1:len(names) + 3])
        body(ins, out, bufs, loc, link, co)

    result = pl.pallas_call(
        kernel,
        out_shape=tuple(jax.ShapeDtypeStruct(*outs[n][1:]) for n in out_names),
        in_specs=[pl.BlockSpec(memory_space=inputs[n][0]) for n in in_names],
        out_specs=tuple(pl.BlockSpec(memory_space=outs[n][0]) for n in out_names),
        scratch_shapes=shapes,
        compiler_params=pltpu.CompilerParams(**params),
    )(*[inputs[n][1] for n in in_names])
    return Names(**dict(zip(out_names, result)))


def hbm(table, prefix=""):
    return {prefix + k: (ANY, *v) for k, v in table.items()}


ROWS = dict(joint=((18, 2, D), F32), output=((6, 2, D), F32), expand=((2, 24, D), F32), shrink=((2, 24, D), F32))
SUMS = dict(gwide=((4, 4, 8, D), F32), gdeep=((4, 2, 8, D), F32))


def slot_order():
    order = np.zeros((192, 192), np.float32)
    for f in range(8):
        for r in range(18):
            order[18 * f + r, 24 * f + r] = 1
        for r in range(6):
            order[144 + 6 * f + r, 24 * f + 18 + r] = 1
    return jnp.asarray(order, BF)


def first_kernel(shards, layer_gains, tokens, length, perm):
    ins = dict(layer_gains=(VMEM, layer_gains), stream=(ANY, tokens), length=(SMEM, length), perm=(VMEM, perm),
        **{k: (VMEM, v) for k, v in shards.items()})
    row = ((T, D), F32)
    outs = {**hbm(WEIGHTS), **hbm(SAVED), **hbm(WEIGHTS, "top_"), **hbm(SAVED, "top_"), "top_stream": (ANY, *row),
        "gains_all": (VMEM, (8, D), F32), "layer_output": (VMEM, (T, D), BF)}
    own = dict(stream=((T, D), BF), second=row, piece=((2, 3, 24, D), BF), slots=((2, 3, 2, 4, 4, 4, 24, 256), BF), later_we=WEIGHTS["we"],
        later_ws=WEIGHTS["ws"])
    return call(first_body, ins, outs, {**WEIGHTS, **SAVED, **ONCE, **own, **SUMS}, 64, 272, 0, ((0, 1),))


def second_kernel(tokens, length, cotangent, ahead, perm):
    names = (*WEIGHTS, *SAVED)
    ins = dict(stream=(ANY, tokens), length=(SMEM, length), perm=(VMEM, perm), cotangent=(VMEM, cotangent),
        gains=(VMEM, ahead.gains_all), top_stream=(ANY, ahead.top_stream), **{k: (ANY, getattr(ahead, k)) for k in names},
        **{"top_" + k: (ANY, getattr(ahead, "top_" + k)) for k in names})
    outs = dict(dstream=(ANY, (T, D), F32), norm=(VMEM, (8, 128), F32), grads=(ANY, (2, 3, 24, D), F32),
        gains_sum=(VMEM, (8, D), F32))
    own = dict(stream=((T, D), BF), top_stream=((T, D), F32), ga=OWN, r1=((2, 3, 3, 2, 2, 4, 24, 256), BF),
        r2=((2, 3, 2, 4, 4, 3, 24, 256), BF), m1=((2, 3, 3, 4, 3, 24, 256), BF), u2=((2, 3, 3, 3, 24, 256), BF), grads=((2, 3, 24, D), F32),
        nwide=((4, 4, 8, 128), F32), ndeep=((4, 2, 8, 128), F32))
    weights = {"top_" + k: WEIGHTS[k] for k in ("we", "ws")}
    return call(second_body, ins, outs, {**WEIGHTS, **weights, **SAVED, **BACK, **own, **SUMS, **SIBLING}, 64, 240, 1, ((0, 1),),
        credit=True)


def update(state, ahead, back):
    ins = dict(dstream=(VMEM, back.dstream), low_output=(VMEM, ahead.layer_output), norm=(VMEM, back.norm),
        grads=(VMEM, back.grads), gains_sum=(VMEM, back.gains_sum), **{k: (VMEM, v) for k, v in state.items()})
    outs = dict(input_gradient=(VMEM, (T, D), F32), layer_output=(VMEM, (T, D), BF), gradient_norm=(VMEM, (1, 1), F32))
    for kind in ("master", "momentum", "variance"):
        for name, v in {**ROWS, "gains": ((2, 4, 6), F32)}.items():
            outs[name + "_" + kind] = (VMEM, *v)
    return call(update_body, ins, outs, {}, 1)


def local(
    tokens,
    lengths,
    cotangent,
    joint_weight,
    output_weight,
    expand_weight,
    shrink_weight,
    layer_gains,
    joint_moment,
    output_moment,
    expand_moment,
    shrink_moment,
    gains_moment,
    joint_square,
    output_square,
    expand_square,
    shrink_square,
    gains_square,
):
    front = lambda a: a.transpose(2, 0, 1)
    swap = lambda a: a.transpose(0, 2, 1)
    shards = dict(joint=front(joint_weight), output=front(output_weight), expand=swap(expand_weight), shrink=shrink_weight)
    perm = slot_order()
    ahead = first_kernel(shards, layer_gains, tokens, lengths, perm)
    back = second_kernel(tokens, lengths, cotangent, ahead, perm)
    state = dict(
        shards,
        joint_moment=front(joint_moment),
        output_moment=front(output_moment),
        expand_moment=swap(expand_moment),
        shrink_moment=shrink_moment,
        joint_square=front(joint_square),
        output_square=front(output_square),
        expand_square=swap(expand_square),
        shrink_square=shrink_square,
        layer_gains=layer_gains,
        gains_moment=gains_moment,
        gains_square=gains_square,
    )
    new = update(state, ahead, back)
    results = [new.layer_output, new.input_gradient, new.gradient_norm.reshape(())]
    for kind in ("master", "momentum", "variance"):
        results += [
            getattr(new, "joint_" + kind).transpose(1, 2, 0),
            getattr(new, "output_" + kind).transpose(1, 2, 0),
            swap(getattr(new, "expand_" + kind)),
            getattr(new, "shrink_" + kind),
            getattr(new, "gains_" + kind),
        ]
    return tuple(results)


AXES = ("dp", "fsdp")


def solution(mesh):
    in_specs = (
        P(AXES, None),
        P(AXES),
        P(AXES, None),
        P(None, None, AXES),
        P(None, None, AXES),
        P(None, None, AXES),
        P(None, AXES, None),
        P(None, None, AXES),
        P(None, None, AXES),
        P(None, None, AXES),
        P(None, None, AXES),
        P(None, AXES, None),
        P(None, None, AXES),
        P(None, None, AXES),
        P(None, None, AXES),
        P(None, None, AXES),
        P(None, AXES, None),
        P(None, None, AXES),
    )
    out_specs = (
        P(AXES, None),
        P(AXES, None),
        P(),
        P(None, None, AXES),
        P(None, None, AXES),
        P(None, None, AXES),
        P(None, AXES, None),
        P(None, None, AXES),
        P(None, None, AXES),
        P(None, None, AXES),
        P(None, None, AXES),
        P(None, AXES, None),
        P(None, None, AXES),
        P(None, None, AXES),
        P(None, None, AXES),
        P(None, None, AXES),
        P(None, AXES, None),
        P(None, None, AXES),
    )
    return jax.shard_map(local, mesh=mesh, in_specs=in_specs, out_specs=out_specs, check_vma=False)
```

```python
import jax
import jax.numpy as jnp
import numpy as np
from jax import lax
from jax.experimental import pallas as pl
from jax.experimental.pallas import tpu as pltpu
from jax.sharding import PartitionSpec as P

MESH = pl.DeviceIdType.MESH
BF = jnp.bfloat16
F32 = jnp.float32
ANY, VMEM, SMEM = pl.ANY, pltpu.VMEM, pltpu.SMEM

def place():
    dp = lax.axis_index("dp"); fs = lax.axis_index("fsdp")
    return (dp // 4, lax.rem(dp // 2, 2) * 2 + fs // 4, lax.rem(fs, 4), lax.rem(dp, 2))

def device_at(x, y, z, c):
    return ((x * 2 + y // 2) * 2 + c, lax.rem(y, 2) * 4 + z)

def moved(co, axis, k):
    n = 2 if axis == 3 else 4
    co = list(co)
    co[axis] = lax.rem(co[axis] + (k % n), n)
    return tuple(co)

PLANES = ((1, 2), (0, 2), (0, 1))
RINGS = ((1, 2), (2, 0), (0, 1))
CORNERS = [(a, b) for a in range(4) for b in range(4) if (a, b) != (0, 0)]


def greet(co, planes):
    steps = {(0, 0, k, 1) for k in range(4)}
    for k in (1, 2, 3):
        steps |= {(k, 0, 0, 0), (0, k, 0, 0), (0, 0, k, 0)}
    for axes in planes:
        for corner in CORNERS:
            step = [0, 0, 0, 0]
            step[axes[0]], step[axes[1]] = corner
            steps.add(tuple(step))
    bar = pltpu.get_barrier_semaphore()
    for step in sorted(steps):
        pl.semaphore_signal(bar, inc=1, device_id=device_at(*stepped(co, step)), device_id_type=MESH)
    return lambda: pl.semaphore_wait(bar, len(steps))


def stepped(co, step):
    for axis, k in enumerate(step):
        if k:
            co = moved(co, axis, k)
    return co


class Link:
    def __init__(self, co, ss, rs):
        self.co, self.ss, self.rs = co, ss, rs
        self.n = 0
        self.out = []
    def send(self, src, dst, axis, k):
        i = self.n
        self.n += 1
        cp = pltpu.make_async_remote_copy(src_ref=src, dst_ref=dst, send_sem=self.ss.at[i], recv_sem=self.rs.at[i],
            device_id=device_at(*moved(self.co, axis, k)), device_id_type=MESH)
        cp.start()
        self.out.append(cp)
        return cp
    def step(self, src, dst, step):
        i = self.n
        self.n += 1
        cp = pltpu.make_async_remote_copy(src_ref=src, dst_ref=dst, send_sem=self.ss.at[i], recv_sem=self.rs.at[i],
            device_id=device_at(*stepped(self.co, step)), device_id_type=MESH)
        cp.start()
        self.out.append(cp)
        return cp

    def plane(self, axes, src_of, dst_of):
        going = []
        for a, b in CORNERS:
            step = [0, 0, 0, 0]
            step[axes[0]], step[axes[1]] = a, b
            going.append(self.step(src_of(a, b), dst_of(a, b), step))
        return going

    def sent(self, copies):
        for cp in copies:
            cp.wait_send()
        self.out = [o for o in self.out if all(o is not cp for cp in copies)]

    def drain(self):
        for cp in self.out:
            cp.wait_send()
        self.out = []

class Local:
    def __init__(self, sems):
        self.sems, self.n = sems, 0
    def copy(self, src, dst):
        cp = pltpu.make_async_copy(src, dst, self.sems.at[self.n])
        self.n += 1
        cp.start()
        return cp

class WideSum:
    def __init__(self, link, wide, deep):
        self.link, self.wide, self.deep = link, wide, deep

    def first(self, value):
        x, y, z, c = self.link.co
        mine = self.wide.at[x, y]
        mine[...] = value
        self.going = self.link.plane((0, 1), lambda a, b: mine, lambda a, b: mine)

    def second(self):
        x, y, z, c = self.link.co
        for cp in self.going:
            cp.wait_recv()
        value = None
        for i in range(4):
            for j in range(4):
                v = self.wide[i, j]
                value = v if value is None else value + v
        mine = self.deep.at[z, c]
        mine[...] = value
        self.going = [self.link.step(mine, mine, (0, 0, a, b)) for a in range(4) for b in range(2) if a or b]

    def total(self):
        for cp in self.going:
            cp.wait_recv()
        value = None
        for i in range(4):
            for j in range(2):
                v = self.deep[i, j]
                value = v if value is None else value + v
        return value


def acc(dst, srcs, lead):
    lead = lead[:-1]
    total = 1
    for d in lead:
        total *= d

    def body(t, carry):
        idx = []
        for d in reversed(lead):
            idx.append(lax.rem(t, d))
            t = t // d
        idx = tuple(reversed(idx))
        v = srcs[0][idx].astype(F32)
        for src in srcs[1:]:
            v = v + src[idx].astype(F32)
        dst[idx] = v.astype(dst.dtype)
        return carry

    lax.fori_loop(0, total, body, 0)


D = 768
LAYERS = 2
STEP = 5
beta_first = 0.9
beta_second = 0.999
adam_epsilon = 1e-08
clip_limit = 1.0
HEADS = 12
HEAD_DIM = 64
T = 256
norm_epsilon = 1e-05
SQ = 0.7978845608028654
CUBE = 0.044715
highest = lax.Precision.HIGHEST


def dot_of(a, b, dims, **kw):
    return lax.dot_general(a, b, (dims, ((), ())), preferred_element_type=F32, **kw)


def dot_nt(a, b):
    return dot_of(a, b, ((1,), (1,)))


def dot_nn(a, b):
    return dot_of(a, b, ((1,), (0,)))


def dot_tn(a, b):
    return dot_of(a, b, ((0,), (0,)))


def loop(n, fn):
    def body(t, carry):
        fn(t)
        return carry
    lax.fori_loop(0, n, body, 0)


def tile(t, size):
    return pl.ds(pl.multiple_of(t * size, size), size)


def stats(v):
    centred = v - jnp.mean(v, axis=-1, keepdims=True)
    scale = lax.rsqrt(jnp.mean(centred * centred, axis=-1, keepdims=True) + norm_epsilon)
    return centred * scale, scale


def norm_rows(src, dst, gain, shift):
    def step(t):
        r = tile(t, 64)
        unit, _ = stats(src[r, :].astype(F32))
        dst[r, :] = (unit * gain + shift).astype(BF)
    loop(T // 64, step)


def norm_back(src, grad, base, dst, gain, low_dst):
    def step(t, carry):
        to_gain, to_shift = carry
        r = tile(t, 64)
        unit, scale = stats(src[r, :].astype(F32))
        g = grad[r, :]
        to_gain = to_gain + jnp.sum((g * unit).reshape(8, 8, D), axis=0)
        to_shift = to_shift + jnp.sum(g.reshape(8, 8, D), axis=0)
        g = g * gain
        out = base[r, :] + scale * (
            g - jnp.mean(g, axis=-1, keepdims=True) - unit * jnp.mean(g * unit, axis=-1, keepdims=True)
        )
        dst[r, :] = out
        if low_dst is not None:
            low_dst[r, :] = out.astype(BF)
        return (to_gain, to_shift)
    zero = jnp.zeros((8, D), F32)
    to_gain, to_shift = lax.fori_loop(0, T // 64, step, (zero, zero))
    return jnp.sum(to_gain, axis=0, keepdims=True), jnp.sum(to_shift, axis=0, keepdims=True)


def grids():
    return lax.broadcasted_iota(jnp.int32, (T, T), 0), lax.broadcasted_iota(jnp.int32, (T, T), 1)


def halves(pair):
    lane = lax.broadcasted_iota(jnp.int32, (T, 128), 1)
    zero = jnp.zeros_like(pair)
    return jnp.where(lane < HEAD_DIM, pair, zero), jnp.where(lane < HEAD_DIM, zero, pair)


SCALE = HEAD_DIM ** -0.5
FT = 384


def slots_at(ref, t, f):
    return ref[t, f // 4, lax.rem(f, 4)].reshape(FT, 256)


def put_slots(ref, f, value):
    for t in range(3):
        ref[t, f // 4, lax.rem(f, 4)] = value[:, 256 * t:256 * t + 256].reshape(4, 4, 24, 256).astype(BF)


def first_scores(proj):
    q, _ = halves(proj[:, 0:128])
    return dot_nt(q * jnp.asarray(SCALE, BF), proj[:, D:D + 128])


def attention(proj, probs, attended, bias, length):
    row, col = grids()
    scores = first_scores(proj)
    chosen = jnp.maximum(scores, 0.0) + jnp.log(1.0 + jnp.exp(-jnp.abs(scores)))
    chosen = jnp.where((col > 0) & (col < row) & (row < length), chosen, 0.0)
    forget = dot_of((col < row).astype(F32), chosen, ((1,), (0,)), precision=highest)
    bias[...] = jnp.where((col <= row) & (col < length), forget, 1e30)

    def pair(p):
        at = tile(p, 128)
        q = halves(proj[:, at] * jnp.asarray(SCALE, BF))
        k = proj[:, tile(6 + p, 128)]
        v = halves(proj[:, tile(12 + p, 128)])
        total = None
        for h in range(2):
            logits = dot_nt(q[h], k) - bias[...]
            e = jnp.exp(logits - jnp.max(logits, axis=-1, keepdims=True))
            e = (e * (1.0 / jnp.sum(e, axis=-1, keepdims=True))).astype(BF)
            probs[2 * p + h] = e
            part = dot_nn(e, v[h])
            total = part if h == 0 else total + part
        attended[:, at] = total.astype(BF)
    loop(6, pair)


def forward_first(s, gains, length):
    norm_rows(s.stream, s.normed, gains[0:1], gains[1:2])
    wj = s.wj.reshape(3 * D, D)
    def project(t):
        s.proj[:, tile(t, 256)] = dot_nt(s.normed[...], wj[tile(t, 256), :]).astype(BF)
    def three(n):
        for k in range(3):
            project(3 * n + k)
    loop(3, three)
    yield
    attention(s.proj, s.probs, s.attended, s.bias, length)
    yield
    wo = s.wo.reshape(D, D)
    def output(t):
        at = tile(t, 256)
        s.mid[:, at] = s.stream[:, at].astype(F32) + dot_nt(s.attended[...], wo[at, :])
    loop(3, output)


def third(t):
    return slice(256 * t, 256 * t + 256)


def forward_second(s, gains):
    norm_rows(s.mid, s.normed2, gains[2:3], gains[3:4])
    s.need("we")
    def raise_(f):
        at = tile(f, FT)
        r = dot_nt(s.normed2[:, third(0)], slots_at(s.we, 0, f))
        for t in (1, 2):
            r = r + dot_nt(s.normed2[:, third(t)], slots_at(s.we, t, f))
        s.raised[:, at] = r
        s.hidden[:, at] = (0.5 * r * (1.0 + jnp.tanh(r * (SQ + SQ * CUBE * r * r)))).astype(BF)
    loop(4 * D // FT, raise_)
    yield
    s.need("ws")
    for t in range(3):
        s.next[:, third(t)] = s.mid[:, third(t)] + dot_nn(s.hidden[...], s.ws[t].reshape(4 * D, 256))


def backward_second(s, gains):
    for name in ("dstream", "ws", "raised", "we", "normed2"):
        s.need(name)

    s.low[...] = s.dstream[...].astype(BF)
    s.acc[...] = jnp.zeros((T, D), F32)
    def step(t):
        t = lax.rem(t + s.flip, 8)
        at = tile(t, FT)
        dh = dot_nt(s.low[:, third(0)], slots_at(s.ws, 0, t))
        for n in (1, 2):
            dh = dh + dot_nt(s.low[:, third(n)], slots_at(s.ws, n, t))
        r = s.raised[:, at]
        th = jnp.tanh(r * (SQ + SQ * CUBE * r * r))
        hid = (0.5 * r * (1.0 + th)).astype(BF)
        slope = 0.5 * (1.0 + th) + 0.5 * r * (1.0 - th * th) * (SQ + 3.0 * SQ * CUBE * r * r)
        dr = (dh * slope).astype(BF)
        put_slots(s.ws, t, dot_tn(hid, s.low[...]))
        for n in range(3):
            s.acc[:, third(n)] += dot_nn(dr, slots_at(s.we, n, t))
        put_slots(s.we, t, dot_tn(dr, s.normed2[...]))
    pieces = 4 * D // FT // 2
    for piece in range(pieces):
        if piece == pieces // 2:
            for name in ("ws_later", "raised_later", "we_later"):
                s.need(name)
        loop(2, lambda t: step(t + 2 * piece))
        if piece < pieces - 1:
            yield
    s.need("mid")
    s.sums += norm_back(s.mid, s.acc, s.dstream, s.dstream, gains[2:3], s.low)
    yield


def attention_back(proj, probs, dout, dproj, bias, keep, length):
    bias[...] = jnp.zeros((T, T), F32)

    def scores_of(p, h, do, v):
        prob = probs[2 * p + h]
        full = prob.astype(F32)
        dsoft = dot_nt(do, v)
        dl = full * (dsoft - jnp.sum(full * dsoft, axis=-1, keepdims=True))
        bias[...] += dl
        return prob, dl

    def pair(p):
        at, at_k, at_v = tile(p, 128), tile(6 + p, 128), tile(12 + p, 128)
        q = halves(proj[:, at] * jnp.asarray(SCALE, BF))
        k = halves(proj[:, at_k] * jnp.asarray(SCALE, BF))
        v = proj[:, at_v]
        do = halves(dout[:, at])
        dq = dk = dv = None
        for h in range(2):
            prob, dl = scores_of(p, h, do[h], v)
            ds = dl.astype(BF)
            parts = (dot_nn(ds, k[h]), dot_tn(ds, q[h]), dot_tn(prob, do[h]))
            dq, dk, dv = parts if h == 0 else (dq + parts[0], dk + parts[1], dv + parts[2])
        dproj[:, at] = dq.astype(BF)
        dproj[:, at_k] = dk.astype(BF)
        dproj[:, at_v] = dv.astype(BF)
    loop(2, lambda t: pair(t + 1))
    yield
    loop(3, lambda t: pair(t + 3))
    yield

    q = halves(proj[:, 0:128] * jnp.asarray(SCALE, BF))
    k = halves(proj[:, D:D + 128] * jnp.asarray(SCALE, BF))
    v = proj[:, 2 * D:2 * D + 128]
    do = halves(dout[:, 0:128])
    prob1, dl1 = scores_of(0, 1, do[1], v)
    prob0, dl0 = scores_of(0, 0, do[0], v)
    keep[...] = dl0
    row, col = grids()
    dchosen = -dot_of((col > row).astype(F32), bias[...], ((1,), (0,)), precision=highest)
    scores = first_scores(proj)
    slope = 1.0 / (1.0 + jnp.exp(-scores))
    extra = jnp.where((col > 0) & (col < row) & (row < length), dchosen * slope, 0.0)
    ds0 = (keep[...] + extra).astype(BF)
    ds1 = dl1.astype(BF)
    dproj[:, 0:128] = (dot_nn(ds0, k[0]) + dot_nn(ds1, k[1])).astype(BF)
    dproj[:, D:D + 128] = (dot_tn(ds0, q[0]) + dot_tn(ds1, q[1])).astype(BF)
    dproj[:, 2 * D:2 * D + 128] = (dot_tn(prob0, do[0]) + dot_tn(prob1, do[1])).astype(BF)


def backward_first(s, gains, length):
    for name in ("wo", "attended", "proj", "probs"):
        s.need(name)
    wo, wj = s.wo.reshape(D, D), s.wj.reshape(3 * D, D)
    def back(t):
        at = tile(t, 256)
        s.dout[:, at] = dot_nn(s.low[...], wo[:, at]).astype(BF)
    loop(3, back)
    def grad(t):
        at = tile(t, 256)
        wo[at, :] = dot_tn(s.low[:, at], s.attended[...]).astype(BF)
    loop(3, grad)
    yield
    yield from attention_back(s.proj, s.probs, s.dout, s.dproj, s.bias, s.keep, length)
    yield
    s.need("wj")
    s.need("normed")
    s.acc[...] = jnp.zeros((T, D), F32)
    def joint(t):
        at = tile(t, 384)
        d = s.dproj[:, at]
        s.acc[...] += dot_nn(d, wj[at, :])
        wj[at, :] = dot_tn(d, s.normed[...]).astype(BF)
    for piece in range(2):
        loop(3, lambda t: joint(t + 3 * piece))
        yield
    s.need("stream")
    s.sums += norm_back(s.stream, s.acc, s.dstream, s.dstream, gains[0:1], None)


class Names:
    def __init__(self, **kw):
        self.__dict__.update(kw)
        self.coming = {}
        self.sums = ()

    def need(self, name):
        for cp in self.coming.pop(name, ()):
            cp.wait()


WEIGHTS = dict(wj=((4, 2, 2, 144, D), BF), wo=((4, 2, 2, 48, D), BF), we=((3, 2, 4, 4, 4, 24, 256), BF), ws=((3, 2, 4, 4, 4, 24, 256), BF))
SAVED = dict(mid=((T, D), F32), normed=((T, D), BF), normed2=((T, D), BF), proj=((T, 3 * D), BF), probs=((HEADS, T, T), BF),
    attended=((T, D), BF), raised=((T, 4 * D), F32))
ONCE = dict(bias=((T, T), F32), hidden=((T, 4 * D), BF), next=((T, D), F32))
BACK = dict(bias=((T, T), F32), keep=((T, T), F32), dstream=((T, D), F32), low=((T, D), BF), acc=((T, D), F32), dout=((T, D), BF),
    dproj=((T, 3 * D), BF))


def fetch(ins, s, loc, names):
    for n in names:
        s.coming[n] = [loc.copy(getattr(ins, n), getattr(s, n))]


def run(pieces):
    for _ in pieces:
        pass


def gains_of(sums):
    gain2, shift2, gain1, shift1 = sums
    return jnp.concatenate([gain1, shift1, gain2, shift2], axis=0)


def live_rows(length):
    return lax.broadcasted_iota(jnp.int32, (T, D), 0) < length


def own_columns(which):
    lane = lax.broadcasted_iota(jnp.int32, (1, D), 1)
    return [(lane == which * 6 + j).astype(F32) for j in range(6)]


OWN = ((3, 4, 4, 4, 24, 256), BF)
SIBLING = dict(sib_wj=((4, 2, 144, D), BF), sib_wo=((4, 2, 48, D), BF), sib_we=OWN, sib_ws=OWN)


def side_of(ref, name, core, at=slice(None)):
    return ref.at[at, :, core] if name in ("wj", "wo") else ref.at[:, core]


class Pair:
    def __init__(self, s, link, c):
        self.s, self.link, self.c = s, link, c
        self.going, self.copies = {}, {}

    def send(self, name, at=slice(None)):
        src, dst = side_of(getattr(self.s, name), name, 1 - self.c, at), getattr(self.s, "sib_" + name)
        cp = self.link.send(src, dst.at[at] if name == "wj" else dst, 3, 1)
        self.going.setdefault(name, []).append(cp)
        self.copies.setdefault(name, []).append(cp)

    def arrived(self, name):
        for cp in self.going.pop(name):
            cp.wait_recv()

    def join(self, name):
        self.arrived(name)
        mine, other = side_of(getattr(self.s, name), name, self.c), getattr(self.s, "sib_" + name)
        acc(mine, [mine, other], (3, 4, 4))

    def join_rows(self, perm):
        self.arrived("wj")
        self.arrived("wo")
        s = self.s
        def step(n):
            x, h = n // 2, lax.rem(n, 2)
            j = s.wj[x, h, self.c].astype(F32) + s.sib_wj[x, h].astype(F32)
            o = s.wo[x, h, self.c].astype(F32) + s.sib_wo[x, h].astype(F32)
            rows = jnp.concatenate([j.astype(BF), o.astype(BF)], axis=0)
            slots = dot_tn(perm, rows)
            for t in range(3):
                s.ga[t, x, pl.ds(2 * h, 2)] = slots[:, 256 * t:256 * t + 256].reshape(2, 4, 24, 256).astype(BF)
        loop(8, step)


def compact(slots, wj, wo, perm):
    def step(n):
        x, h, c = n // 4, lax.rem(n // 2, 2), lax.rem(n, 2)
        for t in range(3):
            rows = dot_nn(perm, slots[t, c, x, pl.ds(2 * h, 2)].reshape(192, 256)).astype(BF)
            wj[x, h, c, :, third(t)] = rows[:144]
            wo[x, h, c, :, third(t)] = rows[144:]

    def four(n):
        for k in range(4):
            step(4 * n + k)
    loop(4, four)


class Gather:
    def __init__(self, link, loc, piece, dst):
        self.link, self.loc, self.piece, self.dst = link, loc, piece, dst
        self.co = link.co

    def slots(self, t, sel):
        return self.dst.at[(t, self.co[3], *sel)]

    def small(self):
        self.own, self.one = [], []
        for t in range(3):
            src, dst = self.piece.at[:, third(t)], self.slots(t, self.co[:3])
            self.own.append(self.loc.copy(src, dst))
            self.one.append([self.link.send(src, dst, RINGS[t][0], k) for k in (1, 3, 2)])

    def slab(self):
        self.two = []
        for t in range(3):
            self.own[t].wait()
            for cp in self.one[t]:
                cp.wait_recv()
            u, v = RINGS[t]
            sel = list(self.co[:3])
            sel[u] = slice(None)
            ref = self.slots(t, sel)
            self.two.append([self.link.send(ref, ref, v, k) for k in (1, 3)])

    def slab_on(self):
        self.three = []
        for t in range(3):
            u, v = RINGS[t]
            for side, back, on in ((0, 3, 1), (1, 1, 3)):
                self.two[t][side].wait_recv()
                sel = list(moved(self.co, v, back)[:3])
                sel[u] = pl.ds(2 * side, 2)
                ref = self.slots(t, sel)
                self.three.append(self.link.send(ref, ref, v, on))

    def block(self):
        for cp in self.three:
            cp.wait_recv()
        self.four = []
        for t in range(3):
            sel = [slice(None)] * 3
            sel[t] = self.co[t]
            ref = self.slots(t, sel)
            self.four.append([self.link.send(ref, ref, t, k) for k in (1, 3)])

    def block_on(self):
        self.five = []
        for t in range(3):
            u, v = RINGS[t]
            for side, back, on in ((0, 3, 1), (1, 1, 3)):
                self.four[t][side].wait_recv()
                sel = [slice(None)] * 3
                sel[t] = moved(self.co, t, back)[t]
                sel[u] = pl.ds(2 * side, 2)
                ref = self.slots(t, sel)
                self.five.append(self.link.send(ref, ref, t, on))

    def across(self):
        for cp in self.five:
            cp.wait_recv()
        c = self.co[3]
        self.six = [self.link.send(self.dst.at[t, c], self.dst.at[t, c], 3, 1) for t in range(3)]

    def ready(self):
        for cp in self.six:
            cp.wait_recv()


def first_body(ins, out, s, loc, link, co):
    x, y, z, c = co
    length = ins.length[0]
    fetch(ins, s, loc, ("stream",))
    targets = [[s.slots.at[0], s.we, s.ws], [s.slots.at[1], s.later_we, s.later_ws]]
    items = []
    for l in range(2):
        rows = jnp.concatenate([ins.joint[:, l, :], ins.output[:, l, :]], axis=0)
        for w, value in enumerate((rows, ins.expand[l], ins.shrink[l])):
            s.piece[l, w] = value.astype(BF)
            items.append(Gather(link, loc, s.piece.at[l, w], targets[l][w]))
    s.met()
    for item in items:
        item.small()
    which = ((x * 2 + y // 2) * 2 + c) * 8 + lax.rem(y, 2) * 4 + z
    masks = own_columns(which)
    placed = []
    for l in range(2):
        rows = ins.layer_gains[l].astype(BF).astype(F32)
        total = rows[:, 0:1] * masks[0]
        for j in range(1, 6):
            total = total + rows[:, j:j + 1] * masks[j]
        placed.append(total)
    gain_sum = WideSum(link, s.gwide, s.gdeep)
    gain_sum.first(jnp.concatenate(placed, axis=0))

    done = []
    perm = ins.perm

    def step(k):
        if k + 2 < 6:
            items[k + 2].block()
        if 0 < k < 7:
            items[k - 1].across()
        if k < 6:
            items[k].block_on()

    def save(*names, prefix=""):
        for n in names:
            done.append(loc.copy(getattr(s, n), getattr(out, prefix + n)))

    for item in items:
        item.slab()
    gain_sum.second()
    for item in items[:3]:
        item.slab_on()
    items[0].block()
    for item in items[3:]:
        item.slab_on()
    items[1].block()
    out.gains_all[...] = gain_sum.total()
    gains = out.gains_all[0:4]
    step(0)
    step(1)
    items[0].ready()
    compact(s.slots.at[0], s.wj, s.wo, perm[...])
    step(2)
    save("wj", "wo")
    s.need("stream")
    first = forward_first(s, gains, length)
    next(first)
    step(3)
    next(first)
    run(first)
    step(4)
    items[1].ready()
    second = forward_second(s, gains)
    next(second)
    items[2].ready()
    save("normed", "proj", "probs", "attended", "mid", "normed2", "raised")
    run(second)
    s.second[...] = s.next[...]
    for cp in done:
        cp.wait()
    done.clear()
    save("we", "ws")
    done.append(loc.copy(s.second, out.top_stream))
    top = Names(**{k: v for k, v in s.__dict__.items() if k not in ("coming", "sums", "stream", "met", "we", "ws")}, stream=s.second, we=s.later_we,
        ws=s.later_ws)
    gains = out.gains_all[4:8]
    step(5)
    items[3].ready()
    compact(s.slots.at[1], s.wj, s.wo, perm[...])
    save("wj", "wo", prefix="top_")
    first = forward_first(top, gains, length)
    next(first)
    step(6)
    items[4].ready()
    done.append(loc.copy(s.later_we, out.top_we))
    next(first)
    run(first)
    save("normed", "proj", "probs", "attended", "mid", prefix="top_")
    second = forward_second(top, gains)
    next(second)
    save("normed2", "raised", prefix="top_")
    link.drain()
    items[5].ready()
    done.append(loc.copy(s.later_ws, out.top_ws))
    run(second)
    out.layer_output[...] = s.next[...].astype(BF)
    for cp in done:
        cp.wait()
    link.drain()


class Reduce:
    def __init__(self, link, s, l, w, source):
        self.link, self.s, self.l, self.w, self.source, self.co = link, s, l, w, source, link.co

    def at(self, t, k):
        sel = [slice(None)] * 3
        sel[t] = moved(self.co, t, k)[t]
        return self.source.at[(t, *sel)]

    def half(self, ref, h):
        return ref.at[pl.ds(2 * h, 2)]

    def r1(self, t, side):
        return self.s.r1.at[self.l, self.w, t, side]

    def r2(self, t, side):
        return self.s.r2.at[self.l, t, side, :, :, self.w]

    def far(self):
        self.hop1 = [[self.link.send(self.half(self.at(t, 2), side), self.r1(t, side), t, k) for side, k in ((0, 1), (1, 3))]
            for t in range(3)]

    def near(self):
        self.hop2 = [[self.link.send(self.half(self.at(t, k), 1 - side), self.half(self.r2(t, side), 1 - side), t, k)
            for side, k in ((0, 1), (1, 3))] for t in range(3)]

    def onward(self):
        for t in range(3):
            for side, k in ((0, 1), (1, 3)):
                self.hop1[t][side].wait_recv()
                o = self.half(self.at(t, k), side)
                acc(o, [o, self.r1(t, side)], (2, 4))
                self.hop2[t].append(self.link.send(o, self.half(self.r2(t, side), side), t, k))

    def collect(self):
        for t in range(3):
            for cp in self.hop2[t]:
                cp.wait_recv()
            acc(self.r2(t, 0), [self.at(t, 0), self.r2(t, 0), self.r2(t, 1)], (4, 4))

    def sent(self):
        self.link.sent([cp for t in range(3) for cp in (*self.hop1[t], *self.hop2[t])])


class Settle:
    def __init__(self, link, s, l, first, count):
        self.link, self.s, self.l, self.first, self.count = link, s, l, first, count
        self.which = pl.ds(first, count)

    def row(self, t, q):
        block = self.s.r2.at[self.l, t, 0]
        return block.at[:, q, self.which] if RINGS[t][1] == PLANES[t][1] else block.at[q, :, self.which]

    def send(self):
        co, self.going = self.link.co, []
        for t in range(3):
            v = RINGS[t][1]
            self.going.append([self.link.send(self.row(t, moved(co, v, k)[v]), self.s.m1.at[self.l, t, k - 1, :, self.which], v, k)
                for k in (2, 1, 3)])

    def cross(self):
        co, self.last = self.link.co, []
        for t in range(3):
            for cp in self.going[t]:
                cp.wait_recv()
            u, v = RINGS[t]
            got = [self.s.m1.at[self.l, t, k, :, self.which] for k in range(3)]
            acc(got[0], [self.row(t, co[v])] + got, (4, self.count))
            self.last.append([self.link.send(self.s.m1.at[self.l, t, 0, moved(co, u, k)[u], self.which],
                self.s.u2.at[self.l, t, k - 1, self.which], u, k) for k in (2, 1, 3)])

    def final(self, square):
        co = self.link.co
        for t in range(3):
            for cp in self.last[t]:
                cp.wait_recv()
            u = RINGS[t][0]
            for w in range(self.first, self.first + self.count):
                g = self.s.m1[self.l, t, 0, co[u], w].astype(F32)
                for k in range(3):
                    g = g + self.s.u2[self.l, t, k, w].astype(F32)
                self.s.grads[self.l, w, :, third(t)] = g
                g = g * g
                g = g[0:8] + g[8:16] + g[16:24]
                g = g[:, 0:128] + g[:, 128:256]
                square = g if square is None else square + g
        return square


def second_body(ins, out, s, loc, link, co):
    x, y, z, c = co
    length = ins.length[0]
    shared = {k: v for k, v in s.__dict__.items() if k not in ("coming", "sums", "met")}
    base = Names(**shared)
    top = Names(**{**shared, **{k: getattr(s, "top_" + k) for k in ("we", "ws", "stream")}})
    layers = (base, top)
    base.flip = top.flip = 4 * (1 - c)
    pairs = [Pair(n, link, c) for n in layers]
    sums = [[Reduce(link, s, l, w, (n.ga, n.we.at[:, c], n.ws.at[:, c])[w]) for w in range(3)] for l, n in enumerate(layers)]
    low, up = sums
    top_end, ff_end, row_end = Settle(link, s, 1, 0, 3), Settle(link, s, 0, 1, 2), Settle(link, s, 0, 0, 1)
    perm = ins.perm

    def bring(n, prefix, *names):
        for name in names:
            n.coming[name] = [loc.copy(getattr(ins, prefix + name), getattr(n, name))]

    def bring_half(n, prefix, h, *names):
        for name in names:
            half = 1 - c if h == 0 else c
            at = (slice(None), tile(half, 2 * D) if name == "raised" else half)
            n.coming[name + "_later" * h] = [loc.copy(getattr(ins, prefix + name).at[at], getattr(n, name).at[at])]

    bring_half(top, "top_", 0, "ws", "raised", "we")
    bring(top, "top_", "normed2")
    bring_half(top, "top_", 1, "ws", "raised", "we")
    bring(top, "top_", "mid", "wo", "attended", "proj", "probs", "wj", "normed", "stream")
    bring(base, "", "we", "ws", "stream")
    s.dstream[...] = jnp.where(live_rows(length), ins.cotangent[...].astype(F32), 0.0)
    g = ins.gains[4:8]
    for k, _ in enumerate(backward_second(top, g)):
        if k == 1:
            s.met()
            pairs[1].send("ws")
            pairs[1].send("we")
    bring(base, "", "raised", "normed2", "mid")
    for k, _ in enumerate(backward_first(top, g, length)):
        if k == 0:
            pairs[1].send("wo")
        if k == 1:
            pairs[1].join("ws")
            up[2].far()
            up[2].near()
        if k == 3:
            bring(base, "", "attended", "proj", "probs")
            pairs[1].join("we")
            up[1].far()
            up[1].near()
        if k == 4:
            pairs[1].send("wj", pl.ds(0, 2))
        if k == 5:
            pairs[1].send("wj", pl.ds(2, 2))
    bring(base, "", "normed")
    square = None
    base.coming["dstream"] = []
    g = ins.gains[0:4]
    for k, _ in enumerate(backward_second(base, g)):
        if k == 0:
            up[2].onward()
        if k == 1:
            pairs[1].join_rows(perm[...])
            up[0].far()
            up[0].near()
            link.sent(pairs[1].copies["wj"] + pairs[1].copies["wo"])
            bring(base, "", "wj", "wo")
            pl.semaphore_signal(s.credit, inc=1, device_id=device_at(*moved(co, 3, 1)), device_id_type=MESH)
            up[1].onward()
        if k == 2:
            pl.semaphore_wait(s.credit, 1)
            pairs[0].send("ws")
            pairs[0].send("we")
    up[2].collect()
    for k, _ in enumerate(backward_first(base, g, length)):
        if k == 0:
            pairs[0].send("wo")
            up[0].onward()
        if k == 1:
            up[1].collect()
            pairs[0].join("ws")
            low[2].far()
            low[2].near()
        if k == 3:
            up[0].collect()
            top_end.send()
            pairs[0].join("we")
            low[1].far()
            low[1].near()
        if k == 4:
            pairs[0].send("wj", pl.ds(0, 2))
        if k == 5:
            pairs[0].send("wj", pl.ds(2, 2))
            low[2].onward()
    gain_sum = WideSum(link, s.gwide, s.gdeep)
    gain_sum.first(jnp.concatenate([gains_of(base.sums), gains_of(top.sums)], axis=0))
    copies = [loc.copy(s.dstream, out.dstream)]
    up[0].sent()
    pairs[0].join_rows(perm[...])
    low[0].far()
    low[0].near()
    low[1].onward()
    top_end.cross()
    low[2].collect()
    gain_sum.second()
    low[0].onward()
    low[1].collect()
    ff_end.send()
    square = top_end.final(square)
    low[0].collect()
    row_end.send()
    ff_end.cross()
    gains_sum = gain_sum.total()
    out.gains_sum[...] = gains_sum
    row_end.cross()
    square = ff_end.final(square)
    square = row_end.final(square)
    copies.append(loc.copy(s.grads, out.grads))
    norm_sum = WideSum(link, s.nwide, s.ndeep)
    norm_sum.first(square)
    link.drain()
    norm_sum.second()
    whole = norm_sum.total()
    norm = jnp.sqrt(jnp.sum(jnp.sum(whole, axis=0, keepdims=True), axis=1, keepdims=True)
        + jnp.sum(jnp.sum(gains_sum * gains_sum, axis=0, keepdims=True), axis=1, keepdims=True))
    out.norm[...] = jnp.broadcast_to(norm, (8, 128))
    for cp in copies:
        cp.wait()
    link.drain()


RATES = dict(matrix=(0.05, 0.1), gains=(0.25, 0.0))


def adam(master, gradient, moment, square, kind, clip):
    rate, decay = RATES[kind]
    clipped = gradient * clip
    momentum = beta_first * moment + (1.0 - beta_first) * clipped
    variance = beta_second * square + (1.0 - beta_second) * clipped * clipped
    corrected_first = momentum / (1.0 - beta_first**STEP)
    corrected_second = variance / (1.0 - beta_second**STEP)
    updated = master - rate * (corrected_first / (jnp.sqrt(corrected_second) + adam_epsilon) + decay * master)
    return updated, momentum, variance


def update_body(ins, out, s, loc, link, co):
    x, y, z, c = co
    out.input_gradient[...] = ins.dstream[...]
    out.layer_output[...] = ins.low_output[...]
    which = ((x * 2 + y // 2) * 2 + c) * 8 + lax.rem(y, 2) * 4 + z
    columns = [jnp.sum(ins.gains_sum[...] * m, axis=-1, keepdims=True) for m in own_columns(which)]
    lane = lax.broadcasted_iota(jnp.int32, (8, 6), 1)
    own_gains = jnp.zeros((8, 6), F32)
    for j in range(6):
        own_gains = own_gains + jnp.where(lane == j, columns[j], 0.0)
    norm = ins.norm[0:1, 0:1]
    out.gradient_norm[...] = norm
    clip = jnp.minimum(1.0, clip_limit / (norm + 1e-06))
    for l in range(2):
        for name, w, rows in (("joint", 0, slice(0, 18)), ("output", 0, slice(18, 24)), ("expand", 1, slice(0, 24)), ("shrink", 2, slice(0, 24))):
            at = (slice(None), l, slice(None)) if w == 0 else (l, slice(None), slice(None))
            new = adam(getattr(ins, name)[at], ins.grads[l, w, rows, :], getattr(ins, name + "_moment")[at], getattr(ins, name + "_square")[at], "matrix", clip)
            for kind, v in zip(("master", "momentum", "variance"), new):
                getattr(out, name + "_" + kind)[at] = v
        new = adam(ins.layer_gains[l], own_gains[4 * l:4 * l + 4], ins.gains_moment[l], ins.gains_square[l], "gains", clip)
        for kind, v in zip(("master", "momentum", "variance"), new):
            getattr(out, "gains_" + kind)[l] = v


def call(body, inputs, outs, scratch, copies, remote=0, collective=None, planes=(), credit=False, limit=63 << 20):
    in_names, out_names, names = list(inputs), list(outs), list(scratch)
    shapes = [pltpu.VMEM(*scratch[n]) for n in names] + [pltpu.SemaphoreType.DMA((copies,))]
    params = dict(vmem_limit_bytes=limit)
    if remote:
        shapes += [pltpu.SemaphoreType.DMA((remote,)), pltpu.SemaphoreType.DMA((remote,))]
        params.update(collective_id=collective, has_side_effects=True)
    if credit:
        shapes.append(pltpu.SemaphoreType.REGULAR)

    def kernel(*refs):
        ins = Names(**dict(zip(in_names, refs)))
        out = Names(**dict(zip(out_names, refs[len(in_names):])))
        rest = refs[len(in_names) + len(out_names):]
        bufs = Names(**dict(zip(names, rest)))
        loc = Local(rest[len(names)])
        co = place()
        if not remote:
            body(ins, out, bufs, loc, None, co)
            return
        if credit:
            bufs.credit = rest[-1]
        bufs.met = greet(co, planes)
        link = Link(co, *rest[len(names) + 1:len(names) + 3])
        body(ins, out, bufs, loc, link, co)

    result = pl.pallas_call(
        kernel,
        out_shape=tuple(jax.ShapeDtypeStruct(*outs[n][1:]) for n in out_names),
        in_specs=[pl.BlockSpec(memory_space=inputs[n][0]) for n in in_names],
        out_specs=tuple(pl.BlockSpec(memory_space=outs[n][0]) for n in out_names),
        scratch_shapes=shapes,
        compiler_params=pltpu.CompilerParams(**params),
    )(*[inputs[n][1] for n in in_names])
    return Names(**dict(zip(out_names, result)))


def hbm(table, prefix=""):
    return {prefix + k: (ANY, *v) for k, v in table.items()}


ROWS = dict(joint=((18, 2, D), F32), output=((6, 2, D), F32), expand=((2, 24, D), F32), shrink=((2, 24, D), F32))
SUMS = dict(gwide=((4, 4, 8, D), F32), gdeep=((4, 2, 8, D), F32))


def slot_order():
    order = np.zeros((192, 192), np.float32)
    for f in range(8):
        for r in range(18):
            order[18 * f + r, 24 * f + r] = 1
        for r in range(6):
            order[144 + 6 * f + r, 24 * f + 18 + r] = 1
    return jnp.asarray(order, BF)


def first_kernel(shards, layer_gains, tokens, length, perm):
    ins = dict(layer_gains=(VMEM, layer_gains), stream=(ANY, tokens), length=(SMEM, length), perm=(VMEM, perm),
        **{k: (VMEM, v) for k, v in shards.items()})
    row = ((T, D), F32)
    outs = {**hbm(WEIGHTS), **hbm(SAVED), **hbm(WEIGHTS, "top_"), **hbm(SAVED, "top_"), "top_stream": (ANY, *row),
        "gains_all": (VMEM, (8, D), F32), "layer_output": (VMEM, (T, D), BF)}
    own = dict(stream=((T, D), BF), second=row, piece=((2, 3, 24, D), BF), slots=((2, 3, 2, 4, 4, 4, 24, 256), BF), later_we=WEIGHTS["we"],
        later_ws=WEIGHTS["ws"])
    return call(first_body, ins, outs, {**WEIGHTS, **SAVED, **ONCE, **own, **SUMS}, 64, 272, 0, ((0, 1),))


def second_kernel(tokens, length, cotangent, ahead, perm):
    names = (*WEIGHTS, *SAVED)
    ins = dict(stream=(ANY, tokens), length=(SMEM, length), perm=(VMEM, perm), cotangent=(VMEM, cotangent),
        gains=(VMEM, ahead.gains_all), top_stream=(ANY, ahead.top_stream), **{k: (ANY, getattr(ahead, k)) for k in names},
        **{"top_" + k: (ANY, getattr(ahead, "top_" + k)) for k in names})
    outs = dict(dstream=(ANY, (T, D), F32), norm=(VMEM, (8, 128), F32), grads=(ANY, (2, 3, 24, D), F32),
        gains_sum=(VMEM, (8, D), F32))
    own = dict(stream=((T, D), BF), top_stream=((T, D), F32), ga=OWN, r1=((2, 3, 3, 2, 2, 4, 24, 256), BF),
        r2=((2, 3, 2, 4, 4, 3, 24, 256), BF), m1=((2, 3, 3, 4, 3, 24, 256), BF), u2=((2, 3, 3, 3, 24, 256), BF), grads=((2, 3, 24, D), F32),
        nwide=((4, 4, 8, 128), F32), ndeep=((4, 2, 8, 128), F32))
    weights = {"top_" + k: WEIGHTS[k] for k in ("we", "ws")}
    return call(second_body, ins, outs, {**WEIGHTS, **weights, **SAVED, **BACK, **own, **SUMS, **SIBLING}, 64, 240, 1, ((0, 1),),
        credit=True)


def update(state, ahead, back):
    ins = dict(dstream=(VMEM, back.dstream), low_output=(VMEM, ahead.layer_output), norm=(VMEM, back.norm),
        grads=(VMEM, back.grads), gains_sum=(VMEM, back.gains_sum), **{k: (VMEM, v) for k, v in state.items()})
    outs = dict(input_gradient=(VMEM, (T, D), F32), layer_output=(VMEM, (T, D), BF), gradient_norm=(VMEM, (1, 1), F32))
    for kind in ("master", "momentum", "variance"):
        for name, v in {**ROWS, "gains": ((2, 4, 6), F32)}.items():
            outs[name + "_" + kind] = (VMEM, *v)
    return call(update_body, ins, outs, {}, 1)


def local(
    tokens,
    lengths,
    cotangent,
    joint_weight,
    output_weight,
    expand_weight,
    shrink_weight,
    layer_gains,
    joint_moment,
    output_moment,
    expand_moment,
    shrink_moment,
    gains_moment,
    joint_square,
    output_square,
    expand_square,
    shrink_square,
    gains_square,
):
    front = lambda a: a.transpose(2, 0, 1)
    swap = lambda a: a.transpose(0, 2, 1)
    shards = dict(joint=front(joint_weight), output=front(output_weight), expand=swap(expand_weight), shrink=shrink_weight)
    perm = slot_order()
    ahead = first_kernel(shards, layer_gains, tokens, lengths, perm)
    back = second_kernel(tokens, lengths, cotangent, ahead, perm)
    state = dict(
        shards,
        joint_moment=front(joint_moment),
        output_moment=front(output_moment),
        expand_moment=swap(expand_moment),
        shrink_moment=shrink_moment,
        joint_square=front(joint_square),
        output_square=front(output_square),
        expand_square=swap(expand_square),
        shrink_square=shrink_square,
        layer_gains=layer_gains,
        gains_moment=gains_moment,
        gains_square=gains_square,
    )
    new = update(state, ahead, back)
    results = [new.layer_output, new.input_gradient, new.gradient_norm.reshape(())]
    for kind in ("master", "momentum", "variance"):
        results += [
            getattr(new, "joint_" + kind).transpose(1, 2, 0),
            getattr(new, "output_" + kind).transpose(1, 2, 0),
            swap(getattr(new, "expand_" + kind)),
            getattr(new, "shrink_" + kind),
            getattr(new, "gains_" + kind),
        ]
    return tuple(results)


AXES = ("dp", "fsdp")


def solution(mesh):
    in_specs = (
        P(AXES, None),
        P(AXES),
        P(AXES, None),
        P(None, None, AXES),
        P(None, None, AXES),
        P(None, None, AXES),
        P(None, AXES, None),
        P(None, None, AXES),
        P(None, None, AXES),
        P(None, None, AXES),
        P(None, None, AXES),
        P(None, AXES, None),
        P(None, None, AXES),
        P(None, None, AXES),
        P(None, None, AXES),
        P(None, None, AXES),
        P(None, AXES, None),
        P(None, None, AXES),
    )
    out_specs = (
        P(AXES, None),
        P(AXES, None),
        P(),
        P(None, None, AXES),
        P(None, None, AXES),
        P(None, None, AXES),
        P(None, AXES, None),
        P(None, None, AXES),
        P(None, None, AXES),
        P(None, None, AXES),
        P(None, None, AXES),
        P(None, AXES, None),
        P(None, None, AXES),
        P(None, None, AXES),
        P(None, None, AXES),
        P(None, None, AXES),
        P(None, AXES, None),
        P(None, None, AXES),
    )
    return jax.shard_map(local, mesh=mesh, in_specs=in_specs, out_specs=out_specs, check_vma=False)
```
